32 devices in a mesh: ctx: 8 (over y, x, core), head: 4 (over z).
Axes of the slice: x: 2, y: 2, z: 4, core: 2. Of those that a mesh axis runs over, the one named last changes fastest.
Arguments:
- query_states: bfloat16 [2048, 2048], P('ctx', 'head'), may hold values from -28 to 28
- key_states: bfloat16 [2048, 2048], P('ctx', 'head'), may hold values from -4 to 4
- value_states: bfloat16 [2048, 2048], P('ctx', 'head'), may hold values from -6 to 6
- out_weight: bfloat16 [2048, 2048], P('head'), may hold values from -0.125 to 0.125
- grad_mixed: bfloat16 [2048, 2048], P(('ctx', 'head')), may hold values from -6 to 6
- key_blocks: int32 [16, 4], P('ctx'), may hold values from 0 to 15, as said below
- host_ids: int32 [16], replicated, may hold values from 0 to 3
- host_bias: float32 [16], P('head'), may hold values from 0.5 to 3
Outputs:
- mixed_out: bfloat16 [2048, 2048], P(('ctx', 'head'))
- grad_query: bfloat16 [2048, 2048], P('ctx', 'head')
- grad_key: bfloat16 [2048, 2048], P('ctx', 'head')
- grad_value: bfloat16 [2048, 2048], P('ctx', 'head')
The draws below stay inside these ranges and needn't reach their ends.
Inputs may be any that keep to these rules, and one draw needn't show every extreme that they name: `key_blocks`: row i lists 4 different blocks, the first being block i itself; every listed block lies among the 2 blocks of a ctx index at most 2 places from that of block i on the closed loop of ctx indices.
All inputs are finite; a program needn't handle non-finite values.
Results may differ from the reference program's by a relative error of at most 0.022.
Values may be sent and summed in bfloat16 or wider, within the bound.
No kernel may reach another device: no remote copies, remote signals or barrier semaphores. Data moves between devices by JAX's collectives and lax.ppermute only.
A program may use at most 64 MiB of HBM per device.

```python
import jax
import jax.numpy as jnp
from jax import lax

D = 2048
HEADS = 16
HDIM = 128
BLK = 128
HOPS = 2
NEIGH = 4
BLK_DEV = 2
NBLK = 16
TOKENS = 2048


def draw_query_states(key, part):
    own_key = jax.random.fold_in(key, 4)
    drawn = jnp.clip(jax.random.normal(own_key, (TOKENS, HEADS * HDIM), jnp.float32), -4.0, 4.0)
    return drawn.astype(jnp.bfloat16)


def draw_key_states(key, part):
    own_key = jax.random.fold_in(key, 3)
    drawn = jnp.clip(jax.random.normal(own_key, (TOKENS, HEADS * HDIM), jnp.float32), -4.0, 4.0)
    return drawn.astype(jnp.bfloat16)


def draw_key_blocks(key, part):
    own_key = jax.random.fold_in(key, 21)
    slot_count = (2 * HOPS + 1) * BLK_DEV
    devices = NBLK // BLK_DEV
    positions = jnp.arange(NBLK, dtype=jnp.int32)
    own_slot = HOPS * BLK_DEV + positions % BLK_DEV
    raw = jax.random.randint(own_key, (NBLK, slot_count), 0, 1 << 20)
    slot_ids = jnp.arange(slot_count, dtype=jnp.int32)
    ranking = raw * slot_count + slot_ids[None, :]
    ranking = jnp.where(slot_ids[None, :] == own_slot[:, None], -1, ranking)
    ordered = jnp.argsort(ranking, axis=1, stable=True)[:, :NEIGH].astype(jnp.int32)
    device_of = jnp.mod((positions // BLK_DEV)[:, None] + ordered // BLK_DEV - HOPS, devices)
    return (device_of * BLK_DEV + ordered % BLK_DEV).astype(jnp.int32)


def place_ends(result, rng, least, top_value):
    shape = result.shape
    spot = [jax.random.randint(jax.random.fold_in(rng, axis), (), 0, shape[axis]) for axis in range(len(shape))]
    result = result.at[tuple(spot)].set(least)
    longest = shape.index(max(shape))
    spot[longest] = (spot[longest] + 1) % shape[longest]
    return result.at[tuple(spot)].set(top_value)


def block_scale(stream_key, extent, cuts, smallest, high):
    gain, own = 1.0, jax.random.fold_in(stream_key, 6)
    for dim, blocks in cuts:
        heights = jnp.exp(jax.random.uniform(jax.random.fold_in(own, dim), (blocks,), jnp.float32, smallest / len(cuts), high / len(cuts)))
        gain = gain * jnp.repeat(heights, extent[dim] // blocks).reshape([-1 if axis == dim else 1 for axis in range(len(extent))])
    return gain


def normal_values(key, shape, spread, reach, split=(), held_as=jnp.bfloat16):
    loudness = block_scale(key, shape, split, -0.22, 0.18) if split else 1.0
    values = jax.random.normal(key, shape, jnp.float32) * spread * loudness
    return jnp.minimum(jnp.maximum(values, -reach), reach).astype(held_as)


def setup_inputs(seed: int = 0) -> dict:
    arg_keys = jax.random.split(jax.random.key(seed), 9)
    return {
        "query_states": draw_query_states(jax.random.fold_in(arg_keys[8], 71), 0),
        "key_states": draw_key_states(jax.random.fold_in(arg_keys[8], 71), 0),
        "value_states": normal_values(arg_keys[2], (TOKENS, HEADS * HDIM), 1.0, 6.0, ((0, 8), (1, 4))),
        "out_weight": normal_values(arg_keys[3], (HEADS * HDIM, D), (HEADS * HDIM) ** -0.5, 0.125, ((0, 4),)),
        "grad_mixed": normal_values(arg_keys[4], (TOKENS, D), 1.0, 6.0, ((0, 32),)),
        "key_blocks": draw_key_blocks(jax.random.fold_in(arg_keys[8], 71), 0),
        "host_ids": place_ends(jax.random.randint(arg_keys[6], (NBLK,), 0, 4), jax.random.fold_in(arg_keys[6], 1), 0, 3).astype(jnp.int32),
        "host_bias": jnp.clip(0.5 + 2.5 * jax.random.uniform(arg_keys[7], (HEADS,), jnp.float32) ** block_scale(arg_keys[7], (HEADS,), ((0, 4),), -0.2, 0.2), 0.5, 3.0),
    }


def pick_head(states, head_index):
    return lax.dynamic_slice_in_dim(states, head_index * HDIM, HDIM, 1).reshape(NBLK, BLK, HDIM)


def head_probs(head_query_rows, selected_keys, bias_value, same_host):
    logit_scale = HDIM ** -0.5
    attention_logits = jnp.einsum("msy,mwfy->mswf", head_query_rows.astype(jnp.float32), selected_keys.astype(jnp.float32)) * logit_scale
    attention_logits = attention_logits + bias_value * same_host[:, None, :, None]
    highest = jnp.max(attention_logits, axis=(2, 3), keepdims=True)
    weights = jnp.exp(attention_logits - highest)
    return weights / jnp.sum(weights, axis=(2, 3), keepdims=True)


def reference(query_states, key_states, value_states, out_weight, grad_mixed, key_blocks, host_ids, host_bias):
    logit_scale = HDIM ** -0.5
    same_host = (host_ids[:, None] == host_ids[key_blocks]).astype(jnp.float32)

    def forward_head(head_index):
        head_query_rows = pick_head(query_states, head_index)
        selected_keys = pick_head(key_states, head_index)[key_blocks]
        selected_values = pick_head(value_states, head_index)[key_blocks]
        probs = head_probs(head_query_rows, selected_keys, host_bias[head_index], same_host)
        batch_probabilities = probs.astype(jnp.bfloat16)
        attention_output = jnp.einsum("hrat,hats->hrs", batch_probabilities.astype(jnp.float32), selected_values.astype(jnp.float32))
        return attention_output.astype(jnp.bfloat16)

    head_list = jnp.arange(HEADS, dtype=jnp.int32)
    attended = lax.map(forward_head, head_list)
    attended = attended.transpose(1, 2, 0, 3).reshape(TOKENS, HEADS * HDIM)
    mixed_out = jnp.dot(attended, out_weight, preferred_element_type=jnp.float32).astype(jnp.bfloat16)
    upstream = jnp.dot(grad_mixed, out_weight.T, preferred_element_type=jnp.float32).astype(jnp.bfloat16)

    def backward_head(head_index):
        head_query_rows = pick_head(query_states, head_index)
        selected_keys = pick_head(key_states, head_index)[key_blocks]
        selected_values = pick_head(value_states, head_index)[key_blocks]
        incoming_head_gradient = pick_head(upstream, head_index).astype(jnp.float32)
        probs = head_probs(head_query_rows, selected_keys, host_bias[head_index], same_host)
        batch_probabilities = probs.astype(jnp.bfloat16).astype(jnp.float32)
        selected_value_gradient = jnp.einsum("vlhu,vlr->vhur", batch_probabilities, incoming_head_gradient)
        probability_gradient = jnp.einsum("msy,mwfy->mswf", incoming_head_gradient, selected_values.astype(jnp.float32))
        row_term = jnp.sum(probs * probability_gradient, axis=(2, 3), keepdims=True)
        logit_gradient = (probs * (probability_gradient - row_term) * logit_scale).astype(jnp.bfloat16).astype(jnp.float32)
        head_query_gradient = jnp.einsum("hrat,hats->hrs", logit_gradient, selected_keys.astype(jnp.float32)).astype(jnp.bfloat16)
        selected_key_gradient = jnp.einsum("vlhu,vlr->vhur", logit_gradient, head_query_rows.astype(jnp.float32))
        grad_key_head = jnp.zeros((NBLK, BLK, HDIM), jnp.float32).at[key_blocks].add(selected_key_gradient)
        grad_value_head = jnp.zeros((NBLK, BLK, HDIM), jnp.float32).at[key_blocks].add(selected_value_gradient)
        return head_query_gradient, grad_key_head.astype(jnp.bfloat16), grad_value_head.astype(jnp.bfloat16)

    grads = lax.map(backward_head, head_list)

    def arrange(stacked):
        return stacked.transpose(1, 2, 0, 3).reshape(TOKENS, HEADS * HDIM)

    return mixed_out, arrange(grads[0]), arrange(grads[1]), arrange(grads[2])
```

```python
import functools

import jax
import jax.numpy as jnp
from jax import lax
from jax.experimental import pallas as pl
from jax.experimental.pallas import tpu as pltpu
from jax.sharding import PartitionSpec as P

HDIM = 128
BLK = 128
HOPS = 2
SCALE = HDIM ** (-0.5)
CUBE = (0, 1, 2, 3, 6, 7)
NT = (((1,), (1,)), ((), ()))
VMEM = pl.BlockSpec(memory_space=pltpu.VMEM)
SMEM = pl.BlockSpec(memory_space=pltpu.SMEM)
ANY = pl.BlockSpec(memory_space=pl.ANY)
PARAMS = pltpu.CompilerParams(vmem_limit_bytes=48 * 1024 * 1024)


def ndot(a, b):
    return lax.dot_general(a, b, (((1,), (0,)), ((), ())), preferred_element_type=jnp.float32)


def tdot(a, b):
    return lax.dot_general(a, b, NT, preferred_element_type=jnp.float32)


def stat_rows(pairs):
    return -(-2 * pairs // 16) * 16


def window_tags(size):
    return CUBE if size == 8 else tuple([0] + [o for o in range(-HOPS, HOPS + 1) if o != 0])


def tag_owner(position, tag, size):
    return position ^ tag if size == 8 else lax.rem(position + tag + size, size)


def find_shard(position, owner, size):
    shard = 0
    for index, tag in enumerate(window_tags(size)):
        shard = shard + jnp.where(tag_owner(position, tag, size) == owner, index, 0)
    return shard


def exchange(x, size):
    def move(v, pairs):
        return lax.ppermute(v, "ctx", pairs)

    if size == 8:
        flip = lambda mask: [(i, i ^ mask) for i in range(size)]
        near = move(x, flip(2))
        mate = move(x, flip(1))
        far = move(near, flip(4))
        return [x, mate, near, move(near, flip(1)), far, move(far, flip(1))]
    return [x] + [
        move(x, [(i, (i - tag) % size) for i in range(size)]) for tag in window_tags(size)[1:]
    ]


def load_windows(groups, sem):
    waits = []
    count = 0
    for refs, window in groups:
        rows = refs[0].shape[0]
        copies = []
        for index, ref in enumerate(refs):
            copy = pltpu.make_async_copy(ref, window.at[pl.ds(index * rows, rows)], sem.at[count])
            copy.start()
            copies.append(copy)
            count += 1
        waits.append(copies)
    return waits


def neighbour_rows(size, blocks_dev, rows, keys_ref, hosts_ref):
    position = lax.axis_index("ctx")
    table = []
    for b in range(blocks_dev):
        host = hosts_ref[position * blocks_dev + b]
        line = []
        for n in range(keys_ref.shape[1]):
            j = keys_ref[b, n]
            owner = lax.div(j, blocks_dev)
            shard = find_shard(position, owner, size)
            row = pl.multiple_of(shard * rows + lax.rem(j, blocks_dev) * BLK, BLK)
            line.append((row, jnp.where(hosts_ref[j] == host, 1.0, 0.0).astype(jnp.float32)))
        table.append(line)
    return table


def attend_kernel(size, groups, nsh, *refs):
    keys_ref, hosts_ref, bias_ref, q_ref, w_ref = refs[:5]
    k_refs = refs[5:5 + nsh]
    v_refs = refs[5 + nsh:5 + 2 * nsh]
    rest = refs[5 + 2 * nsh:]
    part_refs = rest[:groups]
    o32_ref, lse_ref = rest[groups:groups + 2]
    kwin, vwin, att, sem = rest[groups + 2:]
    rows, columns = q_ref.shape
    blocks_dev = rows // BLK
    heads_dev = columns // HDIM
    waits = load_windows([(k_refs, kwin), (v_refs, vwin)], sem)
    table = neighbour_rows(size, blocks_dev, rows, keys_ref, hosts_ref)
    for copies in waits:
        for copy in copies:
            copy.wait()
    lane = lax.broadcasted_iota(jnp.int32, (BLK, BLK), 1)
    lse_all = jnp.zeros((BLK, BLK), jnp.float32)
    for b in range(blocks_dev):
        for h in range(heads_dev):
            cols = slice(h * HDIM, (h + 1) * HDIM)
            q = q_ref[b * BLK:(b + 1) * BLK, cols]
            scores = [
                tdot(q, kwin[pl.ds(row, BLK), cols]) * SCALE + bias_ref[h] * same
                for row, same in table[b]
            ]
            top = jnp.max(functools.reduce(jnp.maximum, scores), axis=1, keepdims=True)
            weights = [jnp.exp(s - top) for s in scores]
            total = jnp.sum(functools.reduce(jnp.add, weights), axis=1, keepdims=True)
            inv = 1.0 / total
            out = jnp.zeros((BLK, HDIM), jnp.float32)
            for (row, _), w in zip(table[b], weights):
                out = out + ndot((w * inv).astype(jnp.bfloat16), vwin[pl.ds(row, BLK), cols])
            o32_ref[b * BLK:(b + 1) * BLK, cols] = out
            att[b * BLK:(b + 1) * BLK, cols] = out.astype(jnp.bfloat16)
            lse_all = jnp.where(lane == b * heads_dev + h, top + jnp.log(total), lse_all)
    lse_ref[...] = lse_all
    me = lax.axis_index("head")
    part = rows // groups
    for step in range(groups):
        owner = lax.rem(me + step, groups)
        chunk = att[pl.ds(pl.multiple_of(owner * part, part), part), :]
        part_refs[step][...] = ndot(chunk, w_ref[...]).astype(jnp.bfloat16)


def upstream_kernel(groups, *refs):
    w_ref, o32_ref, lse_ref = refs[:3]
    piece_refs = refs[3:3 + groups]
    up_ref, stats_ref = refs[3 + groups:]
    rows, columns = o32_ref.shape
    blocks_dev = rows // BLK
    heads_dev = columns // HDIM
    me = lax.axis_index("head")
    part = rows // groups
    for step in range(groups):
        owner = lax.rem(me - step + groups, groups)
        up_ref[pl.ds(pl.multiple_of(owner * part, part), part), :] = tdot(
            piece_refs[step][...], w_ref[...]
        ).astype(jnp.bfloat16)
    pairs = blocks_dev * heads_dev
    lane = lax.broadcasted_iota(jnp.int32, (BLK, BLK), 1)
    stats = lse_ref[...]
    for b in range(blocks_dev):
        for h in range(heads_dev):
            cols = slice(h * HDIM, (h + 1) * HDIM)
            up = up_ref[b * BLK:(b + 1) * BLK, cols].astype(jnp.float32)
            term = jnp.sum(up * o32_ref[b * BLK:(b + 1) * BLK, cols], axis=1, keepdims=True)
            stats = jnp.where(lane == pairs + b * heads_dev + h, term, stats)
    stats_ref[...] = stats
    high = stat_rows(pairs)
    turned = jnp.transpose(stats)[:high, :]
    up_ref[rows:, :] = jnp.zeros((up_ref.shape[0] - rows, columns), jnp.bfloat16)
    for index in range(3):
        piece = turned.astype(jnp.bfloat16)
        turned = turned - piece.astype(jnp.float32)
        row = rows + high * (index * BLK // columns)
        col = index * BLK % columns
        up_ref[row:row + high, col:col + BLK] = piece


def query_kernel(size, nsh, *refs):
    keys_ref, hosts_ref, bias_ref, q_ref, up_ref, stats_ref = refs[:6]
    k_refs = refs[6:6 + nsh]
    v_refs = refs[6 + nsh:6 + 2 * nsh]
    dq_ref, kwin, vwin, sem = refs[6 + 2 * nsh:]
    rows, columns = q_ref.shape
    blocks_dev = rows // BLK
    heads_dev = columns // HDIM
    pairs = blocks_dev * heads_dev
    waits = load_windows([(k_refs, kwin), (v_refs, vwin)], sem)
    table = neighbour_rows(size, blocks_dev, rows, keys_ref, hosts_ref)
    for copies in waits:
        for copy in copies:
            copy.wait()
    for b in range(blocks_dev):
        for h in range(heads_dev):
            cols = slice(h * HDIM, (h + 1) * HDIM)
            pair = b * heads_dev + h
            q = q_ref[b * BLK:(b + 1) * BLK, cols]
            up = up_ref[b * BLK:(b + 1) * BLK, cols]
            lse = stats_ref[:, pair:pair + 1]
            term = stats_ref[:, pairs + pair:pairs + pair + 1]
            total = jnp.zeros((BLK, HDIM), jnp.float32)
            for row, same in table[b]:
                k = kwin[pl.ds(row, BLK), cols]
                p = jnp.exp(tdot(q, k) * SCALE + bias_ref[h] * same - lse)
                dp = tdot(up, vwin[pl.ds(row, BLK), cols])
                ds = (p * (dp - term) * SCALE).astype(jnp.bfloat16)
                total = total + ndot(ds, k)
            dq_ref[b * BLK:(b + 1) * BLK, cols] = total.astype(jnp.bfloat16)


def key_kernel(size, nsh, *refs):
    keys_ref, hosts_ref, bias_ref, k_ref, v_ref = refs[:5]
    q_refs = refs[5:5 + nsh]
    up_refs = refs[5 + nsh:5 + 2 * nsh]
    dk_ref, dv_ref, qwin, upwin, stats, dk_acc, dv_acc, sem = refs[5 + 2 * nsh:]
    rows, columns = k_ref.shape
    long_rows = up_refs[0].shape[0]
    blocks_dev = rows // BLK
    heads_dev = columns // HDIM
    pairs = blocks_dev * heads_dev
    position = lax.axis_index("ctx")
    waits = load_windows([(q_refs, qwin), (up_refs, upwin)], sem)
    dk_acc[...] = jnp.zeros_like(dk_acc)
    dv_acc[...] = jnp.zeros_like(dv_acc)
    for copies in waits:
        for copy in copies:
            copy.wait()
    high = stat_rows(pairs)
    for index in range(nsh):
        total = jnp.zeros((high, BLK), jnp.float32)
        for piece in reversed(range(3)):
            row = index * long_rows + rows + high * (piece * BLK // columns)
            col = piece * BLK % columns
            total = total + upwin[row:row + high, col:col + BLK].astype(jnp.float32)
        stats[index] = total

    tags = window_tags(size)

    def visit(step, carry):
        own = lax.rem(step, blocks_dev)
        mine = position * blocks_dev + own
        inner = lax.rem(lax.div(step, blocks_dev), blocks_dev)
        shard = lax.div(step, blocks_dev * blocks_dev)
        owner = 0
        for index, tag in enumerate(tags):
            owner = owner + jnp.where(shard == index, tag_owner(position, tag, size), 0)
        block = owner * blocks_dev + inner
        hit = keys_ref[block, 0] == mine
        for n in range(1, keys_ref.shape[1]):
            hit = hit | (keys_ref[block, n] == mine)

        @pl.when(hit)
        def _():
            same = jnp.where(hosts_ref[block] == hosts_ref[mine], 1.0, 0.0).astype(jnp.float32)
            krow = pl.ds(pl.multiple_of(own * BLK, BLK), BLK)
            qrow = pl.ds(pl.multiple_of(shard * rows + inner * BLK, BLK), BLK)
            urow = pl.ds(pl.multiple_of(shard * long_rows + inner * BLK, 16), BLK)
            for h in range(heads_dev):
                cols = slice(h * HDIM, (h + 1) * HDIM)
                k = k_ref[krow, cols]
                v = v_ref[krow, cols]
                q = qwin[qrow, cols]
                up = upwin[urow, cols]
                lse = stats[shard, pl.ds(inner * heads_dev + h, 1), :]
                term = stats[shard, pl.ds(pairs + inner * heads_dev + h, 1), :]
                p = jnp.exp(tdot(k, q) * SCALE + bias_ref[h] * same - lse)
                dp = tdot(v, up)
                ds = (p * (dp - term) * SCALE).astype(jnp.bfloat16)
                dk_acc[krow, cols] += ndot(ds, q)
                dv_acc[krow, cols] += ndot(p.astype(jnp.bfloat16), up)

        return carry

    lax.fori_loop(0, nsh * blocks_dev * blocks_dev, visit, 0)
    dk_ref[...] = dk_acc[...].astype(jnp.bfloat16)
    dv_ref[...] = dv_acc[...].astype(jnp.bfloat16)


def cost(flops, nbytes):
    return pl.CostEstimate(flops=flops, bytes_accessed=nbytes, transcendentals=0)


def per_device(
    query_states, key_states, value_states, out_weight, grad_mixed, key_blocks, host_ids, host_bias
):
    size = lax.axis_size("ctx")
    groups = lax.axis_size("head")
    rows, columns = query_states.shape
    width = out_weight.shape[1]
    part = rows // groups
    blocks_dev = rows // BLK
    pairs = blocks_dev * (columns // HDIM)
    nsh = len(window_tags(size))
    bf16, f32 = jnp.bfloat16, jnp.float32
    high = stat_rows(pairs)
    extra = high * (-(-3 * BLK // columns))
    long_rows = rows + extra

    def ring(x, step):
        return lax.ppermute(x, "head", [(i, (i + step) % groups) for i in range(groups)])

    all_keys = lax.all_gather(key_blocks, "ctx", axis=0, tiled=True)
    pieces = [grad_mixed] + [ring(grad_mixed, step) for step in range(1, groups)]
    k_win = exchange(key_states, size)
    v_win = exchange(value_states, size)
    q_win = exchange(query_states, size)

    parts_o32_lse = pl.pallas_call(
        functools.partial(attend_kernel, size, groups, nsh),
        out_shape=[jax.ShapeDtypeStruct((part, width), bf16)] * groups
        + [jax.ShapeDtypeStruct((rows, columns), f32), jax.ShapeDtypeStruct((BLK, BLK), f32)],
        in_specs=[SMEM] * 3 + [VMEM] * 2 + [ANY] * (2 * nsh),
        out_specs=[VMEM] * (groups + 2),
        scratch_shapes=[
            pltpu.VMEM((nsh * rows, columns), bf16),
            pltpu.VMEM((nsh * rows, columns), bf16),
            pltpu.VMEM((rows, columns), bf16),
            pltpu.SemaphoreType.DMA((2 * nsh,)),
        ],
        compiler_params=PARAMS,
        cost_estimate=cost(10**9, 8 * 10**6),
        name="attend",
    )(key_blocks, host_ids, host_bias, query_states, out_weight, *k_win, *v_win)
    parts = parts_o32_lse[:groups]
    o32, lse = parts_o32_lse[groups:]
    mixed = parts[0].astype(f32)
    arrived = [ring(parts[step], step) for step in range(1, groups)]

    up, stats = pl.pallas_call(
        functools.partial(upstream_kernel, groups),
        out_shape=[
            jax.ShapeDtypeStruct((long_rows, columns), bf16),
            jax.ShapeDtypeStruct((BLK, BLK), f32),
        ],
        in_specs=[VMEM] * (3 + groups),
        out_specs=[VMEM] * 2,
        compiler_params=PARAMS,
        cost_estimate=cost(6 * 10**8, 4 * 10**6),
        name="upstream",
    )(out_weight, o32, lse, *pieces)
    up_win = exchange(up, size)

    grad_query = pl.pallas_call(
        functools.partial(query_kernel, size, nsh),
        out_shape=jax.ShapeDtypeStruct((rows, columns), bf16),
        in_specs=[SMEM] * 3 + [VMEM] * 3 + [ANY] * (2 * nsh),
        out_specs=VMEM,
        scratch_shapes=[
            pltpu.VMEM((nsh * rows, columns), bf16),
            pltpu.VMEM((nsh * rows, columns), bf16),
            pltpu.SemaphoreType.DMA((2 * nsh,)),
        ],
        compiler_params=PARAMS,
        cost_estimate=cost(10**9, 8 * 10**6),
        name="query_grad",
    )(key_blocks, host_ids, host_bias, query_states, up, stats, *k_win, *v_win)

    grad_key, grad_value = pl.pallas_call(
        functools.partial(key_kernel, size, nsh),
        out_shape=[jax.ShapeDtypeStruct((rows, columns), bf16)] * 2,
        in_specs=[SMEM] * 3 + [VMEM] * 2 + [ANY] * (2 * nsh),
        out_specs=[VMEM] * 2,
        scratch_shapes=[
            pltpu.VMEM((nsh * rows, columns), bf16),
            pltpu.VMEM((nsh * long_rows, columns), bf16),
            pltpu.VMEM((nsh, high, BLK), f32),
            pltpu.VMEM((rows, columns), f32),
            pltpu.VMEM((rows, columns), f32),
            pltpu.SemaphoreType.DMA((2 * nsh,)),
        ],
        compiler_params=PARAMS,
        cost_estimate=cost(10**9, 8 * 10**6),
        name="key_grad",
    )(all_keys, host_ids, host_bias, key_states, value_states, *q_win, *up_win)

    for piece in arrived:
        mixed = mixed + piece.astype(f32)
    return (mixed.astype(bf16), grad_query, grad_key, grad_value)


def solution(mesh):
    in_specs = (
        P("ctx", "head"),
        P("ctx", "head"),
        P("ctx", "head"),
        P("head", None),
        P(("ctx", "head"), None),
        P("ctx", None),
        P(),
        P("head"),
    )
    out_specs = (P(("ctx", "head"), None), P("ctx", "head"), P("ctx", "head"), P("ctx", "head"))
    return jax.shard_map(
        per_device, mesh=mesh, in_specs=in_specs, out_specs=out_specs, check_vma=False
    )
```

```python
import functools

import jax
import jax.numpy as jnp
from jax import lax
from jax.experimental import pallas as pl
from jax.experimental.pallas import tpu as pltpu
from jax.sharding import PartitionSpec as P

HDIM = 128
BLK = 128
HOPS = 2
SCALE = HDIM ** (-0.5)
CUBE = (0, 1, 2, 3, 6, 7)
NT = (((1,), (1,)), ((), ()))
VMEM = pl.BlockSpec(memory_space=pltpu.VMEM)
SMEM = pl.BlockSpec(memory_space=pltpu.SMEM)
ANY = pl.BlockSpec(memory_space=pl.ANY)
HBM = pl.BlockSpec(memory_space=pltpu.HBM)
NEVER = 1e30
PARAMS = pltpu.CompilerParams(vmem_limit_bytes=60 * 1024 * 1024)


def ndot(a, b):
    return lax.dot_general(a, b, (((1,), (0,)), ((), ())), preferred_element_type=jnp.float32)


def tdot(a, b):
    return lax.dot_general(a, b, NT, preferred_element_type=jnp.float32)


def stat_rows(pairs):
    return -(-2 * pairs // 16) * 16


def window_tags(size):
    return CUBE if size == 8 else tuple([0] + [o for o in range(-HOPS, HOPS + 1) if o != 0])


def tag_owner(position, tag, size):
    return position ^ tag if size == 8 else lax.rem(position + tag + size, size)


def find_shard(position, owner, size):
    shard = 0
    for index, tag in enumerate(window_tags(size)):
        shard = shard + jnp.where(tag_owner(position, tag, size) == owner, index, 0)
    return shard


def exchange(x, size, forward=False):
    def move(v, pairs):
        return lax.ppermute(v, "ctx", pairs)

    if size == 8:
        flip = lambda mask: [(i, i ^ mask) for i in range(size)]
        near = move(x, flip(2))
        far = move(near, flip(4)) if forward else move(x, flip(6))
        mate = move(x, flip(1))
        return [x, mate, near, move(near, flip(1)), far, move(far, flip(1))]
    return [x] + [
        move(x, [(i, (i - tag) % size) for i in range(size)]) for tag in window_tags(size)[1:]
    ]


def start_all(pairs, sem, first=0):
    copies = []
    for index, (source, target) in enumerate(pairs):
        copy = pltpu.make_async_copy(source, target, sem.at[first + index])
        copy.start()
        copies.append(copy)
    return copies


def wait_all(copies):
    for copy in copies:
        copy.wait()


def gather_blocks(size, keys, refs, target, sem, first, blocks_dev, neigh):
    position = lax.axis_index("ctx")
    waits = []
    for b in range(blocks_dev):
        for n in range(neigh):
            j = keys[b, n]
            shard = find_shard(position, lax.div(j, blocks_dev), size)
            row = pl.multiple_of(lax.rem(j, blocks_dev) * BLK, BLK)
            place = b * neigh + n
            for index, ref in enumerate(refs):

                @pl.when(shard == index)
                def _(ref=ref, place=place, row=row):
                    pltpu.make_async_copy(
                        ref.at[pl.ds(row, BLK)], target.at[pl.ds(place * BLK, BLK)], sem.at[first + place]
                    ).start()

            waits.append(
                pltpu.make_async_copy(
                    refs[0].at[pl.ds(0, BLK)], target.at[pl.ds(place * BLK, BLK)], sem.at[first + place]
                )
            )
    return waits


def shift_rows(keys, hosts, bias, b, h, blocks_dev, neigh):
    position = lax.axis_index("ctx")
    slot = lax.broadcasted_iota(jnp.int32, (1, neigh * BLK), 1) // BLK
    shift = jnp.zeros((1, neigh * BLK), jnp.float32)
    host = hosts[position * blocks_dev + b]
    for n in range(neigh):
        value = jnp.where(hosts[keys[b, n]] == host, bias[h], 0.0)
        shift = jnp.where(slot == n, value, shift)
    return shift


def attend_kernel(size, nsh, *refs):
    keys_hbm, hosts_hbm, bias_hbm, q_hbm, w_hbm = refs[:5]
    k_refs = refs[5:5 + nsh]
    v_refs = refs[5 + nsh:5 + 2 * nsh]
    rest = refs[5 + 2 * nsh:]
    mixed_ref, o32_ref, lse_ref = rest[:3]
    keys, hosts, bias, q_ref, w_ref, kcat, vcat, score, att, sem = rest[3:]
    rows, columns = q_ref.shape
    blocks_dev, neigh = keys.shape
    heads_dev = columns // HDIM
    small = start_all([(keys_hbm, keys), (hosts_hbm, hosts), (bias_hbm, bias)], sem)
    large = start_all([(q_hbm, q_ref), (w_hbm, w_ref)], sem, 3)
    wait_all(small)
    places = blocks_dev * neigh
    k_waits = gather_blocks(size, keys, k_refs, kcat, sem, 5, blocks_dev, neigh)
    v_waits = gather_blocks(size, keys, v_refs, vcat, sem, 5 + places, blocks_dev, neigh)
    large[0].wait()
    wait_all(k_waits)
    span = neigh * BLK
    units = [(b, h) for b in range(blocks_dev) for h in range(heads_dev)]
    for b, h in units:
        cols = slice(h * HDIM, (h + 1) * HDIM)
        s = tdot(q_ref[b * BLK:(b + 1) * BLK, cols], kcat[b * span:(b + 1) * span, cols])
        score[b * heads_dev + h] = s * SCALE + shift_rows(keys, hosts, bias, b, h, blocks_dev, neigh)
    wait_all(v_waits)
    lane = lax.broadcasted_iota(jnp.int32, (BLK, BLK), 1)
    lse_all = jnp.zeros((BLK, BLK), jnp.float32)
    for b, h in units:
        cols = slice(h * HDIM, (h + 1) * HDIM)
        s = score[b * heads_dev + h]
        top = jnp.max(s, axis=1, keepdims=True)
        weights = jnp.exp(s - top)
        total = jnp.sum(weights, axis=1, keepdims=True)
        probs = (weights * (1.0 / total)).astype(jnp.bfloat16)
        out = ndot(probs, vcat[b * span:(b + 1) * span, cols])
        o32_ref[b * BLK:(b + 1) * BLK, cols] = out
        att[b * BLK:(b + 1) * BLK, cols] = out.astype(jnp.bfloat16)
        lse_all = jnp.where(lane == b * heads_dev + h, top + jnp.log(total), lse_all)
    lse_ref[...] = lse_all
    large[1].wait()
    mixed_ref[...] = ndot(att[...], w_ref[...]).astype(jnp.bfloat16)


def upstream_kernel(*refs):
    keys_hbm, w_hbm, grads_any, o32_ref, lse_ref, up_ref, stats_ref, keys, w_ref, grads, sem = refs
    rows, columns = o32_ref.shape
    blocks_dev, neigh = keys.shape
    heads_dev = columns // HDIM
    wait_all(start_all([(w_hbm, w_ref), (keys_hbm, keys), (grads_any, grads)], sem))
    up_ref[0:rows, :] = tdot(grads[...], w_ref[...]).astype(jnp.bfloat16)
    pairs = blocks_dev * heads_dev
    lane = lax.broadcasted_iota(jnp.int32, (BLK, BLK), 1)
    stats = lse_ref[...]
    for b in range(blocks_dev):
        for h in range(heads_dev):
            cols = slice(h * HDIM, (h + 1) * HDIM)
            up = up_ref[b * BLK:(b + 1) * BLK, cols].astype(jnp.float32)
            term = jnp.sum(up * o32_ref[b * BLK:(b + 1) * BLK, cols], axis=1, keepdims=True)
            stats = jnp.where(lane == pairs + b * heads_dev + h, term, stats)
    stats_ref[...] = stats
    high = stat_rows(pairs)
    turned = jnp.transpose(stats)[:high, :]
    up_ref[rows:, :] = jnp.zeros((up_ref.shape[0] - rows, columns), jnp.bfloat16)
    pieces = []
    for index in range(3):
        piece = turned.astype(jnp.bfloat16)
        turned = turned - piece.astype(jnp.float32)
        pieces.append(piece)
    spot = lax.broadcasted_iota(jnp.int32, (high, BLK), 1)
    line = lax.broadcasted_iota(jnp.int32, (high, BLK), 0)
    listed = jnp.zeros((high, BLK), jnp.int32)
    for b in range(blocks_dev):
        for n in range(neigh):
            listed = jnp.where(spot == b * neigh + n, keys[b, n], listed)
    listed = jnp.where(line == 0, listed >> 7, listed & 127)
    pieces.append(listed.astype(jnp.float32).astype(jnp.bfloat16))
    for index, piece in enumerate(pieces):
        row = rows + high * (index * BLK // columns)
        col = index * BLK % columns
        up_ref[row:row + high, col:col + BLK] = piece


def query_kernel(size, nsh, *refs):
    keys_hbm, hosts_hbm, bias_hbm, q_hbm, up_ref, stats_ref = refs[:6]
    k_refs = refs[6:6 + nsh]
    v_refs = refs[6 + nsh:6 + 2 * nsh]
    dq_ref, keys, hosts, bias, q_ref, kcat, vcat, sem = refs[6 + 2 * nsh:]
    rows, columns = q_ref.shape
    blocks_dev, neigh = keys.shape
    heads_dev = columns // HDIM
    pairs = blocks_dev * heads_dev
    small = start_all([(keys_hbm, keys), (hosts_hbm, hosts), (bias_hbm, bias)], sem)
    large = start_all([(q_hbm, q_ref)], sem, 3)
    wait_all(small)
    places = blocks_dev * neigh
    waits = gather_blocks(size, keys, k_refs, kcat, sem, 4, blocks_dev, neigh)
    waits += gather_blocks(size, keys, v_refs, vcat, sem, 4 + places, blocks_dev, neigh)
    wait_all(large)
    wait_all(waits)
    span = neigh * BLK
    for b in range(blocks_dev):
        for h in range(heads_dev):
            cols = slice(h * HDIM, (h + 1) * HDIM)
            pair = b * heads_dev + h
            q = q_ref[b * BLK:(b + 1) * BLK, cols]
            up = up_ref[b * BLK:(b + 1) * BLK, cols]
            k = kcat[b * span:(b + 1) * span, cols]
            lse = stats_ref[:, pair:pair + 1]
            term = stats_ref[:, pairs + pair:pairs + pair + 1]
            shift = shift_rows(keys, hosts, bias, b, h, blocks_dev, neigh)
            p = jnp.exp(tdot(q, k) * SCALE + shift - lse)
            dp = tdot(up, vcat[b * span:(b + 1) * span, cols])
            ds = (p * (dp - term) * SCALE).astype(jnp.bfloat16)
            dq_ref[b * BLK:(b + 1) * BLK, cols] = ndot(ds, k).astype(jnp.bfloat16)


def key_kernel(size, nsh, neigh, *refs):
    hosts_hbm, bias_hbm, k_hbm, v_hbm = refs[:4]
    q_refs = refs[4:4 + nsh]
    up_refs = refs[4 + nsh:4 + 2 * nsh]
    dk_ref, dv_ref = refs[4 + 2 * nsh:6 + 2 * nsh]
    (hosts, bias, k_ref, v_ref, qwin, upwin, stats, lists, keys, hits, dk_acc, dv_acc, sem) = refs[
        6 + 2 * nsh:
    ]
    rows, columns = k_ref.shape
    long_rows = up_refs[0].shape[0]
    blocks_dev = rows // BLK
    heads_dev = columns // HDIM
    pairs = blocks_dev * heads_dev
    high = stat_rows(pairs)
    position = lax.axis_index("ctx")
    tail = [
        (ref.at[pl.ds(rows, long_rows - rows)], upwin.at[pl.ds(i * long_rows + rows, long_rows - rows)])
        for i, ref in enumerate(up_refs)
    ]
    first = start_all(tail, sem)
    body = [(ref.at[pl.ds(0, rows)], upwin.at[pl.ds(i * long_rows, rows)]) for i, ref in enumerate(up_refs)]
    body += [(ref, qwin.at[pl.ds(i * rows, rows)]) for i, ref in enumerate(q_refs)]
    body += [(hosts_hbm, hosts), (bias_hbm, bias), (k_hbm, k_ref), (v_hbm, v_ref)]
    later = start_all(body, sem, nsh)
    dk_acc[...] = jnp.zeros_like(dk_acc)
    dv_acc[...] = jnp.zeros_like(dv_acc)
    wait_all(first)

    def part_of(index, piece):
        row = index * long_rows + rows + high * (piece * BLK // columns)
        col = piece * BLK % columns
        return upwin[row:row + high, col:col + BLK].astype(jnp.float32)

    for index in range(nsh):
        stats[index] = (part_of(index, 2) + part_of(index, 1)) + part_of(index, 0)
        listed = part_of(index, 3).astype(jnp.int32)
        lists[index:index + 1, :] = listed[0:1, :] * 128 + listed[1:2, :]
    stats[nsh] = jnp.full((high, BLK), NEVER, jnp.float32)
    copy = pltpu.make_async_copy(lists, keys, sem.at[3 * nsh + 4])
    copy.start()
    copy.wait()

    counts = []
    for own in range(blocks_dev):
        mine = position * blocks_dev + own
        count = 0
        for index in range(nsh):
            for inner in range(blocks_dev):
                hit = keys[index, inner * neigh] == mine
                for n in range(1, neigh):
                    hit = hit | (keys[index, inner * neigh + n] == mine)
                hits[own, count] = index * blocks_dev + inner
                count = count + jnp.where(hit, 1, 0)
        hits[own, count] = -1
        counts.append(count)
    wait_all(later)

    for own in range(blocks_dev):
        mine = position * blocks_dev + own
        krow = slice(own * BLK, (own + 1) * BLK)

        def visit(step, carry, own=own, mine=mine, krow=krow):
            qs, ups, sames, lses, terms = [], [], [], [], []
            for turn in range(2):
                entry = hits[own, 2 * step + turn]
                spare = entry < 0
                entry = jnp.where(spare, 0, entry)
                shard = lax.div(entry, blocks_dev)
                inner = lax.rem(entry, blocks_dev)
                owner = 0
                for index, tag in enumerate(window_tags(size)):
                    owner = owner + jnp.where(shard == index, tag_owner(position, tag, size), 0)
                sames.append(hosts[owner * blocks_dev + inner] == hosts[mine])
                qs.append(pl.ds(pl.multiple_of(shard * rows + inner * BLK, BLK), BLK))
                ups.append(pl.ds(pl.multiple_of(shard * long_rows + inner * BLK, 16), BLK))
                lses.append((jnp.where(spare, nsh, shard), inner))
                terms.append((shard, inner))
            for h in range(heads_dev):
                cols = slice(h * HDIM, (h + 1) * HDIM)
                k = k_ref[krow, cols]
                v = v_ref[krow, cols]
                q = jnp.concatenate([qwin[r, cols] for r in qs], axis=0)
                up = jnp.concatenate([upwin[r, cols] for r in ups], axis=0)
                less = jnp.concatenate(
                    [
                        stats[shard, pl.ds(inner * heads_dev + h, 1), :] - jnp.where(same, bias[h], 0.0)
                        for (shard, inner), same in zip(lses, sames)
                    ],
                    axis=1,
                )
                term = jnp.concatenate(
                    [stats[shard, pl.ds(pairs + inner * heads_dev + h, 1), :] for shard, inner in terms],
                    axis=1,
                )
                p = jnp.exp(tdot(k, q) * SCALE - less)
                ds = (p * (tdot(v, up) - term) * SCALE).astype(jnp.bfloat16)
                dk_acc[krow, cols] += ndot(ds, q)
                dv_acc[krow, cols] += ndot(p.astype(jnp.bfloat16), up)
            return carry

        lax.fori_loop(0, lax.div(counts[own] + 1, 2), visit, 0)
    dk_ref[...] = dk_acc[...].astype(jnp.bfloat16)
    dv_ref[...] = dv_acc[...].astype(jnp.bfloat16)


def cost(flops, nbytes):
    return pl.CostEstimate(flops=flops, bytes_accessed=nbytes, transcendentals=0)


def per_device(
    query_states, key_states, value_states, out_weight, grad_mixed, key_blocks, host_ids, host_bias
):
    size = lax.axis_size("ctx")
    rows, columns = query_states.shape
    width = out_weight.shape[1]
    blocks_dev, neigh = key_blocks.shape
    heads_dev = columns // HDIM
    pairs = blocks_dev * heads_dev
    places = blocks_dev * neigh
    nsh = len(window_tags(size))
    bf16, f32, i32 = jnp.bfloat16, jnp.float32, jnp.int32
    high = stat_rows(pairs)
    extra = high * (-(-4 * BLK // columns))
    long_rows = rows + extra

    all_grads = lax.all_gather(grad_mixed, "head", axis=0, tiled=True)
    v_win = exchange(value_states, size, forward=True)
    k_win = exchange(key_states, size)
    late_query, _ = lax.optimization_barrier((query_states, v_win[2]))
    q_win = exchange(late_query, size)
    scalars = [
        pltpu.SMEM(key_blocks.shape, i32),
        pltpu.SMEM(host_ids.shape, i32),
        pltpu.SMEM(host_bias.shape, f32),
    ]

    share, o32, lse = pl.pallas_call(
        functools.partial(attend_kernel, size, nsh),
        out_shape=[
            jax.ShapeDtypeStruct((rows, width), bf16),
            jax.ShapeDtypeStruct((rows, columns), f32),
            jax.ShapeDtypeStruct((BLK, BLK), f32),
        ],
        in_specs=[HBM] * 5 + ([HBM] + [ANY] * (nsh - 1)) * 2,
        out_specs=[VMEM] * 3,
        scratch_shapes=scalars
        + [
            pltpu.VMEM((rows, columns), bf16),
            pltpu.VMEM((columns, width), bf16),
            pltpu.VMEM((places * BLK, columns), bf16),
            pltpu.VMEM((places * BLK, columns), bf16),
            pltpu.VMEM((pairs, BLK, neigh * BLK), f32),
            pltpu.VMEM((rows, columns), bf16),
            pltpu.SemaphoreType.DMA((5 + 2 * places,)),
        ],
        compiler_params=PARAMS,
        cost_estimate=cost(1000, 1000),
        name="attend",
    )(key_blocks, host_ids, host_bias, query_states, out_weight, *k_win, *v_win)
    mixed_out = lax.psum_scatter(share, "head", scatter_dimension=0, tiled=True)

    up, stats = pl.pallas_call(
        upstream_kernel,
        out_shape=[
            jax.ShapeDtypeStruct((long_rows, columns), bf16),
            jax.ShapeDtypeStruct((BLK, BLK), f32),
        ],
        in_specs=[HBM] * 2 + [ANY] + [VMEM] * 2,
        out_specs=[VMEM] * 2,
        scratch_shapes=[
            pltpu.SMEM(key_blocks.shape, i32),
            pltpu.VMEM((columns, width), bf16),
            pltpu.VMEM((rows, width), bf16),
            pltpu.SemaphoreType.DMA((3,)),
        ],
        compiler_params=PARAMS,
        cost_estimate=cost(1000, 1000),
        name="upstream",
    )(key_blocks, out_weight, all_grads, o32, lse)
    up_win = exchange(up, size)

    grad_query = pl.pallas_call(
        functools.partial(query_kernel, size, nsh),
        out_shape=jax.ShapeDtypeStruct((rows, columns), bf16),
        in_specs=[HBM] * 4 + [VMEM] * 2 + ([HBM] + [ANY] * (nsh - 1)) * 2,
        out_specs=VMEM,
        scratch_shapes=scalars
        + [
            pltpu.VMEM((rows, columns), bf16),
            pltpu.VMEM((places * BLK, columns), bf16),
            pltpu.VMEM((places * BLK, columns), bf16),
            pltpu.SemaphoreType.DMA((4 + 2 * places,)),
        ],
        compiler_params=PARAMS,
        cost_estimate=cost(1000, 1000),
        name="query_grad",
    )(key_blocks, host_ids, host_bias, query_states, up, stats, *k_win, *v_win)

    grad_key, grad_value = pl.pallas_call(
        functools.partial(key_kernel, size, nsh, neigh),
        out_shape=[jax.ShapeDtypeStruct((rows, columns), bf16)] * 2,
        in_specs=[HBM] * 5 + [ANY] * (2 * nsh - 1),
        out_specs=[VMEM] * 2,
        scratch_shapes=[
            pltpu.SMEM(host_ids.shape, i32),
            pltpu.SMEM(host_bias.shape, f32),
            pltpu.VMEM((rows, columns), bf16),
            pltpu.VMEM((rows, columns), bf16),
            pltpu.VMEM((nsh * rows, columns), bf16),
            pltpu.VMEM((nsh * long_rows, columns), bf16),
            pltpu.VMEM((nsh + 1, high, BLK), f32),
            pltpu.VMEM((8, BLK), i32),
            pltpu.SMEM((8, BLK), i32),
            pltpu.SMEM((blocks_dev, nsh * blocks_dev + 2), i32),
            pltpu.VMEM((rows, columns), f32),
            pltpu.VMEM((rows, columns), f32),
            pltpu.SemaphoreType.DMA((3 * nsh + 5,)),
        ],
        compiler_params=PARAMS,
        cost_estimate=cost(1000, 1000),
        name="key_grad",
    )(host_ids, host_bias, key_states, value_states, query_states, *q_win[1:], *up_win)

    return (mixed_out, grad_query, grad_key, grad_value)


def solution(mesh):
    in_specs = (
        P("ctx", "head"),
        P("ctx", "head"),
        P("ctx", "head"),
        P("head", None),
        P(("ctx", "head"), None),
        P("ctx", None),
        P(),
        P("head"),
    )
    out_specs = (P(("ctx", "head"), None), P("ctx", "head"), P("ctx", "head"), P("ctx", "head"))
    return jax.shard_map(
        per_device, mesh=mesh, in_specs=in_specs, out_specs=out_specs, check_vma=False
    )
```

```python
import functools

import jax
import jax.numpy as jnp
from jax import lax
from jax.experimental import pallas as pl
from jax.experimental.pallas import tpu as pltpu
from jax.sharding import PartitionSpec as P

HDIM = 128
BLK = 128
HOPS = 2
SCALE = HDIM ** (-0.5)
CUBE = (0, 1, 2, 3, 6, 7)
PAIR = (0, 1, 2, -2, -1)
NT = (((1,), (1,)), ((), ()))
VMEM = pl.BlockSpec(memory_space=pltpu.VMEM)
SMEM = pl.BlockSpec(memory_space=pltpu.SMEM)
ANY = pl.BlockSpec(memory_space=pl.ANY)
HBM = pl.BlockSpec(memory_space=pltpu.HBM)
NEVER = 1e30


def params(mebibytes):
    return pltpu.CompilerParams(vmem_limit_bytes=mebibytes * 1024 * 1024)


def ndot(a, b):
    return lax.dot_general(a, b, (((1,), (0,)), ((), ())), preferred_element_type=jnp.float32)


def tdot(a, b):
    return lax.dot_general(a, b, NT, preferred_element_type=jnp.float32)


def stat_rows(pairs):
    return -(-2 * pairs // 16) * 16


def tag_owner(position, tag, size, tags):
    if tags is CUBE:
        return position ^ tag
    return lax.rem(position + jnp.where(position % 2 == 0, tag, -tag) + size, size)


def find_shard(position, owner, size, tags):
    shard = 0
    for index, tag in enumerate(tags):
        shard = shard + jnp.where(tag_owner(position, tag, size, tags) == owner, index, 0)
    return shard


def permute_from(x, size, source):
    return lax.ppermute(x, "ctx", [(source(i) % size, i) for i in range(size)])


def exchange_pair(x, size):
    sign = lambda i: 1 if i % 2 == 0 else -1
    share = permute_from(x, size, lambda i: i + 2 * sign(i))
    solo = permute_from(x, size, lambda i: i - 2 * sign(i))
    mate = permute_from(x, size, lambda i: i ^ 1)
    return [x, mate, share, solo, permute_from(share, size, lambda i: i ^ 1)]


def exchange_cube(x, size):
    near = permute_from(x, size, lambda i: i ^ 2)
    far = permute_from(near, size, lambda i: i ^ 4)
    mate = permute_from(x, size, lambda i: i ^ 1)
    swap = lambda i: i ^ 1
    return [x, mate, near, permute_from(near, size, swap), far, permute_from(far, size, swap)]


def start_all(pairs, sem, first=0):
    copies = []
    for index, (source, target) in enumerate(pairs):
        copy = pltpu.make_async_copy(source, target, sem.at[first + index])
        copy.start()
        copies.append(copy)
    return copies


def wait_all(copies):
    for copy in copies:
        copy.wait()


def gather_blocks(size, tags, keys, refs, target, sem, first, blocks_dev, neigh):
    position = lax.axis_index("ctx")
    waits = []
    for b in range(blocks_dev):
        for n in range(neigh):
            j = keys[b, n]
            shard = find_shard(position, lax.div(j, blocks_dev), size, tags)
            row = pl.multiple_of(lax.rem(j, blocks_dev) * BLK, BLK)
            place = b * neigh + n
            for index, ref in enumerate(refs):

                @pl.when(shard == index)
                def _(ref=ref, place=place, row=row):
                    pltpu.make_async_copy(
                        ref.at[pl.ds(row, BLK)], target.at[pl.ds(place * BLK, BLK)], sem.at[first + place]
                    ).start()

            waits.append(
                pltpu.make_async_copy(
                    refs[0].at[pl.ds(0, BLK)], target.at[pl.ds(place * BLK, BLK)], sem.at[first + place]
                )
            )
    return waits


def shift_rows(keys, hosts, bias, b, h, blocks_dev, neigh):
    position = lax.axis_index("ctx")
    slot = lax.broadcasted_iota(jnp.int32, (1, neigh * BLK), 1) // BLK
    shift = jnp.zeros((1, neigh * BLK), jnp.float32)
    host = hosts[position * blocks_dev + b]
    for n in range(neigh):
        value = jnp.where(hosts[keys[b, n]] == host, bias[h], 0.0)
        shift = jnp.where(slot == n, value, shift)
    return shift


def piece_owner(me, step, groups, sign):
    return me ^ step if groups == 4 else lax.rem(me + sign * step + groups, groups)


def attend_kernel(size, groups, v_tags, *refs):
    keys_hbm, hosts_hbm, bias_hbm, q_hbm, w_hbm = refs[:5]
    k_refs = refs[5:5 + len(PAIR)]
    v_refs = refs[5 + len(PAIR):5 + len(PAIR) + len(v_tags)]
    rest = refs[5 + len(PAIR) + len(v_tags):]
    part_refs = rest[:groups]
    o32_ref, lse_ref = rest[groups:groups + 2]
    keys, hosts, bias, q_ref, w_ref, kcat, vcat, score, att, turned, sem = rest[groups + 2:]
    rows, columns = q_ref.shape
    blocks_dev, neigh = keys.shape
    heads_dev = columns // HDIM
    small = start_all([(keys_hbm, keys), (hosts_hbm, hosts), (bias_hbm, bias)], sem)
    large = start_all([(q_hbm, q_ref), (w_hbm, w_ref)], sem, 3)
    wait_all(small)
    places = blocks_dev * neigh
    k_waits = gather_blocks(size, PAIR, keys, k_refs, kcat, sem, 5, blocks_dev, neigh)
    v_waits = gather_blocks(size, v_tags, keys, v_refs, vcat, sem, 5 + places, blocks_dev, neigh)
    large[0].wait()
    wait_all(k_waits)
    span = neigh * BLK
    units = [(b, h) for b in range(blocks_dev) for h in range(heads_dev)]
    for b, h in units:
        cols = slice(h * HDIM, (h + 1) * HDIM)
        s = tdot(q_ref[b * BLK:(b + 1) * BLK, cols], kcat[b * span:(b + 1) * span, cols])
        score[b * heads_dev + h] = s * SCALE + shift_rows(keys, hosts, bias, b, h, blocks_dev, neigh)
    wait_all(v_waits)
    lane = lax.broadcasted_iota(jnp.int32, (BLK, BLK), 1)
    lse_all = jnp.zeros((BLK, BLK), jnp.float32)
    for b, h in units:
        cols = slice(h * HDIM, (h + 1) * HDIM)
        s = score[b * heads_dev + h]
        top = jnp.max(s, axis=1, keepdims=True)
        weights = jnp.exp(s - top)
        total = jnp.sum(weights, axis=1, keepdims=True)
        probs = (weights * (1.0 / total)).astype(jnp.bfloat16)
        out = ndot(probs, vcat[b * span:(b + 1) * span, cols])
        o32_ref[b * BLK:(b + 1) * BLK, cols] = out
        att[b * BLK:(b + 1) * BLK, cols] = out.astype(jnp.bfloat16)
        lse_all = jnp.where(lane == b * heads_dev + h, top + jnp.log(total), lse_all)
    lse_ref[...] = lse_all
    large[1].wait()
    me = lax.axis_index("head")
    part = rows // groups
    for step in range(groups):
        owner = piece_owner(me, step, groups, 1)
        turned[step * part:(step + 1) * part, :] = att[pl.ds(pl.multiple_of(owner * part, part), part), :]
    mixed = ndot(turned[...], w_ref[...]).astype(jnp.bfloat16)
    for step in range(groups):
        part_refs[step][...] = mixed[step * part:(step + 1) * part, :]


def upstream_kernel(groups, *refs):
    keys_hbm, w_hbm, own_hbm, o32_ref, lse_ref = refs[:5]
    piece_refs = refs[5:4 + groups]
    rest = refs[4 + groups + len(PAIR):]
    up_ref, stats_ref, keys, w_ref, grads, sem = rest
    rows, columns = o32_ref.shape
    width = w_ref.shape[1]
    blocks_dev, neigh = keys.shape
    heads_dev = columns // HDIM
    part = rows // groups
    cut = width // 4
    w_waits = [
        start_all([(w_hbm.at[:, c * cut:(c + 1) * cut], w_ref.at[:, c * cut:(c + 1) * cut])], sem, c)[0]
        for c in range(4)
    ]
    pieces = (own_hbm,) + tuple(piece_refs)
    wait_all(
        start_all(
            [(ref, grads.at[pl.ds(step * part, part)]) for step, ref in enumerate(pieces)]
            + [(keys_hbm, keys)],
            sem,
            4,
        )
    )
    total = jnp.zeros((rows, columns), jnp.float32)
    for c in range(4):
        w_waits[c].wait()
        total = total + tdot(grads[:, c * cut:(c + 1) * cut], w_ref[:, c * cut:(c + 1) * cut])
    me = lax.axis_index("head")
    product = total.astype(jnp.bfloat16)
    for step in range(groups):
        owner = piece_owner(me, step, groups, -1)
        up_ref[pl.ds(pl.multiple_of(owner * part, part), part), :] = product[
            step * part:(step + 1) * part, :
        ]
    pairs = blocks_dev * heads_dev
    lane = lax.broadcasted_iota(jnp.int32, (BLK, BLK), 1)
    stats = lse_ref[...]
    for b in range(blocks_dev):
        for h in range(heads_dev):
            cols = slice(h * HDIM, (h + 1) * HDIM)
            up = up_ref[b * BLK:(b + 1) * BLK, cols].astype(jnp.float32)
            term = jnp.sum(up * o32_ref[b * BLK:(b + 1) * BLK, cols], axis=1, keepdims=True)
            stats = jnp.where(lane == pairs + b * heads_dev + h, term, stats)
    stats_ref[...] = stats
    high = stat_rows(pairs)
    turned = jnp.transpose(stats)[:high, :]
    up_ref[rows:, :] = jnp.zeros((up_ref.shape[0] - rows, columns), jnp.bfloat16)
    pieces = []
    for index in range(3):
        piece = turned.astype(jnp.bfloat16)
        turned = turned - piece.astype(jnp.float32)
        pieces.append(piece)
    spot = lax.broadcasted_iota(jnp.int32, (high, BLK), 1)
    line = lax.broadcasted_iota(jnp.int32, (high, BLK), 0)
    listed = jnp.zeros((high, BLK), jnp.int32)
    for b in range(blocks_dev):
        for n in range(neigh):
            listed = jnp.where(spot == b * neigh + n, keys[b, n], listed)
    listed = jnp.where(line == 0, listed >> 7, listed & 127)
    pieces.append(listed.astype(jnp.float32).astype(jnp.bfloat16))
    for index, piece in enumerate(pieces):
        row = rows + high * (index * BLK // columns)
        col = index * BLK % columns
        up_ref[row:row + high, col:col + BLK] = piece


def query_kernel(size, v_tags, *refs):
    keys_hbm, hosts_hbm, bias_hbm, q_hbm, up_ref, stats_ref = refs[:6]
    k_refs = refs[6:6 + len(PAIR)]
    v_refs = refs[6 + len(PAIR):6 + len(PAIR) + len(v_tags)]
    dq_ref, keys, hosts, bias, q_ref, kcat, vcat, sem = refs[6 + len(PAIR) + len(v_tags):]
    rows, columns = q_ref.shape
    blocks_dev, neigh = keys.shape
    heads_dev = columns // HDIM
    pairs = blocks_dev * heads_dev
    small = start_all([(keys_hbm, keys), (hosts_hbm, hosts), (bias_hbm, bias)], sem)
    large = start_all([(q_hbm, q_ref)], sem, 3)
    wait_all(small)
    places = blocks_dev * neigh
    waits = gather_blocks(size, PAIR, keys, k_refs, kcat, sem, 4, blocks_dev, neigh)
    waits += gather_blocks(size, v_tags, keys, v_refs, vcat, sem, 4 + places, blocks_dev, neigh)
    wait_all(large)
    wait_all(waits)
    span = neigh * BLK
    for b in range(blocks_dev):
        for h in range(heads_dev):
            cols = slice(h * HDIM, (h + 1) * HDIM)
            pair = b * heads_dev + h
            q = q_ref[b * BLK:(b + 1) * BLK, cols]
            up = up_ref[b * BLK:(b + 1) * BLK, cols]
            k = kcat[b * span:(b + 1) * span, cols]
            lse = stats_ref[:, pair:pair + 1]
            term = stats_ref[:, pairs + pair:pairs + pair + 1]
            shift = shift_rows(keys, hosts, bias, b, h, blocks_dev, neigh)
            p = jnp.exp(tdot(q, k) * SCALE + shift - lse)
            dp = tdot(up, vcat[b * span:(b + 1) * span, cols])
            ds = (p * (dp - term) * SCALE).astype(jnp.bfloat16)
            dq_ref[b * BLK:(b + 1) * BLK, cols] = ndot(ds, k).astype(jnp.bfloat16)


def key_kernel(size, neigh, *refs):
    nsh = len(PAIR)
    hosts_hbm, bias_hbm, k_hbm, v_hbm = refs[:4]
    q_refs = refs[4:4 + nsh]
    up_refs = refs[4 + nsh:4 + 2 * nsh]
    dk_ref, dv_ref = refs[4 + 2 * nsh:6 + 2 * nsh]
    (hosts, bias, k_ref, v_ref, qwin, upwin, stats, lists, keys, hits, dk_acc, dv_acc, sem) = refs[
        6 + 2 * nsh:
    ]
    rows, columns = k_ref.shape
    long_rows = up_refs[0].shape[0]
    blocks_dev = rows // BLK
    heads_dev = columns // HDIM
    pairs = blocks_dev * heads_dev
    high = stat_rows(pairs)
    position = lax.axis_index("ctx")
    tail = [
        (ref.at[pl.ds(rows, long_rows - rows)], upwin.at[pl.ds(i * long_rows + rows, long_rows - rows)])
        for i, ref in enumerate(up_refs)
    ]
    first = start_all(tail, sem)
    body = [(ref.at[pl.ds(0, rows)], upwin.at[pl.ds(i * long_rows, rows)]) for i, ref in enumerate(up_refs)]
    body += [(ref, qwin.at[pl.ds(i * rows, rows)]) for i, ref in enumerate(q_refs)]
    body += [(hosts_hbm, hosts), (bias_hbm, bias), (k_hbm, k_ref), (v_hbm, v_ref)]
    later = start_all(body, sem, nsh)
    dk_acc[...] = jnp.zeros_like(dk_acc)
    dv_acc[...] = jnp.zeros_like(dv_acc)
    wait_all(first)

    def part_of(index, piece):
        row = index * long_rows + rows + high * (piece * BLK // columns)
        col = piece * BLK % columns
        return upwin[row:row + high, col:col + BLK].astype(jnp.float32)

    for index in range(nsh):
        stats[index] = (part_of(index, 2) + part_of(index, 1)) + part_of(index, 0)
        listed = part_of(index, 3).astype(jnp.int32)
        lists[index:index + 1, :] = listed[0:1, :] * 128 + listed[1:2, :]
    stats[nsh] = jnp.full((high, BLK), NEVER, jnp.float32)
    copy = pltpu.make_async_copy(lists, keys, sem.at[3 * nsh + 4])
    copy.start()
    copy.wait()

    counts = []
    for own in range(blocks_dev):
        mine = position * blocks_dev + own
        count = 0
        for index in range(nsh):
            for inner in range(blocks_dev):
                hit = keys[index, inner * neigh] == mine
                for n in range(1, neigh):
                    hit = hit | (keys[index, inner * neigh + n] == mine)
                hits[own, count] = index * blocks_dev + inner
                count = count + jnp.where(hit, 1, 0)
        hits[own, count] = -1
        counts.append(count)
    wait_all(later)

    for own in range(blocks_dev):
        mine = position * blocks_dev + own
        krow = slice(own * BLK, (own + 1) * BLK)

        def visit(step, carry, own=own, mine=mine, krow=krow):
            qs, ups, sames, lses, terms = [], [], [], [], []
            for turn in range(2):
                entry = hits[own, 2 * step + turn]
                spare = entry < 0
                entry = jnp.where(spare, 0, entry)
                shard = lax.div(entry, blocks_dev)
                inner = lax.rem(entry, blocks_dev)
                owner = 0
                for index, tag in enumerate(PAIR):
                    owner = owner + jnp.where(shard == index, tag_owner(position, tag, size, PAIR), 0)
                sames.append(hosts[owner * blocks_dev + inner] == hosts[mine])
                qs.append(pl.ds(pl.multiple_of(shard * rows + inner * BLK, BLK), BLK))
                ups.append(pl.ds(pl.multiple_of(shard * long_rows + inner * BLK, 16), BLK))
                lses.append((jnp.where(spare, nsh, shard), inner))
                terms.append((shard, inner))
            for h in range(heads_dev):
                cols = slice(h * HDIM, (h + 1) * HDIM)
                k = k_ref[krow, cols]
                v = v_ref[krow, cols]
                q = jnp.concatenate([qwin[r, cols] for r in qs], axis=0)
                up = jnp.concatenate([upwin[r, cols] for r in ups], axis=0)
                less = jnp.concatenate(
                    [
                        stats[shard, pl.ds(inner * heads_dev + h, 1), :] - jnp.where(same, bias[h], 0.0)
                        for (shard, inner), same in zip(lses, sames)
                    ],
                    axis=1,
                )
                term = jnp.concatenate(
                    [stats[shard, pl.ds(pairs + inner * heads_dev + h, 1), :] for shard, inner in terms],
                    axis=1,
                )
                p = jnp.exp(tdot(k, q) * SCALE - less)
                ds = (p * (tdot(v, up) - term) * SCALE).astype(jnp.bfloat16)
                dk_acc[krow, cols] += ndot(ds, q)
                dv_acc[krow, cols] += ndot(p.astype(jnp.bfloat16), up)
            return carry

        lax.fori_loop(0, lax.div(counts[own] + 1, 2), visit, 0)
    dk_ref[...] = dk_acc[...].astype(jnp.bfloat16)
    dv_ref[...] = dv_acc[...].astype(jnp.bfloat16)


def copy_kernel(count, extra, *refs):
    wait_all(start_all(list(zip(refs[:count], refs[count + extra:2 * count + extra])), refs[-1]))


def copies_after(arrays, before):
    return pl.pallas_call(
        functools.partial(copy_kernel, len(arrays), len(before)),
        out_shape=[jax.ShapeDtypeStruct(x.shape, x.dtype) for x in arrays],
        in_specs=[ANY] * (len(arrays) + len(before)),
        out_specs=[ANY] * len(arrays),
        scratch_shapes=[pltpu.SemaphoreType.DMA((len(arrays),))],
        compiler_params=params(60),
        cost_estimate=cost(1000, 1000),
        name="copies_after",
    )(*arrays, *before)


def cost(flops, nbytes):
    return pl.CostEstimate(flops=flops, bytes_accessed=nbytes, transcendentals=0)


def per_device(
    query_states, key_states, value_states, out_weight, grad_mixed, key_blocks, host_ids, host_bias
):
    size = lax.axis_size("ctx")
    rows, columns = query_states.shape
    width = out_weight.shape[1]
    blocks_dev, neigh = key_blocks.shape
    heads_dev = columns // HDIM
    pairs = blocks_dev * heads_dev
    places = blocks_dev * neigh
    groups = lax.axis_size("head")
    part = rows // groups
    v_tags = CUBE if size == 8 else PAIR
    nsh = len(PAIR)
    bf16, f32, i32 = jnp.bfloat16, jnp.float32, jnp.int32
    high = stat_rows(pairs)
    extra = high * (-(-4 * BLK // columns))
    long_rows = rows + extra

    def ring(x, step):
        return lax.ppermute(x, "head", [(i, (i + step) % groups) for i in range(groups)])

    def flip(x, mask):
        return lax.ppermute(x, "head", [(i, i ^ mask) for i in range(groups)])

    paired = groups == 4
    v_win = exchange_cube(value_states, size) if v_tags is CUBE else exchange_pair(value_states, size)
    k_win = exchange_pair(key_states, size)
    if paired:
        opposite = flip(grad_mixed, 2)
        beside = flip(grad_mixed, 1)
        pieces = [grad_mixed, beside, opposite, flip(opposite, 1)]
    else:
        pieces = [grad_mixed] + [ring(grad_mixed, step) for step in range(1, groups)]
    (late_query,) = copies_after((query_states,), tuple(pieces[1:3]))
    q_win = exchange_pair(late_query, size)
    scalars = [
        pltpu.SMEM(key_blocks.shape, i32),
        pltpu.SMEM(host_ids.shape, i32),
        pltpu.SMEM(host_bias.shape, f32),
    ]

    parts_o32_lse = pl.pallas_call(
        functools.partial(attend_kernel, size, groups, v_tags),
        out_shape=[jax.ShapeDtypeStruct((part, width), bf16)] * groups
        + [jax.ShapeDtypeStruct((rows, columns), f32), jax.ShapeDtypeStruct((BLK, BLK), f32)],
        in_specs=[HBM] * 5 + [ANY] * (len(PAIR) + len(v_tags)),
        out_specs=[VMEM] * (groups + 2),
        scratch_shapes=scalars
        + [
            pltpu.VMEM((rows, columns), bf16),
            pltpu.VMEM((columns, width), bf16),
            pltpu.VMEM((places * BLK, columns), bf16),
            pltpu.VMEM((places * BLK, columns), bf16),
            pltpu.VMEM((pairs, BLK, neigh * BLK), f32),
            pltpu.VMEM((rows, columns), bf16),
            pltpu.VMEM((rows, columns), bf16),
            pltpu.SemaphoreType.DMA((5 + 2 * places,)),
        ],
        compiler_params=params(60),
        cost_estimate=cost(4 * 10**9, 8 * 10**6),
        name="attend",
    )(key_blocks, host_ids, host_bias, query_states, out_weight, *k_win, *v_win)
    parts = parts_o32_lse[:groups]
    o32, lse = parts_o32_lse[groups:]
    mixed = parts[0].astype(f32)
    if paired:
        relay = flip(parts[3], 1)
        beside_sum = flip(parts[1], 1)
        passed = (parts[2].astype(f32) + relay.astype(f32)).astype(bf16)
        arrived = [beside_sum, flip(passed, 2)]
    else:
        arrived = [ring(parts[step], step) for step in range(1, groups)]

    up, stats = pl.pallas_call(
        functools.partial(upstream_kernel, groups),
        out_shape=[
            jax.ShapeDtypeStruct((long_rows, columns), bf16),
            jax.ShapeDtypeStruct((BLK, BLK), f32),
        ],
        in_specs=[HBM] * 3 + [VMEM] * 2 + [ANY] * (groups - 1 + len(PAIR)),
        out_specs=[VMEM] * 2,
        scratch_shapes=[
            pltpu.SMEM(key_blocks.shape, i32),
            pltpu.VMEM((columns, width), bf16),
            pltpu.VMEM((rows, width), bf16),
            pltpu.SemaphoreType.DMA((5 + groups,)),
        ],
        compiler_params=params(60),
        cost_estimate=cost(6 * 10**9, 6 * 10**6),
        name="upstream",
    )(key_blocks, out_weight, grad_mixed, o32, lse, *pieces[1:], *q_win)
    up_win = exchange_pair(up, size)

    grad_query = pl.pallas_call(
        functools.partial(query_kernel, size, v_tags),
        out_shape=jax.ShapeDtypeStruct((rows, columns), bf16),
        in_specs=[HBM] * 4 + [VMEM] * 2 + [ANY] * (len(PAIR) + len(v_tags)),
        out_specs=VMEM,
        scratch_shapes=scalars
        + [
            pltpu.VMEM((rows, columns), bf16),
            pltpu.VMEM((places * BLK, columns), bf16),
            pltpu.VMEM((places * BLK, columns), bf16),
            pltpu.SemaphoreType.DMA((4 + 2 * places,)),
        ],
        compiler_params=params(60),
        cost_estimate=cost(10**9, 10**6),
        name="query_grad",
    )(key_blocks, host_ids, host_bias, query_states, up, stats, *k_win, *v_win)

    grad_key, grad_value = pl.pallas_call(
        functools.partial(key_kernel, size, neigh),
        out_shape=[jax.ShapeDtypeStruct((rows, columns), bf16)] * 2,
        in_specs=[HBM] * 5 + [ANY] * (2 * nsh - 1),
        out_specs=[VMEM] * 2,
        scratch_shapes=[
            pltpu.SMEM(host_ids.shape, i32),
            pltpu.SMEM(host_bias.shape, f32),
            pltpu.VMEM((rows, columns), bf16),
            pltpu.VMEM((rows, columns), bf16),
            pltpu.VMEM((nsh * rows, columns), bf16),
            pltpu.VMEM((nsh * long_rows, columns), bf16),
            pltpu.VMEM((nsh + 1, high, BLK), f32),
            pltpu.VMEM((8, BLK), i32),
            pltpu.SMEM((8, BLK), i32),
            pltpu.SMEM((blocks_dev, nsh * blocks_dev + 2), i32),
            pltpu.VMEM((rows, columns), f32),
            pltpu.VMEM((rows, columns), f32),
            pltpu.SemaphoreType.DMA((3 * nsh + 5,)),
        ],
        compiler_params=params(60),
        cost_estimate=cost(10**9, 10**6),
        name="key_grad",
    )(host_ids, host_bias, key_states, value_states, query_states, *q_win[1:], *up_win)

    for piece in arrived:
        mixed = mixed + piece.astype(f32)
    return (mixed.astype(bf16), grad_query, grad_key, grad_value)


def solution(mesh):
    in_specs = (
        P("ctx", "head"),
        P("ctx", "head"),
        P("ctx", "head"),
        P("head", None),
        P(("ctx", "head"), None),
        P("ctx", None),
        P(),
        P("head"),
    )
    out_specs = (P(("ctx", "head"), None), P("ctx", "head"), P("ctx", "head"), P("ctx", "head"))
    return jax.shard_map(
        per_device, mesh=mesh, in_specs=in_specs, out_specs=out_specs, check_vma=False
    )
```

```python
import functools

import jax
import jax.numpy as jnp
from jax import lax
from jax.experimental import pallas as pl
from jax.experimental.pallas import tpu as pltpu
from jax.sharding import PartitionSpec as P

HDIM = 128
BLK = 128
HOPS = 2
SCALE = HDIM ** (-0.5)
CUBE = (0, 1, 2, 3, 6, 7)
PAIR = (0, 1, 2, -2, -1)
NT = (((1,), (1,)), ((), ()))
VMEM = pl.BlockSpec(memory_space=pltpu.VMEM)
SMEM = pl.BlockSpec(memory_space=pltpu.SMEM)
ANY = pl.BlockSpec(memory_space=pl.ANY)
HBM = pl.BlockSpec(memory_space=pltpu.HBM)
NEVER = 1e30


def params(mebibytes):
    return pltpu.CompilerParams(vmem_limit_bytes=mebibytes * 1024 * 1024)


def ndot(a, b):
    return lax.dot_general(a, b, (((1,), (0,)), ((), ())), preferred_element_type=jnp.float32)


def tdot(a, b):
    return lax.dot_general(a, b, NT, preferred_element_type=jnp.float32)


def stat_rows(pairs):
    return -(-2 * pairs // 16) * 16


def tag_owner(position, tag, size, tags):
    if tags is CUBE:
        return position ^ tag
    return lax.rem(position + jnp.where(position % 2 == 0, tag, -tag) + size, size)


def find_shard(position, owner, size, tags):
    shard = 0
    for index, tag in enumerate(tags):
        shard = shard + jnp.where(tag_owner(position, tag, size, tags) == owner, index, 0)
    return shard


def permute_from(x, size, source):
    return lax.ppermute(x, "ctx", [(source(i) % size, i) for i in range(size)])


def exchange_pair(x, size):
    sign = lambda i: 1 if i % 2 == 0 else -1
    share = permute_from(x, size, lambda i: i + 2 * sign(i))
    solo = permute_from(x, size, lambda i: i - 2 * sign(i))
    mate = permute_from(x, size, lambda i: i ^ 1)
    return [x, mate, share, solo, permute_from(share, size, lambda i: i ^ 1)]


def exchange_cube(x, size):
    near = permute_from(x, size, lambda i: i ^ 2)
    far = permute_from(near, size, lambda i: i ^ 4)
    mate = permute_from(x, size, lambda i: i ^ 1)
    swap = lambda i: i ^ 1
    return [x, mate, near, permute_from(near, size, swap), far, permute_from(far, size, swap)]


def start_all(pairs, sem, first=0):
    copies = []
    for index, (source, target) in enumerate(pairs):
        copy = pltpu.make_async_copy(source, target, sem.at[first + index])
        copy.start()
        copies.append(copy)
    return copies


def wait_all(copies):
    for copy in copies:
        copy.wait()


def gather_blocks(size, tags, keys, refs, target, sem, first, blocks_dev, neigh):
    position = lax.axis_index("ctx")
    waits = []
    for b in range(blocks_dev):
        for n in range(neigh):
            j = keys[b, n]
            shard = find_shard(position, lax.div(j, blocks_dev), size, tags)
            row = pl.multiple_of(lax.rem(j, blocks_dev) * BLK, BLK)
            place = b * neigh + n
            for index, ref in enumerate(refs):

                @pl.when(shard == index)
                def _(ref=ref, place=place, row=row):
                    pltpu.make_async_copy(
                        ref.at[pl.ds(row, BLK)], target.at[pl.ds(place * BLK, BLK)], sem.at[first + place]
                    ).start()

            waits.append(
                pltpu.make_async_copy(
                    refs[0].at[pl.ds(0, BLK)], target.at[pl.ds(place * BLK, BLK)], sem.at[first + place]
                )
            )
    return waits


def shift_rows(keys, hosts, bias, b, h, blocks_dev, neigh):
    position = lax.axis_index("ctx")
    slot = lax.broadcasted_iota(jnp.int32, (1, neigh * BLK), 1) // BLK
    shift = jnp.zeros((1, neigh * BLK), jnp.float32)
    host = hosts[position * blocks_dev + b]
    for n in range(neigh):
        value = jnp.where(hosts[keys[b, n]] == host, bias[h], 0.0)
        shift = jnp.where(slot == n, value, shift)
    return shift


def piece_owner(me, step, groups, sign):
    return me ^ step if groups == 4 else lax.rem(me + sign * step + groups, groups)


def attend_kernel(size, groups, v_tags, *refs):
    keys_hbm, hosts_hbm, bias_hbm, q_hbm, w_hbm = refs[:5]
    k_refs = refs[5:5 + len(PAIR)]
    v_refs = refs[5 + len(PAIR):5 + len(PAIR) + len(v_tags)]
    rest = refs[5 + len(PAIR) + len(v_tags):]
    part_refs = rest[:groups]
    o32_ref, lse_ref = rest[groups:groups + 2]
    keys, hosts, bias, q_ref, w_ref, kcat, vcat, score, att, turned, sem = rest[groups + 2:]
    rows, columns = q_ref.shape
    blocks_dev, neigh = keys.shape
    heads_dev = columns // HDIM
    small = start_all([(keys_hbm, keys), (hosts_hbm, hosts), (bias_hbm, bias)], sem)
    large = start_all([(q_hbm, q_ref), (w_hbm, w_ref)], sem, 3)
    wait_all(small)
    places = blocks_dev * neigh
    k_waits = gather_blocks(size, PAIR, keys, k_refs, kcat, sem, 5, blocks_dev, neigh)
    v_waits = gather_blocks(size, v_tags, keys, v_refs, vcat, sem, 5 + places, blocks_dev, neigh)
    large[0].wait()
    wait_all(k_waits)
    span = neigh * BLK
    units = [(b, h) for b in range(blocks_dev) for h in range(heads_dev)]
    for b, h in units:
        cols = slice(h * HDIM, (h + 1) * HDIM)
        s = tdot(q_ref[b * BLK:(b + 1) * BLK, cols], kcat[b * span:(b + 1) * span, cols])
        score[b * heads_dev + h] = s * SCALE + shift_rows(keys, hosts, bias, b, h, blocks_dev, neigh)
    wait_all(v_waits)
    lane = lax.broadcasted_iota(jnp.int32, (BLK, BLK), 1)
    lse_all = jnp.zeros((BLK, BLK), jnp.float32)
    for b, h in units:
        cols = slice(h * HDIM, (h + 1) * HDIM)
        s = score[b * heads_dev + h]
        top = jnp.max(s, axis=1, keepdims=True)
        weights = jnp.exp(s - top)
        total = jnp.sum(weights, axis=1, keepdims=True)
        probs = (weights * (1.0 / total)).astype(jnp.bfloat16)
        out = ndot(probs, vcat[b * span:(b + 1) * span, cols])
        o32_ref[b * BLK:(b + 1) * BLK, cols] = out
        att[b * BLK:(b + 1) * BLK, cols] = out.astype(jnp.bfloat16)
        lse_all = jnp.where(lane == b * heads_dev + h, top + jnp.log(total), lse_all)
    lse_ref[...] = lse_all
    large[1].wait()
    me = lax.axis_index("head")
    part = rows // groups
    for step in range(groups):
        owner = piece_owner(me, step, groups, 1)
        turned[step * part:(step + 1) * part, :] = att[pl.ds(pl.multiple_of(owner * part, part), part), :]
    mixed = ndot(turned[...], w_ref[...]).astype(jnp.bfloat16)
    for step in range(groups):
        part_refs[step][...] = mixed[step * part:(step + 1) * part, :]


def upstream_kernel(groups, *refs):
    keys_hbm, w_hbm, own_hbm, o32_ref, lse_ref = refs[:5]
    piece_refs = refs[5:4 + groups]
    rest = refs[8 + groups:]
    up_ref, stats_ref, keys, w_ref, grads, sem = rest
    rows, columns = o32_ref.shape
    width = w_ref.shape[1]
    blocks_dev, neigh = keys.shape
    heads_dev = columns // HDIM
    part = rows // groups
    cut = width // 4
    w_waits = [
        start_all([(w_hbm.at[:, c * cut:(c + 1) * cut], w_ref.at[:, c * cut:(c + 1) * cut])], sem, c)[0]
        for c in range(4)
    ]
    pieces = (own_hbm,) + tuple(piece_refs)
    wait_all(
        start_all(
            [(ref, grads.at[pl.ds(step * part, part)]) for step, ref in enumerate(pieces)]
            + [(keys_hbm, keys)],
            sem,
            4,
        )
    )
    total = jnp.zeros((rows, columns), jnp.float32)
    for c in range(4):
        w_waits[c].wait()
        total = total + tdot(grads[:, c * cut:(c + 1) * cut], w_ref[:, c * cut:(c + 1) * cut])
    me = lax.axis_index("head")
    product = total.astype(jnp.bfloat16)
    for step in range(groups):
        owner = piece_owner(me, step, groups, -1)
        up_ref[pl.ds(pl.multiple_of(owner * part, part), part), :] = product[
            step * part:(step + 1) * part, :
        ]
    pairs = blocks_dev * heads_dev
    lane = lax.broadcasted_iota(jnp.int32, (BLK, BLK), 1)
    stats = lse_ref[...]
    for b in range(blocks_dev):
        for h in range(heads_dev):
            cols = slice(h * HDIM, (h + 1) * HDIM)
            up = up_ref[b * BLK:(b + 1) * BLK, cols].astype(jnp.float32)
            term = jnp.sum(up * o32_ref[b * BLK:(b + 1) * BLK, cols], axis=1, keepdims=True)
            stats = jnp.where(lane == pairs + b * heads_dev + h, term, stats)
    stats_ref[...] = stats
    high = stat_rows(pairs)
    turned = jnp.transpose(stats)[:high, :]
    up_ref[rows:, :] = jnp.zeros((up_ref.shape[0] - rows, columns), jnp.bfloat16)
    pieces = []
    for index in range(3):
        piece = turned.astype(jnp.bfloat16)
        turned = turned - piece.astype(jnp.float32)
        pieces.append(piece)
    spot = lax.broadcasted_iota(jnp.int32, (high, BLK), 1)
    line = lax.broadcasted_iota(jnp.int32, (high, BLK), 0)
    listed = jnp.zeros((high, BLK), jnp.int32)
    for b in range(blocks_dev):
        for n in range(neigh):
            listed = jnp.where(spot == b * neigh + n, keys[b, n], listed)
    listed = jnp.where(line == 0, listed >> 7, listed & 127)
    pieces.append(listed.astype(jnp.float32).astype(jnp.bfloat16))
    for index, piece in enumerate(pieces):
        row = rows + high * (index * BLK // columns)
        col = index * BLK % columns
        up_ref[row:row + high, col:col + BLK] = piece


def query_kernel(size, v_tags, *refs):
    keys_hbm, hosts_hbm, bias_hbm, q_hbm, up_ref, stats_ref = refs[:6]
    k_refs = refs[6:6 + len(PAIR)]
    v_refs = refs[6 + len(PAIR):6 + len(PAIR) + len(v_tags)]
    dq_ref, keys, hosts, bias, q_ref, kcat, vcat, sem = refs[7 + len(PAIR) + len(v_tags):]
    rows, columns = q_ref.shape
    blocks_dev, neigh = keys.shape
    heads_dev = columns // HDIM
    pairs = blocks_dev * heads_dev
    small = start_all([(keys_hbm, keys), (hosts_hbm, hosts), (bias_hbm, bias)], sem)
    large = start_all([(q_hbm, q_ref)], sem, 3)
    wait_all(small)
    places = blocks_dev * neigh
    waits = gather_blocks(size, PAIR, keys, k_refs, kcat, sem, 4, blocks_dev, neigh)
    waits += gather_blocks(size, v_tags, keys, v_refs, vcat, sem, 4 + places, blocks_dev, neigh)
    wait_all(large)
    wait_all(waits)
    span = neigh * BLK
    for b in range(blocks_dev):
        for h in range(heads_dev):
            cols = slice(h * HDIM, (h + 1) * HDIM)
            pair = b * heads_dev + h
            q = q_ref[b * BLK:(b + 1) * BLK, cols]
            up = up_ref[b * BLK:(b + 1) * BLK, cols]
            k = kcat[b * span:(b + 1) * span, cols]
            lse = stats_ref[:, pair:pair + 1]
            term = stats_ref[:, pairs + pair:pairs + pair + 1]
            shift = shift_rows(keys, hosts, bias, b, h, blocks_dev, neigh)
            p = jnp.exp(tdot(q, k) * SCALE + shift - lse)
            dp = tdot(up, vcat[b * span:(b + 1) * span, cols])
            ds = (p * (dp - term) * SCALE).astype(jnp.bfloat16)
            dq_ref[b * BLK:(b + 1) * BLK, cols] = ndot(ds, k).astype(jnp.bfloat16)


def key_kernel(size, neigh, *refs):
    nsh = len(PAIR)
    hosts_hbm, bias_hbm, k_hbm, v_hbm = refs[:4]
    q_refs = refs[4:4 + nsh]
    up_refs = refs[4 + nsh:4 + 2 * nsh]
    dk_ref, dv_ref = refs[4 + 2 * nsh:6 + 2 * nsh]
    (hosts, bias, k_ref, v_ref, qwin, upwin, stats, lists, keys, hits, dk_acc, dv_acc, sem) = refs[
        6 + 2 * nsh:
    ]
    rows, columns = k_ref.shape
    long_rows = up_refs[0].shape[0]
    blocks_dev = rows // BLK
    heads_dev = columns // HDIM
    pairs = blocks_dev * heads_dev
    high = stat_rows(pairs)
    position = lax.axis_index("ctx")
    tail = [
        (ref.at[pl.ds(rows, long_rows - rows)], upwin.at[pl.ds(i * long_rows + rows, long_rows - rows)])
        for i, ref in enumerate(up_refs)
    ]
    first = start_all(tail, sem)
    body = [(ref.at[pl.ds(0, rows)], upwin.at[pl.ds(i * long_rows, rows)]) for i, ref in enumerate(up_refs)]
    body += [(ref, qwin.at[pl.ds(i * rows, rows)]) for i, ref in enumerate(q_refs)]
    body += [(hosts_hbm, hosts), (bias_hbm, bias), (k_hbm, k_ref), (v_hbm, v_ref)]
    later = start_all(body, sem, nsh)
    dk_acc[...] = jnp.zeros_like(dk_acc)
    dv_acc[...] = jnp.zeros_like(dv_acc)
    wait_all(first)

    def part_of(index, piece):
        row = index * long_rows + rows + high * (piece * BLK // columns)
        col = piece * BLK % columns
        return upwin[row:row + high, col:col + BLK].astype(jnp.float32)

    for index in range(nsh):
        stats[index] = (part_of(index, 2) + part_of(index, 1)) + part_of(index, 0)
        listed = part_of(index, 3).astype(jnp.int32)
        lists[index:index + 1, :] = listed[0:1, :] * 128 + listed[1:2, :]
    stats[nsh] = jnp.full((high, BLK), NEVER, jnp.float32)
    copy = pltpu.make_async_copy(lists, keys, sem.at[3 * nsh + 4])
    copy.start()
    copy.wait()

    counts = []
    for own in range(blocks_dev):
        mine = position * blocks_dev + own
        count = 0
        for index in range(nsh):
            for inner in range(blocks_dev):
                hit = keys[index, inner * neigh] == mine
                for n in range(1, neigh):
                    hit = hit | (keys[index, inner * neigh + n] == mine)
                hits[own, count] = index * blocks_dev + inner
                count = count + jnp.where(hit, 1, 0)
        hits[own, count] = -1
        counts.append(count)
    wait_all(later)

    for own in range(blocks_dev):
        mine = position * blocks_dev + own
        krow = slice(own * BLK, (own + 1) * BLK)

        def visit(step, carry, own=own, mine=mine, krow=krow):
            qs, ups, sames, lses, terms = [], [], [], [], []
            for turn in range(2):
                entry = hits[own, 2 * step + turn]
                spare = entry < 0
                entry = jnp.where(spare, 0, entry)
                shard = lax.div(entry, blocks_dev)
                inner = lax.rem(entry, blocks_dev)
                owner = 0
                for index, tag in enumerate(PAIR):
                    owner = owner + jnp.where(shard == index, tag_owner(position, tag, size, PAIR), 0)
                sames.append(hosts[owner * blocks_dev + inner] == hosts[mine])
                qs.append(pl.ds(pl.multiple_of(shard * rows + inner * BLK, BLK), BLK))
                ups.append(pl.ds(pl.multiple_of(shard * long_rows + inner * BLK, 16), BLK))
                lses.append((jnp.where(spare, nsh, shard), inner))
                terms.append((shard, inner))
            for h in range(heads_dev):
                cols = slice(h * HDIM, (h + 1) * HDIM)
                k = k_ref[krow, cols]
                v = v_ref[krow, cols]
                q = jnp.concatenate([qwin[r, cols] for r in qs], axis=0)
                up = jnp.concatenate([upwin[r, cols] for r in ups], axis=0)
                less = jnp.concatenate(
                    [
                        stats[shard, pl.ds(inner * heads_dev + h, 1), :] - jnp.where(same, bias[h], 0.0)
                        for (shard, inner), same in zip(lses, sames)
                    ],
                    axis=1,
                )
                term = jnp.concatenate(
                    [stats[shard, pl.ds(pairs + inner * heads_dev + h, 1), :] for shard, inner in terms],
                    axis=1,
                )
                p = jnp.exp(tdot(k, q) * SCALE - less)
                ds = (p * (tdot(v, up) - term) * SCALE).astype(jnp.bfloat16)
                dk_acc[krow, cols] += ndot(ds, q)
                dv_acc[krow, cols] += ndot(p.astype(jnp.bfloat16), up)
            return carry

        lax.fori_loop(0, lax.div(counts[own] + 1, 2), visit, 0)
    dk_ref[...] = dk_acc[...].astype(jnp.bfloat16)
    dv_ref[...] = dv_acc[...].astype(jnp.bfloat16)


def copy_kernel(count, extra, *refs):
    sources, targets = refs[:count], refs[count + extra:2 * count + extra]
    between, sem = refs[2 * count + extra:-1], refs[-1]
    wait_all(start_all(list(zip(sources, between)), sem))
    wait_all(start_all(list(zip(between, targets)), sem))


def copies_after(arrays, before):
    return pl.pallas_call(
        functools.partial(copy_kernel, len(arrays), len(before)),
        out_shape=[jax.ShapeDtypeStruct(x.shape, x.dtype) for x in arrays],
        in_specs=[ANY] * (len(arrays) + len(before)),
        out_specs=[ANY] * len(arrays),
        scratch_shapes=[pltpu.VMEM(x.shape, x.dtype) for x in arrays]
        + [pltpu.SemaphoreType.DMA((len(arrays),))],
        compiler_params=params(60),
        cost_estimate=cost(1000, 1000),
        name="copies_after",
    )(*arrays, *before)


def cost(flops, nbytes):
    return pl.CostEstimate(flops=flops, bytes_accessed=nbytes, transcendentals=0)


def per_device(
    query_states, key_states, value_states, out_weight, grad_mixed, key_blocks, host_ids, host_bias
):
    size = lax.axis_size("ctx")
    rows, columns = query_states.shape
    width = out_weight.shape[1]
    blocks_dev, neigh = key_blocks.shape
    heads_dev = columns // HDIM
    pairs = blocks_dev * heads_dev
    places = blocks_dev * neigh
    groups = lax.axis_size("head")
    part = rows // groups
    v_tags = CUBE if size == 8 else PAIR
    nsh = len(PAIR)
    bf16, f32, i32 = jnp.bfloat16, jnp.float32, jnp.int32
    high = stat_rows(pairs)
    extra = high * (-(-4 * BLK // columns))
    long_rows = rows + extra

    def ring(x, step):
        return lax.ppermute(x, "head", [(i, (i + step) % groups) for i in range(groups)])

    def flip(x, mask):
        return lax.ppermute(x, "head", [(i, i ^ mask) for i in range(groups)])

    paired = groups == 4
    v_win = exchange_cube(value_states, size) if v_tags is CUBE else exchange_pair(value_states, size)
    k_win = exchange_pair(key_states, size)
    if paired:
        opposite = flip(grad_mixed, 2)
        beside = flip(grad_mixed, 1)
        pieces = [grad_mixed, beside, opposite, flip(opposite, 1)]
    else:
        pieces = [grad_mixed] + [ring(grad_mixed, step) for step in range(1, groups)]
    (late_query,) = copies_after((query_states,), tuple(pieces[1:3]))
    q_win = exchange_pair(late_query, size)
    scalars = [
        pltpu.SMEM(key_blocks.shape, i32),
        pltpu.SMEM(host_ids.shape, i32),
        pltpu.SMEM(host_bias.shape, f32),
    ]

    parts_o32_lse = pl.pallas_call(
        functools.partial(attend_kernel, size, groups, v_tags),
        out_shape=[jax.ShapeDtypeStruct((part, width), bf16)] * groups
        + [jax.ShapeDtypeStruct((rows, columns), f32), jax.ShapeDtypeStruct((BLK, BLK), f32)],
        in_specs=[HBM] * 5 + [ANY] * (len(PAIR) + len(v_tags)),
        out_specs=[VMEM] * (groups + 2),
        scratch_shapes=scalars
        + [
            pltpu.VMEM((rows, columns), bf16),
            pltpu.VMEM((columns, width), bf16),
            pltpu.VMEM((places * BLK, columns), bf16),
            pltpu.VMEM((places * BLK, columns), bf16),
            pltpu.VMEM((pairs, BLK, neigh * BLK), f32),
            pltpu.VMEM((rows, columns), bf16),
            pltpu.VMEM((rows, columns), bf16),
            pltpu.SemaphoreType.DMA((5 + 2 * places,)),
        ],
        compiler_params=params(60),
        cost_estimate=cost(4 * 10**9, 8 * 10**6),
        name="attend",
    )(key_blocks, host_ids, host_bias, query_states, out_weight, *k_win, *v_win)
    parts = parts_o32_lse[:groups]
    o32, lse = parts_o32_lse[groups:]
    mixed = parts[0].astype(f32)
    if paired:
        relay = flip(parts[3], 1)
        beside_sum = flip(parts[1], 1)
        passed = (parts[2].astype(f32) + relay.astype(f32)).astype(bf16)
        arrived = [beside_sum, flip(passed, 2)]
    else:
        arrived = [ring(parts[step], step) for step in range(1, groups)]

    up, stats = pl.pallas_call(
        functools.partial(upstream_kernel, groups),
        out_shape=[
            jax.ShapeDtypeStruct((long_rows, columns), bf16),
            jax.ShapeDtypeStruct((BLK, BLK), f32),
        ],
        in_specs=[HBM] * 3 + [VMEM] * 2 + [ANY] * (groups + 3),
        out_specs=[VMEM] * 2,
        scratch_shapes=[
            pltpu.SMEM(key_blocks.shape, i32),
            pltpu.VMEM((columns, width), bf16),
            pltpu.VMEM((rows, width), bf16),
            pltpu.SemaphoreType.DMA((5 + groups,)),
        ],
        compiler_params=params(60),
        cost_estimate=cost(6 * 10**9, 6 * 10**6),
        name="upstream",
    )(key_blocks, out_weight, grad_mixed, o32, lse, *pieces[1:], *q_win[:4])
    up_win = exchange_pair(up, size)

    grad_query = pl.pallas_call(
        functools.partial(query_kernel, size, v_tags),
        out_shape=jax.ShapeDtypeStruct((rows, columns), bf16),
        in_specs=[HBM] * 4 + [VMEM] * 2 + [ANY] * (len(PAIR) + len(v_tags) + 1),
        out_specs=VMEM,
        scratch_shapes=scalars
        + [
            pltpu.VMEM((rows, columns), bf16),
            pltpu.VMEM((places * BLK, columns), bf16),
            pltpu.VMEM((places * BLK, columns), bf16),
            pltpu.SemaphoreType.DMA((4 + 2 * places,)),
        ],
        compiler_params=params(60),
        cost_estimate=cost(10**9, 10**6),
        name="query_grad",
    )(key_blocks, host_ids, host_bias, query_states, up, stats, *k_win, *v_win, q_win[4])

    grad_key, grad_value = pl.pallas_call(
        functools.partial(key_kernel, size, neigh),
        out_shape=[jax.ShapeDtypeStruct((rows, columns), bf16)] * 2,
        in_specs=[HBM] * 5 + [ANY] * (2 * nsh - 1),
        out_specs=[VMEM] * 2,
        scratch_shapes=[
            pltpu.SMEM(host_ids.shape, i32),
            pltpu.SMEM(host_bias.shape, f32),
            pltpu.VMEM((rows, columns), bf16),
            pltpu.VMEM((rows, columns), bf16),
            pltpu.VMEM((nsh * rows, columns), bf16),
            pltpu.VMEM((nsh * long_rows, columns), bf16),
            pltpu.VMEM((nsh + 1, high, BLK), f32),
            pltpu.VMEM((8, BLK), i32),
            pltpu.SMEM((8, BLK), i32),
            pltpu.SMEM((blocks_dev, nsh * blocks_dev + 2), i32),
            pltpu.VMEM((rows, columns), f32),
            pltpu.VMEM((rows, columns), f32),
            pltpu.SemaphoreType.DMA((3 * nsh + 5,)),
        ],
        compiler_params=params(60),
        cost_estimate=cost(10**9, 10**6),
        name="key_grad",
    )(host_ids, host_bias, key_states, value_states, query_states, *q_win[1:], *up_win)

    for piece in arrived:
        mixed = mixed + piece.astype(f32)
    return (mixed.astype(bf16), grad_query, grad_key, grad_value)


def solution(mesh):
    in_specs = (
        P("ctx", "head"),
        P("ctx", "head"),
        P("ctx", "head"),
        P("head", None),
        P(("ctx", "head"), None),
        P("ctx", None),
        P(),
        P("head"),
    )
    out_specs = (P(("ctx", "head"), None), P("ctx", "head"), P("ctx", "head"), P("ctx", "head"))
    return jax.shard_map(
        per_device, mesh=mesh, in_specs=in_specs, out_specs=out_specs, check_vma=False
    )
```

```python
import functools

import jax
import jax.numpy as jnp
from jax import lax
from jax.experimental import pallas as pl
from jax.experimental.pallas import tpu as pltpu
from jax.sharding import PartitionSpec as P

HDIM = 128
BLK = 128
HOPS = 2
SCALE = HDIM ** (-0.5)
CUBE = (0, 1, 2, 3, 6, 7)
PAIR = (0, 1, 2, -2, -1)
NT = (((1,), (1,)), ((), ()))
VMEM = pl.BlockSpec(memory_space=pltpu.VMEM)
SMEM = pl.BlockSpec(memory_space=pltpu.SMEM)
ANY = pl.BlockSpec(memory_space=pl.ANY)
HBM = pl.BlockSpec(memory_space=pltpu.HBM)
NEVER = 1e30


def params(mebibytes):
    return pltpu.CompilerParams(vmem_limit_bytes=mebibytes * 1024 * 1024)


def ndot(a, b):
    return lax.dot_general(a, b, (((1,), (0,)), ((), ())), preferred_element_type=jnp.float32)


def tdot(a, b):
    return lax.dot_general(a, b, NT, preferred_element_type=jnp.float32)


def stat_rows(pairs):
    return -(-2 * pairs // 16) * 16


def tag_owner(position, tag, size, tags):
    if tags is CUBE:
        return position ^ tag
    return lax.rem(position + jnp.where(position % 2 == 0, tag, -tag) + size, size)


def find_shard(position, owner, size, tags):
    shard = 0
    for index, tag in enumerate(tags):
        shard = shard + jnp.where(tag_owner(position, tag, size, tags) == owner, index, 0)
    return shard


def permute_from(x, size, source):
    return lax.ppermute(x, "ctx", [(source(i) % size, i) for i in range(size)])


def exchange_pair(x, size):
    sign = lambda i: 1 if i % 2 == 0 else -1
    share = permute_from(x, size, lambda i: i + 2 * sign(i))
    solo = permute_from(x, size, lambda i: i - 2 * sign(i))
    mate = permute_from(x, size, lambda i: i ^ 1)
    return [x, mate, share, solo, permute_from(share, size, lambda i: i ^ 1)]


def exchange_cube(x, size):
    near = permute_from(x, size, lambda i: i ^ 2)
    far = permute_from(near, size, lambda i: i ^ 4)
    mate = permute_from(x, size, lambda i: i ^ 1)
    swap = lambda i: i ^ 1
    return [x, mate, near, permute_from(near, size, swap), far, permute_from(far, size, swap)]


def start_all(pairs, sem, first=0):
    copies = []
    for index, (source, target) in enumerate(pairs):
        copy = pltpu.make_async_copy(source, target, sem.at[first + index])
        copy.start()
        copies.append(copy)
    return copies


def wait_all(copies):
    for copy in copies:
        copy.wait()


def gather_blocks(size, tags, keys, refs, target, sem, first, blocks_dev, neigh):
    position = lax.axis_index("ctx")
    waits = []
    for b in range(blocks_dev):
        for n in range(neigh):
            j = keys[b, n]
            shard = find_shard(position, lax.div(j, blocks_dev), size, tags)
            row = pl.multiple_of(lax.rem(j, blocks_dev) * BLK, BLK)
            place = b * neigh + n
            for index, ref in enumerate(refs):

                @pl.when(shard == index)
                def _(ref=ref, place=place, row=row):
                    pltpu.make_async_copy(
                        ref.at[pl.ds(row, BLK)], target.at[pl.ds(place * BLK, BLK)], sem.at[first + place]
                    ).start()

            waits.append(
                pltpu.make_async_copy(
                    refs[0].at[pl.ds(0, BLK)], target.at[pl.ds(place * BLK, BLK)], sem.at[first + place]
                )
            )
    return waits


def shift_rows(keys, hosts, bias, b, h, blocks_dev, neigh):
    position = lax.axis_index("ctx")
    slot = lax.broadcasted_iota(jnp.int32, (1, neigh * BLK), 1) // BLK
    shift = jnp.zeros((1, neigh * BLK), jnp.float32)
    host = hosts[position * blocks_dev + b]
    for n in range(neigh):
        value = jnp.where(hosts[keys[b, n]] == host, bias[h], 0.0)
        shift = jnp.where(slot == n, value, shift)
    return shift


def piece_owner(me, step, groups, sign):
    return me ^ step if groups == 4 else lax.rem(me + sign * step + groups, groups)


def attend_kernel(size, groups, tags, *refs):
    count = len(tags)
    keys_hbm, hosts_hbm, bias_hbm, q_hbm, w_hbm, own_hbm = refs[:6]
    k_refs = refs[6:6 + count]
    v_refs = refs[6 + count:6 + 2 * count]
    piece_refs = refs[6 + 2 * count:5 + 2 * count + groups]
    rest = refs[8 + 2 * count + groups:]
    part_refs = rest[:groups]
    up_ref, stats_ref = rest[groups:groups + 2]
    (keys, hosts, bias, q_ref, w_ref, grads, kcat, vcat, score, att, turned, o32_ref, sem) = rest[groups + 2:]
    rows, columns = q_ref.shape
    blocks_dev, neigh = keys.shape
    heads_dev = columns // HDIM
    pairs = blocks_dev * heads_dev
    part = rows // groups
    small = start_all([(keys_hbm, keys), (hosts_hbm, hosts), (bias_hbm, bias)], sem)
    places = blocks_dev * neigh
    large = start_all(
        [(q_hbm, q_ref), (w_hbm, w_ref)]
        + [
            (ref, grads.at[pl.ds(step * part, part)])
            for step, ref in enumerate((own_hbm,) + tuple(piece_refs))
        ],
        sem,
        3 + 2 * places,
    )
    wait_all(small)
    k_waits = gather_blocks(size, tags, keys, k_refs, kcat, sem, 3, blocks_dev, neigh)
    v_waits = gather_blocks(size, tags, keys, v_refs, vcat, sem, 3 + places, blocks_dev, neigh)
    large[0].wait()
    wait_all(k_waits)
    span = neigh * BLK
    units = [(b, h) for b in range(blocks_dev) for h in range(heads_dev)]
    for b, h in units:
        cols = slice(h * HDIM, (h + 1) * HDIM)
        s = tdot(q_ref[b * BLK:(b + 1) * BLK, cols], kcat[b * span:(b + 1) * span, cols])
        score[b * heads_dev + h] = s * SCALE + shift_rows(keys, hosts, bias, b, h, blocks_dev, neigh)
    wait_all(v_waits)
    lane = lax.broadcasted_iota(jnp.int32, (BLK, BLK), 1)
    lse_all = jnp.zeros((BLK, BLK), jnp.float32)
    for b, h in units:
        cols = slice(h * HDIM, (h + 1) * HDIM)
        s = score[b * heads_dev + h]
        top = jnp.max(s, axis=1, keepdims=True)
        weights = jnp.exp(s - top)
        total = jnp.sum(weights, axis=1, keepdims=True)
        probs = (weights * (1.0 / total)).astype(jnp.bfloat16)
        out = ndot(probs, vcat[b * span:(b + 1) * span, cols])
        o32_ref[b * BLK:(b + 1) * BLK, cols] = out
        att[b * BLK:(b + 1) * BLK, cols] = out.astype(jnp.bfloat16)
        lse_all = jnp.where(lane == b * heads_dev + h, top + jnp.log(total), lse_all)
    me = lax.axis_index("head")
    for step in range(groups):
        owner = piece_owner(me, step, groups, 1)
        turned[step * part:(step + 1) * part, :] = att[pl.ds(pl.multiple_of(owner * part, part), part), :]
    wait_all(large[1:])
    mixed = ndot(turned[...], w_ref[...]).astype(jnp.bfloat16)
    for step in range(groups):
        part_refs[step][...] = mixed[step * part:(step + 1) * part, :]
    product = tdot(grads[...], w_ref[...]).astype(jnp.bfloat16)
    for step in range(groups):
        owner = piece_owner(me, step, groups, -1)
        up_ref[pl.ds(pl.multiple_of(owner * part, part), part), :] = product[
            step * part:(step + 1) * part, :
        ]
    stats = lse_all
    for b, h in units:
        cols = slice(h * HDIM, (h + 1) * HDIM)
        up = up_ref[b * BLK:(b + 1) * BLK, cols].astype(jnp.float32)
        term = jnp.sum(up * o32_ref[b * BLK:(b + 1) * BLK, cols], axis=1, keepdims=True)
        stats = jnp.where(lane == pairs + b * heads_dev + h, term, stats)
    stats_ref[...] = stats
    high = stat_rows(pairs)
    turned = jnp.transpose(stats)[:high, :]
    up_ref[rows:, :] = jnp.zeros((up_ref.shape[0] - rows, columns), jnp.bfloat16)
    pieces = []
    for index in range(3):
        piece = turned.astype(jnp.bfloat16)
        turned = turned - piece.astype(jnp.float32)
        pieces.append(piece)
    spot = lax.broadcasted_iota(jnp.int32, (high, BLK), 1)
    line = lax.broadcasted_iota(jnp.int32, (high, BLK), 0)
    listed = jnp.zeros((high, BLK), jnp.int32)
    for b in range(blocks_dev):
        for n in range(neigh):
            listed = jnp.where(spot == b * neigh + n, keys[b, n], listed)
    listed = jnp.where(line == 0, listed >> 7, listed & 127)
    pieces.append(listed.astype(jnp.float32).astype(jnp.bfloat16))
    for index, piece in enumerate(pieces):
        row = rows + high * (index * BLK // columns)
        col = index * BLK % columns
        up_ref[row:row + high, col:col + BLK] = piece


def query_kernel(size, tags, *refs):
    count = len(tags)
    keys_hbm, hosts_hbm, bias_hbm, q_hbm, up_ref, stats_ref = refs[:6]
    k_refs = refs[6:6 + count]
    v_refs = refs[6 + count:6 + 2 * count]
    dq_ref, keys, hosts, bias, q_ref, kcat, vcat, sem = refs[7 + 2 * count:]
    rows, columns = q_ref.shape
    blocks_dev, neigh = keys.shape
    heads_dev = columns // HDIM
    pairs = blocks_dev * heads_dev
    small = start_all([(keys_hbm, keys), (hosts_hbm, hosts), (bias_hbm, bias)], sem)
    large = start_all([(q_hbm, q_ref)], sem, 3)
    wait_all(small)
    places = blocks_dev * neigh
    waits = gather_blocks(size, tags, keys, k_refs, kcat, sem, 4, blocks_dev, neigh)
    waits += gather_blocks(size, tags, keys, v_refs, vcat, sem, 4 + places, blocks_dev, neigh)
    wait_all(large)
    wait_all(waits)
    span = neigh * BLK
    for b in range(blocks_dev):
        for h in range(heads_dev):
            cols = slice(h * HDIM, (h + 1) * HDIM)
            pair = b * heads_dev + h
            q = q_ref[b * BLK:(b + 1) * BLK, cols]
            up = up_ref[b * BLK:(b + 1) * BLK, cols]
            k = kcat[b * span:(b + 1) * span, cols]
            lse = stats_ref[:, pair:pair + 1]
            term = stats_ref[:, pairs + pair:pairs + pair + 1]
            shift = shift_rows(keys, hosts, bias, b, h, blocks_dev, neigh)
            p = jnp.exp(tdot(q, k) * SCALE + shift - lse)
            dp = tdot(up, vcat[b * span:(b + 1) * span, cols])
            ds = (p * (dp - term) * SCALE).astype(jnp.bfloat16)
            dq_ref[b * BLK:(b + 1) * BLK, cols] = ndot(ds, k).astype(jnp.bfloat16)


def key_kernel(size, neigh, tags, *refs):
    nsh = len(PAIR)
    count = len(tags)
    hosts_hbm, bias_hbm, k_hbm, v_hbm = refs[:4]
    q_refs = refs[4:4 + count]
    up_refs = refs[4 + count:4 + count + nsh]
    dk_ref, dv_ref = refs[4 + count + nsh:6 + count + nsh]
    (hosts, bias, k_ref, v_ref, qwin, upwin, stats, lists, keys, hits, dk_acc, dv_acc, sem) = refs[
        6 + count + nsh:
    ]
    rows, columns = k_ref.shape
    long_rows = up_refs[0].shape[0]
    blocks_dev = rows // BLK
    heads_dev = columns // HDIM
    pairs = blocks_dev * heads_dev
    high = stat_rows(pairs)
    position = lax.axis_index("ctx")
    tail = [
        (ref.at[pl.ds(rows, long_rows - rows)], upwin.at[pl.ds(i * long_rows + rows, long_rows - rows)])
        for i, ref in enumerate(up_refs)
    ]
    first = start_all(tail, sem)
    body = [(ref.at[pl.ds(0, rows)], upwin.at[pl.ds(i * long_rows, rows)]) for i, ref in enumerate(up_refs)]
    body += [(ref, qwin.at[pl.ds(i * rows, rows)]) for i, ref in enumerate(q_refs)]
    body += [(hosts_hbm, hosts), (bias_hbm, bias), (k_hbm, k_ref), (v_hbm, v_ref)]
    later = start_all(body, sem, nsh)
    dk_acc[...] = jnp.zeros_like(dk_acc)
    dv_acc[...] = jnp.zeros_like(dv_acc)
    wait_all(first)

    def part_of(index, piece):
        row = index * long_rows + rows + high * (piece * BLK // columns)
        col = piece * BLK % columns
        return upwin[row:row + high, col:col + BLK].astype(jnp.float32)

    for index in range(nsh):
        stats[index] = (part_of(index, 2) + part_of(index, 1)) + part_of(index, 0)
        listed = part_of(index, 3).astype(jnp.int32)
        lists[index:index + 1, :] = listed[0:1, :] * 128 + listed[1:2, :]
    stats[nsh] = jnp.full((high, BLK), NEVER, jnp.float32)
    copy = pltpu.make_async_copy(lists, keys, sem.at[2 * nsh + count + 4])
    copy.start()
    copy.wait()

    counts = []
    for own in range(blocks_dev):
        mine = position * blocks_dev + own
        count = 0
        for index in range(nsh):
            for inner in range(blocks_dev):
                hit = keys[index, inner * neigh] == mine
                for n in range(1, neigh):
                    hit = hit | (keys[index, inner * neigh + n] == mine)
                hits[own, count] = index * blocks_dev + inner
                count = count + jnp.where(hit, 1, 0)
        hits[own, count] = -1
        counts.append(count)
    wait_all(later)

    for own in range(blocks_dev):
        mine = position * blocks_dev + own
        krow = slice(own * BLK, (own + 1) * BLK)

        def visit(step, carry, own=own, mine=mine, krow=krow):
            qs, ups, sames, lses, terms = [], [], [], [], []
            for turn in range(2):
                entry = hits[own, 2 * step + turn]
                spare = entry < 0
                entry = jnp.where(spare, 0, entry)
                shard = lax.div(entry, blocks_dev)
                inner = lax.rem(entry, blocks_dev)
                owner = 0
                for index, tag in enumerate(PAIR):
                    owner = owner + jnp.where(shard == index, tag_owner(position, tag, size, PAIR), 0)
                sames.append(hosts[owner * blocks_dev + inner] == hosts[mine])
                place = find_shard(position, owner, size, tags)
                qs.append(pl.ds(pl.multiple_of(place * rows + inner * BLK, BLK), BLK))
                ups.append(pl.ds(pl.multiple_of(shard * long_rows + inner * BLK, 16), BLK))
                lses.append((jnp.where(spare, nsh, shard), inner))
                terms.append((shard, inner))
            for h in range(heads_dev):
                cols = slice(h * HDIM, (h + 1) * HDIM)
                k = k_ref[krow, cols]
                v = v_ref[krow, cols]
                q = jnp.concatenate([qwin[r, cols] for r in qs], axis=0)
                up = jnp.concatenate([upwin[r, cols] for r in ups], axis=0)
                less = jnp.concatenate(
                    [
                        stats[shard, pl.ds(inner * heads_dev + h, 1), :] - jnp.where(same, bias[h], 0.0)
                        for (shard, inner), same in zip(lses, sames)
                    ],
                    axis=1,
                )
                term = jnp.concatenate(
                    [stats[shard, pl.ds(pairs + inner * heads_dev + h, 1), :] for shard, inner in terms],
                    axis=1,
                )
                p = jnp.exp(tdot(k, q) * SCALE - less)
                ds = (p * (tdot(v, up) - term) * SCALE).astype(jnp.bfloat16)
                dk_acc[krow, cols] += ndot(ds, q)
                dv_acc[krow, cols] += ndot(p.astype(jnp.bfloat16), up)
            return carry

        lax.fori_loop(0, lax.div(counts[own] + 1, 2), visit, 0)
    dk_ref[...] = dk_acc[...].astype(jnp.bfloat16)
    dv_ref[...] = dv_acc[...].astype(jnp.bfloat16)


def sum_kernel(count, *refs):
    total = refs[0][...].astype(jnp.float32)
    for ref in refs[1:count]:
        total = total + ref[...].astype(jnp.float32)
    refs[-1][...] = total.astype(jnp.bfloat16)


def sum_after(arrays, before):
    return pl.pallas_call(
        functools.partial(sum_kernel, len(arrays)),
        out_shape=jax.ShapeDtypeStruct(arrays[0].shape, jnp.bfloat16),
        in_specs=[VMEM] * len(arrays) + [ANY],
        out_specs=VMEM,
        compiler_params=params(60),
        cost_estimate=cost(1000, 1000),
        name="sum_after",
    )(*arrays, before)


def copy_kernel(count, extra, *refs):
    sources, targets = refs[:count], refs[count + extra:2 * count + extra]
    between, sem = refs[2 * count + extra:-1], refs[-1]
    wait_all(start_all(list(zip(sources, between)), sem))
    wait_all(start_all(list(zip(between, targets)), sem))


def copies_after(arrays, before):
    return pl.pallas_call(
        functools.partial(copy_kernel, len(arrays), len(before)),
        out_shape=[jax.ShapeDtypeStruct(x.shape, x.dtype) for x in arrays],
        in_specs=[ANY] * (len(arrays) + len(before)),
        out_specs=[ANY] * len(arrays),
        scratch_shapes=[pltpu.VMEM(x.shape, x.dtype) for x in arrays]
        + [pltpu.SemaphoreType.DMA((len(arrays),))],
        compiler_params=params(60),
        cost_estimate=cost(1000, 1000),
        name="copies_after",
    )(*arrays, *before)


def cost(flops, nbytes):
    return pl.CostEstimate(flops=flops, bytes_accessed=nbytes, transcendentals=0)


def per_device(
    query_states, key_states, value_states, out_weight, grad_mixed, key_blocks, host_ids, host_bias
):
    size = lax.axis_size("ctx")
    rows, columns = query_states.shape
    width = out_weight.shape[1]
    blocks_dev, neigh = key_blocks.shape
    heads_dev = columns // HDIM
    pairs = blocks_dev * heads_dev
    places = blocks_dev * neigh
    groups = lax.axis_size("head")
    part = rows // groups
    tags = CUBE if size == 8 else PAIR
    exchange = exchange_cube if size == 8 else exchange_pair
    nsh = len(PAIR)
    bf16, f32, i32 = jnp.bfloat16, jnp.float32, jnp.int32
    high = stat_rows(pairs)
    extra = high * (-(-4 * BLK // columns))
    long_rows = rows + extra

    def ring(x, step):
        return lax.ppermute(x, "head", [(i, (i + step) % groups) for i in range(groups)])

    def flip(x, mask):
        return lax.ppermute(x, "head", [(i, i ^ mask) for i in range(groups)])

    paired = groups == 4
    v_win = exchange(value_states, size)
    k_win = exchange(key_states, size)
    if paired:
        opposite = flip(grad_mixed, 2)
        beside = flip(grad_mixed, 1)
        pieces = [grad_mixed, beside, opposite, flip(opposite, 1)]
    else:
        pieces = [grad_mixed] + [ring(grad_mixed, step) for step in range(1, groups)]
    (late_query,) = copies_after((query_states,), (pieces[2],))
    q_win = exchange(late_query, size)
    scalars = [
        pltpu.SMEM(key_blocks.shape, i32),
        pltpu.SMEM(host_ids.shape, i32),
        pltpu.SMEM(host_bias.shape, f32),
    ]

    outputs = pl.pallas_call(
        functools.partial(attend_kernel, size, groups, tags),
        out_shape=[jax.ShapeDtypeStruct((part, width), bf16)] * groups
        + [
            jax.ShapeDtypeStruct((long_rows, columns), bf16),
            jax.ShapeDtypeStruct((BLK, BLK), f32),
        ],
        in_specs=[HBM] * 6 + [ANY] * (2 * len(tags) + groups - 1 + 3),
        out_specs=[VMEM] * (groups + 2),
        scratch_shapes=scalars
        + [
            pltpu.VMEM((rows, columns), bf16),
            pltpu.VMEM((columns, width), bf16),
            pltpu.VMEM((rows, width), bf16),
            pltpu.VMEM((places * BLK, columns), bf16),
            pltpu.VMEM((places * BLK, columns), bf16),
            pltpu.VMEM((pairs, BLK, neigh * BLK), f32),
            pltpu.VMEM((rows, columns), bf16),
            pltpu.VMEM((rows, columns), bf16),
            pltpu.VMEM((rows, columns), f32),
            pltpu.SemaphoreType.DMA((5 + groups + 2 * places,)),
        ],
        compiler_params=params(60),
        cost_estimate=cost(4 * 10**9, 8 * 10**6),
        name="attend",
    )(key_blocks, host_ids, host_bias, query_states, out_weight, grad_mixed, *k_win, *v_win, *pieces[1:], q_win[1], q_win[2], q_win[3])
    parts = outputs[:groups]
    up, stats = outputs[groups:]
    if paired:
        relay = flip(parts[3], 1)
        beside_sum = flip(parts[1], 1)
        passed = (parts[2].astype(f32) + relay.astype(f32)).astype(bf16)
        arrived = [beside_sum, flip(passed, 2)]
    else:
        arrived = [ring(parts[step], step) for step in range(1, groups)]

    up_win = exchange_pair(up, size)

    grad_query = pl.pallas_call(
        functools.partial(query_kernel, size, tags),
        out_shape=jax.ShapeDtypeStruct((rows, columns), bf16),
        in_specs=[HBM] * 4 + [VMEM] * 2 + [ANY] * (2 * len(tags) + 1),
        out_specs=VMEM,
        scratch_shapes=scalars
        + [
            pltpu.VMEM((rows, columns), bf16),
            pltpu.VMEM((places * BLK, columns), bf16),
            pltpu.VMEM((places * BLK, columns), bf16),
            pltpu.SemaphoreType.DMA((4 + 2 * places,)),
        ],
        compiler_params=params(60),
        cost_estimate=cost(10**9, 10**6),
        name="query_grad",
    )(key_blocks, host_ids, host_bias, query_states, up, stats, *k_win, *v_win, q_win[4])

    grad_key, grad_value = pl.pallas_call(
        functools.partial(key_kernel, size, neigh, tags),
        out_shape=[jax.ShapeDtypeStruct((rows, columns), bf16)] * 2,
        in_specs=[HBM] * 5 + [ANY] * (len(tags) + nsh - 1),
        out_specs=[VMEM] * 2,
        scratch_shapes=[
            pltpu.SMEM(host_ids.shape, i32),
            pltpu.SMEM(host_bias.shape, f32),
            pltpu.VMEM((rows, columns), bf16),
            pltpu.VMEM((rows, columns), bf16),
            pltpu.VMEM((len(tags) * rows, columns), bf16),
            pltpu.VMEM((nsh * long_rows, columns), bf16),
            pltpu.VMEM((nsh + 1, high, BLK), f32),
            pltpu.VMEM((8, BLK), i32),
            pltpu.SMEM((8, BLK), i32),
            pltpu.SMEM((blocks_dev, nsh * blocks_dev + 2), i32),
            pltpu.VMEM((rows, columns), f32),
            pltpu.VMEM((rows, columns), f32),
            pltpu.SemaphoreType.DMA((2 * nsh + len(tags) + 5,)),
        ],
        compiler_params=params(60),
        cost_estimate=cost(10**9, 10**6),
        name="key_grad",
    )(host_ids, host_bias, key_states, value_states, query_states, *q_win[1:], *up_win)

    mixed_out = sum_after((parts[0], *arrived), grad_key)
    return (mixed_out, grad_query, grad_key, grad_value)


def solution(mesh):
    in_specs = (
        P("ctx", "head"),
        P("ctx", "head"),
        P("ctx", "head"),
        P("head", None),
        P(("ctx", "head"), None),
        P("ctx", None),
        P(),
        P("head"),
    )
    out_specs = (P(("ctx", "head"), None), P("ctx", "head"), P("ctx", "head"), P("ctx", "head"))
    return jax.shard_map(
        per_device, mesh=mesh, in_specs=in_specs, out_specs=out_specs, check_vma=False
    )
```

```python
import functools

import jax
import jax.numpy as jnp
from jax import lax
from jax.experimental import pallas as pl
from jax.experimental.pallas import tpu as pltpu
from jax.sharding import PartitionSpec as P

HDIM = 128
BLK = 128
HOPS = 2
SCALE = HDIM ** (-0.5)
CUBE = (0, 1, 2, 3, 6, 7)
PAIR = (0, 1, 2, -2, -1)
NT = (((1,), (1,)), ((), ()))
VMEM = pl.BlockSpec(memory_space=pltpu.VMEM)
SMEM = pl.BlockSpec(memory_space=pltpu.SMEM)
ANY = pl.BlockSpec(memory_space=pl.ANY)
HBM = pl.BlockSpec(memory_space=pltpu.HBM)
NEVER = 1e30


def params(mebibytes):
    return pltpu.CompilerParams(vmem_limit_bytes=mebibytes * 1024 * 1024)


def ndot(a, b):
    return lax.dot_general(a, b, (((1,), (0,)), ((), ())), preferred_element_type=jnp.float32)


def tdot(a, b):
    return lax.dot_general(a, b, NT, preferred_element_type=jnp.float32)


def stat_rows(pairs):
    return -(-2 * pairs // 16) * 16


def tag_owner(position, tag, size, tags):
    if tags is CUBE:
        return position ^ tag
    return lax.rem(position + jnp.where(position % 2 == 0, tag, -tag) + size, size)


def find_shard(position, owner, size, tags):
    shard = 0
    for index, tag in enumerate(tags):
        shard = shard + jnp.where(tag_owner(position, tag, size, tags) == owner, index, 0)
    return shard


def permute_from(x, size, source):
    return lax.ppermute(x, "ctx", [(source(i) % size, i) for i in range(size)])


def exchange_pair(x, size):
    sign = lambda i: 1 if i % 2 == 0 else -1
    share = permute_from(x, size, lambda i: i + 2 * sign(i))
    solo = permute_from(x, size, lambda i: i - 2 * sign(i))
    mate = permute_from(x, size, lambda i: i ^ 1)
    return [x, mate, share, solo, permute_from(share, size, lambda i: i ^ 1)]


def exchange_cube(x, size):
    near = permute_from(x, size, lambda i: i ^ 2)
    far = permute_from(near, size, lambda i: i ^ 4)
    mate = permute_from(x, size, lambda i: i ^ 1)
    swap = lambda i: i ^ 1
    return [x, mate, near, permute_from(near, size, swap), far, permute_from(far, size, swap)]


def start_all(pairs, sem, first=0):
    copies = []
    for index, (source, target) in enumerate(pairs):
        copy = pltpu.make_async_copy(source, target, sem.at[first + index])
        copy.start()
        copies.append(copy)
    return copies


def wait_all(copies):
    for copy in copies:
        copy.wait()


def gather_blocks(size, tags, keys, refs, target, sem, first, blocks_dev, neigh):
    position = lax.axis_index("ctx")
    waits = []
    for b in range(blocks_dev):
        for n in range(neigh):
            j = keys[b, n]
            shard = find_shard(position, lax.div(j, blocks_dev), size, tags)
            row = pl.multiple_of(lax.rem(j, blocks_dev) * BLK, BLK)
            place = b * neigh + n
            for index, ref in enumerate(refs):

                @pl.when(shard == index)
                def _(ref=ref, place=place, row=row):
                    pltpu.make_async_copy(
                        ref.at[pl.ds(row, BLK)], target.at[pl.ds(place * BLK, BLK)], sem.at[first + place]
                    ).start()

            waits.append(
                pltpu.make_async_copy(
                    refs[0].at[pl.ds(0, BLK)], target.at[pl.ds(place * BLK, BLK)], sem.at[first + place]
                )
            )
    return waits


def shift_rows(keys, hosts, bias, b, h, blocks_dev, neigh):
    position = lax.axis_index("ctx")
    slot = lax.broadcasted_iota(jnp.int32, (1, neigh * BLK), 1) // BLK
    shift = jnp.zeros((1, neigh * BLK), jnp.float32)
    host = hosts[position * blocks_dev + b]
    for n in range(neigh):
        value = jnp.where(hosts[keys[b, n]] == host, bias[h], 0.0)
        shift = jnp.where(slot == n, value, shift)
    return shift


def piece_owner(me, step, groups, sign):
    return me ^ step if groups == 4 else lax.rem(me + sign * step + groups, groups)


def attend_kernel(size, groups, v_tags, *refs):
    keys_hbm, hosts_hbm, bias_hbm, q_hbm, w_hbm = refs[:5]
    k_refs = refs[5:5 + len(PAIR)]
    v_refs = refs[5 + len(PAIR):5 + len(PAIR) + len(v_tags)]
    rest = refs[5 + len(PAIR) + len(v_tags):]
    part_refs = rest[:groups]
    o32_ref, lse_ref = rest[groups:groups + 2]
    keys, hosts, bias, q_ref, w_ref, kcat, vcat, score, att, turned, sem = rest[groups + 2:]
    rows, columns = q_ref.shape
    blocks_dev, neigh = keys.shape
    heads_dev = columns // HDIM
    small = start_all([(keys_hbm, keys), (hosts_hbm, hosts), (bias_hbm, bias)], sem)
    large = start_all([(q_hbm, q_ref), (w_hbm, w_ref)], sem, 3)
    wait_all(small)
    places = blocks_dev * neigh
    k_waits = gather_blocks(size, PAIR, keys, k_refs, kcat, sem, 5, blocks_dev, neigh)
    v_waits = gather_blocks(size, v_tags, keys, v_refs, vcat, sem, 5 + places, blocks_dev, neigh)
    large[0].wait()
    wait_all(k_waits)
    span = neigh * BLK
    units = [(b, h) for b in range(blocks_dev) for h in range(heads_dev)]
    for b, h in units:
        cols = slice(h * HDIM, (h + 1) * HDIM)
        s = tdot(q_ref[b * BLK:(b + 1) * BLK, cols], kcat[b * span:(b + 1) * span, cols])
        score[b * heads_dev + h] = s * SCALE + shift_rows(keys, hosts, bias, b, h, blocks_dev, neigh)
    wait_all(v_waits)
    lane = lax.broadcasted_iota(jnp.int32, (BLK, BLK), 1)
    lse_all = jnp.zeros((BLK, BLK), jnp.float32)
    for b, h in units:
        cols = slice(h * HDIM, (h + 1) * HDIM)
        s = score[b * heads_dev + h]
        top = jnp.max(s, axis=1, keepdims=True)
        weights = jnp.exp(s - top)
        total = jnp.sum(weights, axis=1, keepdims=True)
        probs = (weights * (1.0 / total)).astype(jnp.bfloat16)
        out = ndot(probs, vcat[b * span:(b + 1) * span, cols])
        o32_ref[b * BLK:(b + 1) * BLK, cols] = out
        att[b * BLK:(b + 1) * BLK, cols] = out.astype(jnp.bfloat16)
        lse_all = jnp.where(lane == b * heads_dev + h, top + jnp.log(total), lse_all)
    lse_ref[...] = lse_all
    large[1].wait()
    me = lax.axis_index("head")
    part = rows // groups
    for step in range(groups):
        owner = piece_owner(me, step, groups, 1)
        turned[step * part:(step + 1) * part, :] = att[pl.ds(pl.multiple_of(owner * part, part), part), :]
    mixed = ndot(turned[...], w_ref[...]).astype(jnp.bfloat16)
    for step in range(groups):
        part_refs[step][...] = mixed[step * part:(step + 1) * part, :]


def upstream_kernel(groups, *refs):
    keys_hbm, w_hbm, own_hbm, o32_ref, lse_ref = refs[:5]
    piece_refs = refs[5:4 + groups]
    rest = refs[4 + groups + 1:]
    up_ref, stats_ref, keys, w_ref, grads, sem = rest
    rows, columns = o32_ref.shape
    width = w_ref.shape[1]
    blocks_dev, neigh = keys.shape
    heads_dev = columns // HDIM
    part = rows // groups
    cut = width // 4
    w_waits = [
        start_all([(w_hbm.at[:, c * cut:(c + 1) * cut], w_ref.at[:, c * cut:(c + 1) * cut])], sem, c)[0]
        for c in range(4)
    ]
    pieces = (own_hbm,) + tuple(piece_refs)
    wait_all(
        start_all(
            [(ref, grads.at[pl.ds(step * part, part)]) for step, ref in enumerate(pieces)]
            + [(keys_hbm, keys)],
            sem,
            4,
        )
    )
    total = jnp.zeros((rows, columns), jnp.float32)
    for c in range(4):
        w_waits[c].wait()
        total = total + tdot(grads[:, c * cut:(c + 1) * cut], w_ref[:, c * cut:(c + 1) * cut])
    me = lax.axis_index("head")
    product = total.astype(jnp.bfloat16)
    for step in range(groups):
        owner = piece_owner(me, step, groups, -1)
        up_ref[pl.ds(pl.multiple_of(owner * part, part), part), :] = product[
            step * part:(step + 1) * part, :
        ]
    pairs = blocks_dev * heads_dev
    lane = lax.broadcasted_iota(jnp.int32, (BLK, BLK), 1)
    stats = lse_ref[...]
    for b in range(blocks_dev):
        for h in range(heads_dev):
            cols = slice(h * HDIM, (h + 1) * HDIM)
            up = up_ref[b * BLK:(b + 1) * BLK, cols].astype(jnp.float32)
            term = jnp.sum(up * o32_ref[b * BLK:(b + 1) * BLK, cols], axis=1, keepdims=True)
            stats = jnp.where(lane == pairs + b * heads_dev + h, term, stats)
    stats_ref[...] = stats
    high = stat_rows(pairs)
    turned = jnp.transpose(stats)[:high, :]
    up_ref[rows:, :] = jnp.zeros((up_ref.shape[0] - rows, columns), jnp.bfloat16)
    pieces = []
    for index in range(3):
        piece = turned.astype(jnp.bfloat16)
        turned = turned - piece.astype(jnp.float32)
        pieces.append(piece)
    spot = lax.broadcasted_iota(jnp.int32, (high, BLK), 1)
    line = lax.broadcasted_iota(jnp.int32, (high, BLK), 0)
    listed = jnp.zeros((high, BLK), jnp.int32)
    for b in range(blocks_dev):
        for n in range(neigh):
            listed = jnp.where(spot == b * neigh + n, keys[b, n], listed)
    listed = jnp.where(line == 0, listed >> 7, listed & 127)
    pieces.append(listed.astype(jnp.float32).astype(jnp.bfloat16))
    for index, piece in enumerate(pieces):
        row = rows + high * (index * BLK // columns)
        col = index * BLK % columns
        up_ref[row:row + high, col:col + BLK] = piece


def query_kernel(size, v_tags, *refs):
    keys_hbm, hosts_hbm, bias_hbm, q_hbm, up_ref, stats_ref = refs[:6]
    k_refs = refs[6:6 + len(PAIR)]
    v_refs = refs[6 + len(PAIR):6 + len(PAIR) + len(v_tags)]
    dq_ref, keys, hosts, bias, q_ref, kcat, vcat, sem = refs[6 + len(PAIR) + len(v_tags) + 1:]
    rows, columns = q_ref.shape
    blocks_dev, neigh = keys.shape
    heads_dev = columns // HDIM
    pairs = blocks_dev * heads_dev
    small = start_all([(keys_hbm, keys), (hosts_hbm, hosts), (bias_hbm, bias)], sem)
    large = start_all([(q_hbm, q_ref)], sem, 3)
    wait_all(small)
    places = blocks_dev * neigh
    waits = gather_blocks(size, PAIR, keys, k_refs, kcat, sem, 4, blocks_dev, neigh)
    waits += gather_blocks(size, v_tags, keys, v_refs, vcat, sem, 4 + places, blocks_dev, neigh)
    wait_all(large)
    wait_all(waits)
    span = neigh * BLK
    for b in range(blocks_dev):
        for h in range(heads_dev):
            cols = slice(h * HDIM, (h + 1) * HDIM)
            pair = b * heads_dev + h
            q = q_ref[b * BLK:(b + 1) * BLK, cols]
            up = up_ref[b * BLK:(b + 1) * BLK, cols]
            k = kcat[b * span:(b + 1) * span, cols]
            lse = stats_ref[:, pair:pair + 1]
            term = stats_ref[:, pairs + pair:pairs + pair + 1]
            shift = shift_rows(keys, hosts, bias, b, h, blocks_dev, neigh)
            p = jnp.exp(tdot(q, k) * SCALE + shift - lse)
            dp = tdot(up, vcat[b * span:(b + 1) * span, cols])
            ds = (p * (dp - term) * SCALE).astype(jnp.bfloat16)
            dq_ref[b * BLK:(b + 1) * BLK, cols] = ndot(ds, k).astype(jnp.bfloat16)


def key_kernel(size, neigh, *refs):
    nsh = len(PAIR)
    hosts_hbm, bias_hbm, k_hbm, v_hbm = refs[:4]
    q_refs = refs[4:4 + nsh]
    up_refs = refs[4 + nsh:4 + 2 * nsh]
    dk_ref, dv_ref = refs[4 + 2 * nsh:6 + 2 * nsh]
    (hosts, bias, k_ref, v_ref, qwin, upwin, stats, lists, keys, hits, dk_acc, dv_acc, sem) = refs[
        6 + 2 * nsh:
    ]
    rows, columns = k_ref.shape
    long_rows = up_refs[0].shape[0]
    blocks_dev = rows // BLK
    heads_dev = columns // HDIM
    pairs = blocks_dev * heads_dev
    high = stat_rows(pairs)
    position = lax.axis_index("ctx")
    tail = [
        (ref.at[pl.ds(rows, long_rows - rows)], upwin.at[pl.ds(i * long_rows + rows, long_rows - rows)])
        for i, ref in enumerate(up_refs)
    ]
    first = start_all(tail, sem)
    body = [(ref.at[pl.ds(0, rows)], upwin.at[pl.ds(i * long_rows, rows)]) for i, ref in enumerate(up_refs)]
    body += [(ref, qwin.at[pl.ds(i * rows, rows)]) for i, ref in enumerate(q_refs)]
    body += [(hosts_hbm, hosts), (bias_hbm, bias), (k_hbm, k_ref), (v_hbm, v_ref)]
    later = start_all(body, sem, nsh)
    dk_acc[...] = jnp.zeros_like(dk_acc)
    dv_acc[...] = jnp.zeros_like(dv_acc)
    wait_all(first)

    def part_of(index, piece):
        row = index * long_rows + rows + high * (piece * BLK // columns)
        col = piece * BLK % columns
        return upwin[row:row + high, col:col + BLK].astype(jnp.float32)

    for index in range(nsh):
        stats[index] = (part_of(index, 2) + part_of(index, 1)) + part_of(index, 0)
        listed = part_of(index, 3).astype(jnp.int32)
        lists[index:index + 1, :] = listed[0:1, :] * 128 + listed[1:2, :]
    stats[nsh] = jnp.full((high, BLK), NEVER, jnp.float32)
    copy = pltpu.make_async_copy(lists, keys, sem.at[3 * nsh + 4])
    copy.start()
    copy.wait()

    counts = []
    for own in range(blocks_dev):
        mine = position * blocks_dev + own
        count = 0
        for index in range(nsh):
            for inner in range(blocks_dev):
                hit = keys[index, inner * neigh] == mine
                for n in range(1, neigh):
                    hit = hit | (keys[index, inner * neigh + n] == mine)
                hits[own, count] = index * blocks_dev + inner
                count = count + jnp.where(hit, 1, 0)
        hits[own, count] = -1
        counts.append(count)
    wait_all(later)

    for own in range(blocks_dev):
        mine = position * blocks_dev + own
        krow = slice(own * BLK, (own + 1) * BLK)

        def visit(step, carry, own=own, mine=mine, krow=krow):
            qs, ups, sames, lses, terms = [], [], [], [], []
            for turn in range(2):
                entry = hits[own, 2 * step + turn]
                spare = entry < 0
                entry = jnp.where(spare, 0, entry)
                shard = lax.div(entry, blocks_dev)
                inner = lax.rem(entry, blocks_dev)
                owner = 0
                for index, tag in enumerate(PAIR):
                    owner = owner + jnp.where(shard == index, tag_owner(position, tag, size, PAIR), 0)
                sames.append(hosts[owner * blocks_dev + inner] == hosts[mine])
                qs.append(pl.ds(pl.multiple_of(shard * rows + inner * BLK, BLK), BLK))
                ups.append(pl.ds(pl.multiple_of(shard * long_rows + inner * BLK, 16), BLK))
                lses.append((jnp.where(spare, nsh, shard), inner))
                terms.append((shard, inner))
            for h in range(heads_dev):
                cols = slice(h * HDIM, (h + 1) * HDIM)
                k = k_ref[krow, cols]
                v = v_ref[krow, cols]
                q = jnp.concatenate([qwin[r, cols] for r in qs], axis=0)
                up = jnp.concatenate([upwin[r, cols] for r in ups], axis=0)
                less = jnp.concatenate(
                    [
                        stats[shard, pl.ds(inner * heads_dev + h, 1), :] - jnp.where(same, bias[h], 0.0)
                        for (shard, inner), same in zip(lses, sames)
                    ],
                    axis=1,
                )
                term = jnp.concatenate(
                    [stats[shard, pl.ds(pairs + inner * heads_dev + h, 1), :] for shard, inner in terms],
                    axis=1,
                )
                p = jnp.exp(tdot(k, q) * SCALE - less)
                ds = (p * (tdot(v, up) - term) * SCALE).astype(jnp.bfloat16)
                dk_acc[krow, cols] += ndot(ds, q)
                dv_acc[krow, cols] += ndot(p.astype(jnp.bfloat16), up)
            return carry

        lax.fori_loop(0, lax.div(counts[own] + 1, 2), visit, 0)
    dk_ref[...] = dk_acc[...].astype(jnp.bfloat16)
    dv_ref[...] = dv_acc[...].astype(jnp.bfloat16)


def sum_kernel(count, *refs):
    total = refs[0][...].astype(jnp.float32)
    for ref in refs[1:count]:
        total = total + ref[...].astype(jnp.float32)
    refs[-1][...] = total.astype(jnp.bfloat16)


def sum_after(arrays, before):
    return pl.pallas_call(
        functools.partial(sum_kernel, len(arrays)),
        out_shape=jax.ShapeDtypeStruct(arrays[0].shape, jnp.bfloat16),
        in_specs=[VMEM] * len(arrays) + [ANY],
        out_specs=VMEM,
        compiler_params=params(60),
        cost_estimate=cost(1000, 1000),
        name="sum_after",
    )(*arrays, before)


def copy_kernel(count, extra, *refs):
    sources, targets = refs[:count], refs[count + extra:2 * count + extra]
    between, sem = refs[2 * count + extra:-1], refs[-1]
    wait_all(start_all(list(zip(sources, between)), sem))
    wait_all(start_all(list(zip(between, targets)), sem))


def copies_after(arrays, before):
    return pl.pallas_call(
        functools.partial(copy_kernel, len(arrays), len(before)),
        out_shape=[jax.ShapeDtypeStruct(x.shape, x.dtype) for x in arrays],
        in_specs=[ANY] * (len(arrays) + len(before)),
        out_specs=[ANY] * len(arrays),
        scratch_shapes=[pltpu.VMEM(x.shape, x.dtype) for x in arrays]
        + [pltpu.SemaphoreType.DMA((len(arrays),))],
        compiler_params=params(60),
        cost_estimate=cost(1000, 1000),
        name="copies_after",
    )(*arrays, *before)


def cost(flops, nbytes):
    return pl.CostEstimate(flops=flops, bytes_accessed=nbytes, transcendentals=0)


def per_device(
    query_states, key_states, value_states, out_weight, grad_mixed, key_blocks, host_ids, host_bias
):
    size = lax.axis_size("ctx")
    rows, columns = query_states.shape
    width = out_weight.shape[1]
    blocks_dev, neigh = key_blocks.shape
    heads_dev = columns // HDIM
    pairs = blocks_dev * heads_dev
    places = blocks_dev * neigh
    groups = lax.axis_size("head")
    part = rows // groups
    v_tags = CUBE if size == 8 else PAIR
    nsh = len(PAIR)
    bf16, f32, i32 = jnp.bfloat16, jnp.float32, jnp.int32
    high = stat_rows(pairs)
    extra = high * (-(-4 * BLK // columns))
    long_rows = rows + extra

    def ring(x, step):
        return lax.ppermute(x, "head", [(i, (i + step) % groups) for i in range(groups)])

    def flip(x, mask):
        return lax.ppermute(x, "head", [(i, i ^ mask) for i in range(groups)])

    paired = groups == 4
    v_win = exchange_cube(value_states, size) if v_tags is CUBE else exchange_pair(value_states, size)
    k_win = exchange_pair(key_states, size)
    if paired:
        opposite = flip(grad_mixed, 2)
        beside = flip(grad_mixed, 1)
        pieces = [grad_mixed, beside, opposite, flip(opposite, 1)]
    else:
        pieces = [grad_mixed] + [ring(grad_mixed, step) for step in range(1, groups)]
    (late_query,) = copies_after((query_states,), (pieces[1], pieces[2]))
    q_win = exchange_pair(late_query, size)
    scalars = [
        pltpu.SMEM(key_blocks.shape, i32),
        pltpu.SMEM(host_ids.shape, i32),
        pltpu.SMEM(host_bias.shape, f32),
    ]

    parts_o32_lse = pl.pallas_call(
        functools.partial(attend_kernel, size, groups, v_tags),
        out_shape=[jax.ShapeDtypeStruct((part, width), bf16)] * groups
        + [jax.ShapeDtypeStruct((rows, columns), f32), jax.ShapeDtypeStruct((BLK, BLK), f32)],
        in_specs=[HBM] * 5 + [ANY] * (len(PAIR) + len(v_tags)),
        out_specs=[VMEM] * (groups + 2),
        scratch_shapes=scalars
        + [
            pltpu.VMEM((rows, columns), bf16),
            pltpu.VMEM((columns, width), bf16),
            pltpu.VMEM((places * BLK, columns), bf16),
            pltpu.VMEM((places * BLK, columns), bf16),
            pltpu.VMEM((pairs, BLK, neigh * BLK), f32),
            pltpu.VMEM((rows, columns), bf16),
            pltpu.VMEM((rows, columns), bf16),
            pltpu.SemaphoreType.DMA((5 + 2 * places,)),
        ],
        compiler_params=params(60),
        cost_estimate=cost(10**9, 10**6),
        name="attend",
    )(key_blocks, host_ids, host_bias, query_states, out_weight, *k_win, *v_win)
    parts = parts_o32_lse[:groups]
    o32, lse = parts_o32_lse[groups:]
    mixed = parts[0].astype(f32)
    if paired:
        relay = flip(parts[3], 1)
        beside_sum = flip(parts[1], 1)
        passed = (parts[2].astype(f32) + relay.astype(f32)).astype(bf16)
        arrived = [beside_sum, flip(passed, 2)]
    else:
        arrived = [ring(parts[step], step) for step in range(1, groups)]

    up, stats = pl.pallas_call(
        functools.partial(upstream_kernel, groups),
        out_shape=[
            jax.ShapeDtypeStruct((long_rows, columns), bf16),
            jax.ShapeDtypeStruct((BLK, BLK), f32),
        ],
        in_specs=[HBM] * 3 + [VMEM] * 2 + [ANY] * (groups - 1 + 1),
        out_specs=[VMEM] * 2,
        scratch_shapes=[
            pltpu.SMEM(key_blocks.shape, i32),
            pltpu.VMEM((columns, width), bf16),
            pltpu.VMEM((rows, width), bf16),
            pltpu.SemaphoreType.DMA((5 + groups,)),
        ],
        compiler_params=params(60),
        cost_estimate=cost(1000, 1000),
        name="upstream",
    )(key_blocks, out_weight, grad_mixed, o32, lse, *pieces[1:], q_win[1])
    up_win = exchange_pair(up, size)

    grad_query = pl.pallas_call(
        functools.partial(query_kernel, size, v_tags),
        out_shape=jax.ShapeDtypeStruct((rows, columns), bf16),
        in_specs=[HBM] * 4 + [VMEM] * 2 + [ANY] * (len(PAIR) + len(v_tags) + 1),
        out_specs=VMEM,
        scratch_shapes=scalars
        + [
            pltpu.VMEM((rows, columns), bf16),
            pltpu.VMEM((places * BLK, columns), bf16),
            pltpu.VMEM((places * BLK, columns), bf16),
            pltpu.SemaphoreType.DMA((4 + 2 * places,)),
        ],
        compiler_params=params(60),
        cost_estimate=cost(16 * 10**9, 32 * 10**6),
        name="query_grad",
    )(key_blocks, host_ids, host_bias, query_states, up, stats, *k_win, *v_win, q_win[4])

    grad_key, grad_value = pl.pallas_call(
        functools.partial(key_kernel, size, neigh),
        out_shape=[jax.ShapeDtypeStruct((rows, columns), bf16)] * 2,
        in_specs=[HBM] * 5 + [ANY] * (2 * nsh - 1),
        out_specs=[VMEM] * 2,
        scratch_shapes=[
            pltpu.SMEM(host_ids.shape, i32),
            pltpu.SMEM(host_bias.shape, f32),
            pltpu.VMEM((rows, columns), bf16),
            pltpu.VMEM((rows, columns), bf16),
            pltpu.VMEM((nsh * rows, columns), bf16),
            pltpu.VMEM((nsh * long_rows, columns), bf16),
            pltpu.VMEM((nsh + 1, high, BLK), f32),
            pltpu.VMEM((8, BLK), i32),
            pltpu.SMEM((8, BLK), i32),
            pltpu.SMEM((blocks_dev, nsh * blocks_dev + 2), i32),
            pltpu.VMEM((rows, columns), f32),
            pltpu.VMEM((rows, columns), f32),
            pltpu.SemaphoreType.DMA((3 * nsh + 5,)),
        ],
        compiler_params=params(60),
        cost_estimate=cost(1000, 1000),
        name="key_grad",
    )(host_ids, host_bias, key_states, value_states, query_states, *q_win[1:], *up_win)

    mixed_out = sum_after((parts[0], *arrived), grad_key)
    return (mixed_out, grad_query, grad_key, grad_value)


def solution(mesh):
    in_specs = (
        P("ctx", "head"),
        P("ctx", "head"),
        P("ctx", "head"),
        P("head", None),
        P(("ctx", "head"), None),
        P("ctx", None),
        P(),
        P("head"),
    )
    out_specs = (P(("ctx", "head"), None), P("ctx", "head"), P("ctx", "head"), P("ctx", "head"))
    return jax.shard_map(
        per_device, mesh=mesh, in_specs=in_specs, out_specs=out_specs, check_vma=False
    )
```

```python
import functools

import jax
import jax.numpy as jnp
from jax import lax
from jax.experimental import pallas as pl
from jax.experimental.pallas import tpu as pltpu
from jax.sharding import PartitionSpec as P

HDIM = 128
BLK = 128
HOPS = 2
SCALE = HDIM ** (-0.5)
CUBE = (0, 1, 2, 3, 6, 7)
PAIR = (0, 1, 2, -2, -1)
NT = (((1,), (1,)), ((), ()))
VMEM = pl.BlockSpec(memory_space=pltpu.VMEM)
SMEM = pl.BlockSpec(memory_space=pltpu.SMEM)
ANY = pl.BlockSpec(memory_space=pl.ANY)
HBM = pl.BlockSpec(memory_space=pltpu.HBM)
NEVER = 1e30


def params(mebibytes):
    return pltpu.CompilerParams(vmem_limit_bytes=mebibytes * 1024 * 1024)


def ndot(a, b):
    return lax.dot_general(a, b, (((1,), (0,)), ((), ())), preferred_element_type=jnp.float32)


def tdot(a, b):
    return lax.dot_general(a, b, NT, preferred_element_type=jnp.float32)


def stat_rows(pairs):
    return -(-2 * pairs // 16) * 16


def tag_owner(position, tag, size, tags):
    if tags is CUBE:
        return position ^ tag
    return lax.rem(position + jnp.where(position % 2 == 0, tag, -tag) + size, size)


def find_shard(position, owner, size, tags):
    shard = 0
    for index, tag in enumerate(tags):
        shard = shard + jnp.where(tag_owner(position, tag, size, tags) == owner, index, 0)
    return shard


def permute_from(x, size, source):
    return lax.ppermute(x, "ctx", [(source(i) % size, i) for i in range(size)])


def exchange_pair(x, size):
    sign = lambda i: 1 if i % 2 == 0 else -1
    share = permute_from(x, size, lambda i: i + 2 * sign(i))
    solo = permute_from(x, size, lambda i: i - 2 * sign(i))
    mate = permute_from(x, size, lambda i: i ^ 1)
    return [x, mate, share, solo, permute_from(share, size, lambda i: i ^ 1)]


def exchange_cube(x, size):
    near = permute_from(x, size, lambda i: i ^ 2)
    far = permute_from(near, size, lambda i: i ^ 4)
    mate = permute_from(x, size, lambda i: i ^ 1)
    swap = lambda i: i ^ 1
    return [x, mate, near, permute_from(near, size, swap), far, permute_from(far, size, swap)]


def start_all(pairs, sem, first=0):
    copies = []
    for index, (source, target) in enumerate(pairs):
        copy = pltpu.make_async_copy(source, target, sem.at[first + index])
        copy.start()
        copies.append(copy)
    return copies


def wait_all(copies):
    for copy in copies:
        copy.wait()


def gather_blocks(size, tags, keys, refs, target, sem, first, blocks_dev, neigh):
    position = lax.axis_index("ctx")
    waits = []
    for b in range(blocks_dev):
        for n in range(neigh):
            j = keys[b, n]
            shard = find_shard(position, lax.div(j, blocks_dev), size, tags)
            row = pl.multiple_of(lax.rem(j, blocks_dev) * BLK, BLK)
            place = b * neigh + n
            for index, ref in enumerate(refs):

                @pl.when(shard == index)
                def _(ref=ref, place=place, row=row):
                    pltpu.make_async_copy(
                        ref.at[pl.ds(row, BLK)], target.at[pl.ds(place * BLK, BLK)], sem.at[first + place]
                    ).start()

            waits.append(
                pltpu.make_async_copy(
                    refs[0].at[pl.ds(0, BLK)], target.at[pl.ds(place * BLK, BLK)], sem.at[first + place]
                )
            )
    return waits


def shift_rows(keys, hosts, bias, b, h, blocks_dev, neigh):
    position = lax.axis_index("ctx")
    slot = lax.broadcasted_iota(jnp.int32, (1, neigh * BLK), 1) // BLK
    shift = jnp.zeros((1, neigh * BLK), jnp.float32)
    host = hosts[position * blocks_dev + b]
    for n in range(neigh):
        value = jnp.where(hosts[keys[b, n]] == host, bias[h], 0.0)
        shift = jnp.where(slot == n, value, shift)
    return shift


def piece_owner(me, step, groups, sign):
    return me ^ step if groups == 4 else lax.rem(me + sign * step + groups, groups)


def attend_kernel(size, groups, v_tags, *refs):
    keys_hbm, hosts_hbm, bias_hbm, q_hbm, w_hbm = refs[:5]
    k_refs = refs[5:5 + len(PAIR)]
    v_refs = refs[5 + len(PAIR):5 + len(PAIR) + len(v_tags)]
    rest = refs[5 + len(PAIR) + len(v_tags):]
    part_refs = rest[:groups]
    o32_ref, lse_ref = rest[groups:groups + 2]
    keys, hosts, bias, q_ref, w_ref, kcat, vcat, score, att, turned, sem = rest[groups + 2:]
    rows, columns = q_ref.shape
    blocks_dev, neigh = keys.shape
    heads_dev = columns // HDIM
    small = start_all([(keys_hbm, keys), (hosts_hbm, hosts), (bias_hbm, bias)], sem)
    large = start_all([(q_hbm, q_ref), (w_hbm, w_ref)], sem, 3)
    wait_all(small)
    places = blocks_dev * neigh
    k_waits = gather_blocks(size, PAIR, keys, k_refs, kcat, sem, 5, blocks_dev, neigh)
    v_waits = gather_blocks(size, v_tags, keys, v_refs, vcat, sem, 5 + places, blocks_dev, neigh)
    large[0].wait()
    wait_all(k_waits)
    span = neigh * BLK
    units = [(b, h) for b in range(blocks_dev) for h in range(heads_dev)]
    for b, h in units:
        cols = slice(h * HDIM, (h + 1) * HDIM)
        s = tdot(q_ref[b * BLK:(b + 1) * BLK, cols], kcat[b * span:(b + 1) * span, cols])
        score[b * heads_dev + h] = s * SCALE + shift_rows(keys, hosts, bias, b, h, blocks_dev, neigh)
    wait_all(v_waits)
    lane = lax.broadcasted_iota(jnp.int32, (BLK, BLK), 1)
    lse_all = jnp.zeros((BLK, BLK), jnp.float32)
    for b, h in units:
        cols = slice(h * HDIM, (h + 1) * HDIM)
        s = score[b * heads_dev + h]
        top = jnp.max(s, axis=1, keepdims=True)
        weights = jnp.exp(s - top)
        total = jnp.sum(weights, axis=1, keepdims=True)
        probs = (weights * (1.0 / total)).astype(jnp.bfloat16)
        out = ndot(probs, vcat[b * span:(b + 1) * span, cols])
        o32_ref[b * BLK:(b + 1) * BLK, cols] = out
        att[b * BLK:(b + 1) * BLK, cols] = out.astype(jnp.bfloat16)
        lse_all = jnp.where(lane == b * heads_dev + h, top + jnp.log(total), lse_all)
    lse_ref[...] = lse_all
    large[1].wait()
    me = lax.axis_index("head")
    part = rows // groups
    for step in range(groups):
        owner = piece_owner(me, step, groups, 1)
        turned[step * part:(step + 1) * part, :] = att[pl.ds(pl.multiple_of(owner * part, part), part), :]
    mixed = ndot(turned[...], w_ref[...]).astype(jnp.bfloat16)
    for step in range(groups):
        part_refs[step][...] = mixed[step * part:(step + 1) * part, :]


def upstream_kernel(groups, *refs):
    keys_hbm, w_hbm, own_hbm, o32_any, lse_any = refs[:5]
    piece_refs = refs[5:4 + groups]
    rest = refs[4 + groups + 1:]
    up_ref, stats_ref, keys, w_ref, grads, o32_ref, lse_ref, sem = rest
    rows, columns = o32_ref.shape
    blocks_dev, neigh = keys.shape
    heads_dev = columns // HDIM
    part = rows // groups
    cut = columns // 2
    waits = [
        start_all([(w_hbm.at[c * cut:(c + 1) * cut], w_ref.at[c * cut:(c + 1) * cut])], sem, c)[0]
        for c in range(2)
    ]
    pieces = (own_hbm,) + tuple(piece_refs)
    early = start_all(
        [(ref, grads.at[pl.ds(step * part, part)]) for step, ref in enumerate(pieces)]
        + [(keys_hbm, keys)],
        sem,
        2,
    )
    late = start_all([(o32_any, o32_ref), (lse_any, lse_ref)], sem, 3 + groups)
    wait_all(early)
    me = lax.axis_index("head")
    for c in range(2):
        waits[c].wait()
        product = tdot(grads[...], w_ref[c * cut:(c + 1) * cut, :]).astype(jnp.bfloat16)
        for step in range(groups):
            owner = piece_owner(me, step, groups, -1)
            up_ref[pl.ds(pl.multiple_of(owner * part, part), part), c * cut:(c + 1) * cut] = product[
                step * part:(step + 1) * part, :
            ]
    wait_all(late)
    pairs = blocks_dev * heads_dev
    lane = lax.broadcasted_iota(jnp.int32, (BLK, BLK), 1)
    stats = lse_ref[...]
    for b in range(blocks_dev):
        for h in range(heads_dev):
            cols = slice(h * HDIM, (h + 1) * HDIM)
            up = up_ref[b * BLK:(b + 1) * BLK, cols].astype(jnp.float32)
            term = jnp.sum(up * o32_ref[b * BLK:(b + 1) * BLK, cols], axis=1, keepdims=True)
            stats = jnp.where(lane == pairs + b * heads_dev + h, term, stats)
    stats_ref[...] = stats
    high = stat_rows(pairs)
    turned = jnp.transpose(stats)[:high, :]
    up_ref[rows:, :] = jnp.zeros((up_ref.shape[0] - rows, columns), jnp.bfloat16)
    pieces = []
    for index in range(3):
        piece = turned.astype(jnp.bfloat16)
        turned = turned - piece.astype(jnp.float32)
        pieces.append(piece)
    spot = lax.broadcasted_iota(jnp.int32, (high, BLK), 1)
    line = lax.broadcasted_iota(jnp.int32, (high, BLK), 0)
    listed = jnp.zeros((high, BLK), jnp.int32)
    for b in range(blocks_dev):
        for n in range(neigh):
            listed = jnp.where(spot == b * neigh + n, keys[b, n], listed)
    listed = jnp.where(line == 0, listed >> 7, listed & 127)
    pieces.append(listed.astype(jnp.float32).astype(jnp.bfloat16))
    for index, piece in enumerate(pieces):
        row = rows + high * (index * BLK // columns)
        col = index * BLK % columns
        up_ref[row:row + high, col:col + BLK] = piece


def query_kernel(size, v_tags, *refs):
    keys_hbm, hosts_hbm, bias_hbm, q_hbm, up_ref, stats_ref = refs[:6]
    k_refs = refs[6:6 + len(PAIR)]
    v_refs = refs[6 + len(PAIR):6 + len(PAIR) + len(v_tags)]
    dq_ref, keys, hosts, bias, q_ref, kcat, vcat, sem = refs[6 + len(PAIR) + len(v_tags) + 1:]
    rows, columns = q_ref.shape
    blocks_dev, neigh = keys.shape
    heads_dev = columns // HDIM
    pairs = blocks_dev * heads_dev
    small = start_all([(keys_hbm, keys), (hosts_hbm, hosts), (bias_hbm, bias)], sem)
    large = start_all([(q_hbm, q_ref)], sem, 3)
    wait_all(small)
    places = blocks_dev * neigh
    waits = gather_blocks(size, PAIR, keys, k_refs, kcat, sem, 4, blocks_dev, neigh)
    waits += gather_blocks(size, v_tags, keys, v_refs, vcat, sem, 4 + places, blocks_dev, neigh)
    wait_all(large)
    wait_all(waits)
    span = neigh * BLK
    for b in range(blocks_dev):
        for h in range(heads_dev):
            cols = slice(h * HDIM, (h + 1) * HDIM)
            pair = b * heads_dev + h
            q = q_ref[b * BLK:(b + 1) * BLK, cols]
            up = up_ref[b * BLK:(b + 1) * BLK, cols]
            k = kcat[b * span:(b + 1) * span, cols]
            lse = stats_ref[:, pair:pair + 1]
            term = stats_ref[:, pairs + pair:pairs + pair + 1]
            shift = shift_rows(keys, hosts, bias, b, h, blocks_dev, neigh)
            p = jnp.exp(tdot(q, k) * SCALE + shift - lse)
            dp = tdot(up, vcat[b * span:(b + 1) * span, cols])
            ds = (p * (dp - term) * SCALE).astype(jnp.bfloat16)
            dq_ref[b * BLK:(b + 1) * BLK, cols] = ndot(ds, k).astype(jnp.bfloat16)


def key_kernel(size, neigh, *refs):
    nsh = len(PAIR)
    hosts_hbm, bias_hbm, k_hbm, v_hbm = refs[:4]
    q_refs = refs[4:4 + nsh]
    up_refs = refs[4 + nsh:4 + 2 * nsh]
    dk_ref, dv_ref, mark_ref = refs[4 + 2 * nsh:7 + 2 * nsh]
    (hosts, bias, k_ref, v_ref, qwin, upwin, stats, lists, keys, hits, dk_acc, dv_acc, sem) = refs[
        7 + 2 * nsh:
    ]
    rows, columns = k_ref.shape
    long_rows = up_refs[0].shape[0]
    blocks_dev = rows // BLK
    heads_dev = columns // HDIM
    pairs = blocks_dev * heads_dev
    high = stat_rows(pairs)
    position = lax.axis_index("ctx")
    tail = [
        (ref.at[pl.ds(rows, long_rows - rows)], upwin.at[pl.ds(i * long_rows + rows, long_rows - rows)])
        for i, ref in enumerate(up_refs)
    ]
    first = start_all(tail, sem)
    body = [(ref.at[pl.ds(0, rows)], upwin.at[pl.ds(i * long_rows, rows)]) for i, ref in enumerate(up_refs)]
    body += [(ref, qwin.at[pl.ds(i * rows, rows)]) for i, ref in enumerate(q_refs)]
    body += [(hosts_hbm, hosts), (bias_hbm, bias), (k_hbm, k_ref), (v_hbm, v_ref)]
    later = start_all(body, sem, nsh)
    dk_acc[...] = jnp.zeros_like(dk_acc)
    dv_acc[...] = jnp.zeros_like(dv_acc)
    wait_all(first)

    def part_of(index, piece):
        row = index * long_rows + rows + high * (piece * BLK // columns)
        col = piece * BLK % columns
        return upwin[row:row + high, col:col + BLK].astype(jnp.float32)

    for index in range(nsh):
        stats[index] = (part_of(index, 2) + part_of(index, 1)) + part_of(index, 0)
        listed = part_of(index, 3).astype(jnp.int32)
        lists[index:index + 1, :] = listed[0:1, :] * 128 + listed[1:2, :]
    stats[nsh] = jnp.full((high, BLK), NEVER, jnp.float32)
    copy = pltpu.make_async_copy(lists, keys, sem.at[3 * nsh + 4])
    copy.start()
    copy.wait()

    counts = []
    for own in range(blocks_dev):
        mine = position * blocks_dev + own
        count = 0
        for index in range(nsh):
            for inner in range(blocks_dev):
                hit = keys[index, inner * neigh] == mine
                for n in range(1, neigh):
                    hit = hit | (keys[index, inner * neigh + n] == mine)
                hits[own, count] = index * blocks_dev + inner
                count = count + jnp.where(hit, 1, 0)
        hits[own, count] = -1
        counts.append(count)
    wait_all(later)

    for own in range(blocks_dev):
        mine = position * blocks_dev + own
        krow = slice(own * BLK, (own + 1) * BLK)

        def visit(step, carry, own=own, mine=mine, krow=krow):
            qs, ups, sames, lses, terms = [], [], [], [], []
            for turn in range(2):
                entry = hits[own, 2 * step + turn]
                spare = entry < 0
                entry = jnp.where(spare, 0, entry)
                shard = lax.div(entry, blocks_dev)
                inner = lax.rem(entry, blocks_dev)
                owner = 0
                for index, tag in enumerate(PAIR):
                    owner = owner + jnp.where(shard == index, tag_owner(position, tag, size, PAIR), 0)
                sames.append(hosts[owner * blocks_dev + inner] == hosts[mine])
                qs.append(pl.ds(pl.multiple_of(shard * rows + inner * BLK, BLK), BLK))
                ups.append(pl.ds(pl.multiple_of(shard * long_rows + inner * BLK, 16), BLK))
                lses.append((jnp.where(spare, nsh, shard), inner))
                terms.append((shard, inner))
            for h in range(heads_dev):
                cols = slice(h * HDIM, (h + 1) * HDIM)
                k = k_ref[krow, cols]
                v = v_ref[krow, cols]
                q = jnp.concatenate([qwin[r, cols] for r in qs], axis=0)
                up = jnp.concatenate([upwin[r, cols] for r in ups], axis=0)
                less = jnp.concatenate(
                    [
                        stats[shard, pl.ds(inner * heads_dev + h, 1), :] - jnp.where(same, bias[h], 0.0)
                        for (shard, inner), same in zip(lses, sames)
                    ],
                    axis=1,
                )
                term = jnp.concatenate(
                    [stats[shard, pl.ds(pairs + inner * heads_dev + h, 1), :] for shard, inner in terms],
                    axis=1,
                )
                p = jnp.exp(tdot(k, q) * SCALE - less)
                ds = (p * (tdot(v, up) - term) * SCALE).astype(jnp.bfloat16)
                dk_acc[krow, cols] += ndot(ds, q)
                dv_acc[krow, cols] += ndot(p.astype(jnp.bfloat16), up)
            return carry

        lax.fori_loop(0, lax.div(counts[own] + 1, 2), visit, 0)
    dk_ref[...] = dk_acc[...].astype(jnp.bfloat16)
    dv_ref[...] = dv_acc[...].astype(jnp.bfloat16)
    mark_ref[...] = jnp.zeros_like(mark_ref)


def sum_kernel(count, *refs):
    total = refs[0][...].astype(jnp.float32)
    for ref in refs[1:count]:
        total = total + ref[...].astype(jnp.float32)
    refs[-1][...] = total.astype(jnp.bfloat16)


def sum_after(arrays, before):
    return pl.pallas_call(
        functools.partial(sum_kernel, len(arrays)),
        out_shape=jax.ShapeDtypeStruct(arrays[0].shape, jnp.bfloat16),
        in_specs=[VMEM] * len(arrays) + [ANY],
        out_specs=VMEM,
        compiler_params=params(8),
        cost_estimate=cost(1000, 1000),
        name="sum_after",
    )(*arrays, before)


def copy_kernel(count, extra, *refs):
    sources, targets = refs[:count], refs[count + extra:2 * count + extra]
    between, sem = refs[2 * count + extra:-1], refs[-1]
    wait_all(start_all(list(zip(sources, between)), sem))
    wait_all(start_all(list(zip(between, targets)), sem))


def copies_after(arrays, before):
    return pl.pallas_call(
        functools.partial(copy_kernel, len(arrays), len(before)),
        out_shape=[jax.ShapeDtypeStruct(x.shape, x.dtype) for x in arrays],
        in_specs=[ANY] * (len(arrays) + len(before)),
        out_specs=[ANY] * len(arrays),
        scratch_shapes=[pltpu.VMEM(x.shape, x.dtype) for x in arrays]
        + [pltpu.SemaphoreType.DMA((len(arrays),))],
        compiler_params=params(60),
        cost_estimate=cost(1000, 1000),
        name="copies_after",
    )(*arrays, *before)


def cost(flops, nbytes):
    return pl.CostEstimate(flops=flops, bytes_accessed=nbytes, transcendentals=0)


def per_device(
    query_states, key_states, value_states, out_weight, grad_mixed, key_blocks, host_ids, host_bias
):
    size = lax.axis_size("ctx")
    rows, columns = query_states.shape
    width = out_weight.shape[1]
    blocks_dev, neigh = key_blocks.shape
    heads_dev = columns // HDIM
    pairs = blocks_dev * heads_dev
    places = blocks_dev * neigh
    groups = lax.axis_size("head")
    part = rows // groups
    v_tags = CUBE if size == 8 else PAIR
    nsh = len(PAIR)
    bf16, f32, i32 = jnp.bfloat16, jnp.float32, jnp.int32
    high = stat_rows(pairs)
    extra = high * (-(-4 * BLK // columns))
    long_rows = rows + extra

    def ring(x, step):
        return lax.ppermute(x, "head", [(i, (i + step) % groups) for i in range(groups)])

    def flip(x, mask):
        return lax.ppermute(x, "head", [(i, i ^ mask) for i in range(groups)])

    paired = groups == 4
    v_win = exchange_cube(value_states, size) if v_tags is CUBE else exchange_pair(value_states, size)
    k_win = exchange_pair(key_states, size)
    if paired:
        opposite = flip(grad_mixed, 2)
        beside = flip(grad_mixed, 1)
        pieces = [grad_mixed, beside, opposite, flip(opposite, 1)]
    else:
        pieces = [grad_mixed] + [ring(grad_mixed, step) for step in range(1, groups)]
    (late_query,) = copies_after((query_states,), (pieces[1], pieces[2]))
    q_win = exchange_pair(late_query, size)
    scalars = [
        pltpu.SMEM(key_blocks.shape, i32),
        pltpu.SMEM(host_ids.shape, i32),
        pltpu.SMEM(host_bias.shape, f32),
    ]

    parts_o32_lse = pl.pallas_call(
        functools.partial(attend_kernel, size, groups, v_tags),
        out_shape=[jax.ShapeDtypeStruct((part, width), bf16)] * groups
        + [jax.ShapeDtypeStruct((rows, columns), f32), jax.ShapeDtypeStruct((BLK, BLK), f32)],
        in_specs=[HBM] * 5 + [ANY] * (len(PAIR) + len(v_tags)),
        out_specs=[VMEM] * (groups + 2),
        scratch_shapes=scalars
        + [
            pltpu.VMEM((rows, columns), bf16),
            pltpu.VMEM((columns, width), bf16),
            pltpu.VMEM((places * BLK, columns), bf16),
            pltpu.VMEM((places * BLK, columns), bf16),
            pltpu.VMEM((pairs, BLK, neigh * BLK), f32),
            pltpu.VMEM((rows, columns), bf16),
            pltpu.VMEM((rows, columns), bf16),
            pltpu.SemaphoreType.DMA((5 + 2 * places,)),
        ],
        compiler_params=params(60),
        cost_estimate=cost(10**9, 10**6),
        name="attend",
    )(key_blocks, host_ids, host_bias, query_states, out_weight, *k_win, *v_win)
    parts = parts_o32_lse[:groups]
    o32, lse = parts_o32_lse[groups:]
    mixed = parts[0].astype(f32)
    if paired:
        relay = flip(parts[3], 1)
        beside_sum = flip(parts[1], 1)
        passed = (parts[2].astype(f32) + relay.astype(f32)).astype(bf16)
        arrived = [beside_sum, flip(passed, 2)]
    else:
        arrived = [ring(parts[step], step) for step in range(1, groups)]

    up, stats = pl.pallas_call(
        functools.partial(upstream_kernel, groups),
        out_shape=[
            jax.ShapeDtypeStruct((long_rows, columns), bf16),
            jax.ShapeDtypeStruct((BLK, BLK), f32),
        ],
        in_specs=[HBM] * 3 + [ANY] * (groups + 2),
        out_specs=[VMEM] * 2,
        scratch_shapes=[
            pltpu.SMEM(key_blocks.shape, i32),
            pltpu.VMEM((columns, width), bf16),
            pltpu.VMEM((rows, width), bf16),
            pltpu.VMEM((rows, columns), f32),
            pltpu.VMEM((BLK, BLK), f32),
            pltpu.SemaphoreType.DMA((5 + groups,)),
        ],
        compiler_params=params(60),
        cost_estimate=cost(1000, 1000),
        name="upstream",
    )(key_blocks, out_weight, grad_mixed, o32, lse, *pieces[1:], q_win[1])
    up_win = exchange_pair(up, size)

    grad_query = pl.pallas_call(
        functools.partial(query_kernel, size, v_tags),
        out_shape=jax.ShapeDtypeStruct((rows, columns), bf16),
        in_specs=[HBM] * 4 + [VMEM] * 2 + [ANY] * (len(PAIR) + len(v_tags) + 1),
        out_specs=VMEM,
        scratch_shapes=scalars
        + [
            pltpu.VMEM((rows, columns), bf16),
            pltpu.VMEM((places * BLK, columns), bf16),
            pltpu.VMEM((places * BLK, columns), bf16),
            pltpu.SemaphoreType.DMA((4 + 2 * places,)),
        ],
        compiler_params=params(20),
        cost_estimate=cost(16 * 10**9, 32 * 10**6),
        name="query_grad",
    )(key_blocks, host_ids, host_bias, query_states, up, stats, *k_win, *v_win, q_win[4])

    grad_key, grad_value, mark = pl.pallas_call(
        functools.partial(key_kernel, size, neigh),
        out_shape=[jax.ShapeDtypeStruct((rows, columns), bf16)] * 2
        + [jax.ShapeDtypeStruct((8, BLK), f32)],
        in_specs=[HBM] * 5 + [ANY] * (2 * nsh - 1),
        out_specs=[VMEM] * 3,
        scratch_shapes=[
            pltpu.SMEM(host_ids.shape, i32),
            pltpu.SMEM(host_bias.shape, f32),
            pltpu.VMEM((rows, columns), bf16),
            pltpu.VMEM((rows, columns), bf16),
            pltpu.VMEM((nsh * rows, columns), bf16),
            pltpu.VMEM((nsh * long_rows, columns), bf16),
            pltpu.VMEM((nsh + 1, high, BLK), f32),
            pltpu.VMEM((8, BLK), i32),
            pltpu.SMEM((8, BLK), i32),
            pltpu.SMEM((blocks_dev, nsh * blocks_dev + 2), i32),
            pltpu.VMEM((rows, columns), f32),
            pltpu.VMEM((rows, columns), f32),
            pltpu.SemaphoreType.DMA((3 * nsh + 5,)),
        ],
        compiler_params=params(20),
        cost_estimate=cost(1000, 1000),
        name="key_grad",
    )(host_ids, host_bias, key_states, value_states, query_states, *q_win[1:], *up_win)

    mixed_out = sum_after((parts[0], *arrived), mark)
    return (mixed_out, grad_query, grad_key, grad_value)


def solution(mesh):
    in_specs = (
        P("ctx", "head"),
        P("ctx", "head"),
        P("ctx", "head"),
        P("head", None),
        P(("ctx", "head"), None),
        P("ctx", None),
        P(),
        P("head"),
    )
    out_specs = (P(("ctx", "head"), None), P("ctx", "head"), P("ctx", "head"), P("ctx", "head"))
    return jax.shard_map(
        per_device, mesh=mesh, in_specs=in_specs, out_specs=out_specs, check_vma=False
    )
```

```python
import functools

import jax
import jax.numpy as jnp
from jax import lax
from jax.experimental import pallas as pl
from jax.experimental.pallas import tpu as pltpu
from jax.sharding import PartitionSpec as P

HDIM = 128
BLK = 128
HOPS = 2
SCALE = HDIM ** (-0.5)
CUBE = (0, 1, 2, 3, 6, 7)
PAIR = (0, 1, 2, -2, -1)
NT = (((1,), (1,)), ((), ()))
VMEM = pl.BlockSpec(memory_space=pltpu.VMEM)
SMEM = pl.BlockSpec(memory_space=pltpu.SMEM)
ANY = pl.BlockSpec(memory_space=pl.ANY)
HBM = pl.BlockSpec(memory_space=pltpu.HBM)
NEVER = 1e30


def params(mebibytes):
    return pltpu.CompilerParams(vmem_limit_bytes=mebibytes * 1024 * 1024)


def ndot(a, b):
    return lax.dot_general(a, b, (((1,), (0,)), ((), ())), preferred_element_type=jnp.float32)


def tdot(a, b):
    return lax.dot_general(a, b, NT, preferred_element_type=jnp.float32)


def stat_rows(pairs):
    return -(-2 * pairs // 16) * 16


def tag_owner(position, tag, size, tags):
    if tags is CUBE:
        return position ^ tag
    return lax.rem(position + jnp.where(position % 2 == 0, tag, -tag) + size, size)


def find_shard(position, owner, size, tags):
    shard = 0
    for index, tag in enumerate(tags):
        shard = shard + jnp.where(tag_owner(position, tag, size, tags) == owner, index, 0)
    return shard


def permute_from(x, size, source):
    return lax.ppermute(x, "ctx", [(source(i) % size, i) for i in range(size)])


def exchange_pair(x, size):
    sign = lambda i: 1 if i % 2 == 0 else -1
    share = permute_from(x, size, lambda i: i + 2 * sign(i))
    solo = permute_from(x, size, lambda i: i - 2 * sign(i))
    mate = permute_from(x, size, lambda i: i ^ 1)
    return [x, mate, share, solo, permute_from(share, size, lambda i: i ^ 1)]


def exchange_cube(x, size):
    near = permute_from(x, size, lambda i: i ^ 2)
    far = permute_from(near, size, lambda i: i ^ 4)
    mate = permute_from(x, size, lambda i: i ^ 1)
    swap = lambda i: i ^ 1
    return [x, mate, near, permute_from(near, size, swap), far, permute_from(far, size, swap)]


def start_all(pairs, sem, first=0):
    copies = []
    for index, (source, target) in enumerate(pairs):
        copy = pltpu.make_async_copy(source, target, sem.at[first + index])
        copy.start()
        copies.append(copy)
    return copies


def wait_all(copies):
    for copy in copies:
        copy.wait()


def gather_blocks(size, tags, keys, refs, target, sem, first, blocks_dev, neigh):
    position = lax.axis_index("ctx")
    waits = []
    for b in range(blocks_dev):
        for n in range(neigh):
            j = keys[b, n]
            shard = find_shard(position, lax.div(j, blocks_dev), size, tags)
            row = pl.multiple_of(lax.rem(j, blocks_dev) * BLK, BLK)
            place = b * neigh + n
            for index, ref in enumerate(refs):

                @pl.when(shard == index)
                def _(ref=ref, place=place, row=row):
                    pltpu.make_async_copy(
                        ref.at[pl.ds(row, BLK)], target.at[pl.ds(place * BLK, BLK)], sem.at[first + place]
                    ).start()

            waits.append(
                pltpu.make_async_copy(
                    refs[0].at[pl.ds(0, BLK)], target.at[pl.ds(place * BLK, BLK)], sem.at[first + place]
                )
            )
    return waits


def shift_rows(keys, hosts, bias, b, h, blocks_dev, neigh):
    position = lax.axis_index("ctx")
    slot = lax.broadcasted_iota(jnp.int32, (1, neigh * BLK), 1) // BLK
    shift = jnp.zeros((1, neigh * BLK), jnp.float32)
    host = hosts[position * blocks_dev + b]
    for n in range(neigh):
        value = jnp.where(hosts[keys[b, n]] == host, bias[h], 0.0)
        shift = jnp.where(slot == n, value, shift)
    return shift


def piece_owner(me, step, groups, sign):
    return me ^ step if groups == 4 else lax.rem(me + sign * step + groups, groups)


def attend_kernel(size, groups, v_tags, *refs):
    keys_hbm, hosts_hbm, bias_hbm, q_hbm, w_hbm = refs[:5]
    k_refs = refs[5:5 + len(PAIR)]
    v_refs = refs[5 + len(PAIR):5 + len(PAIR) + len(v_tags)]
    rest = refs[5 + len(PAIR) + len(v_tags):]
    part_refs = rest[:groups]
    o32_ref, lse_ref = rest[groups:groups + 2]
    keys, hosts, bias, q_ref, w_ref, kcat, vcat, score, att, turned, sem = rest[groups + 2:]
    rows, columns = q_ref.shape
    blocks_dev, neigh = keys.shape
    heads_dev = columns // HDIM
    small = start_all([(keys_hbm, keys), (hosts_hbm, hosts), (bias_hbm, bias)], sem)
    large = start_all([(q_hbm, q_ref), (w_hbm, w_ref)], sem, 3)
    wait_all(small)
    places = blocks_dev * neigh
    k_waits = gather_blocks(size, PAIR, keys, k_refs, kcat, sem, 5, blocks_dev, neigh)
    v_waits = gather_blocks(size, v_tags, keys, v_refs, vcat, sem, 5 + places, blocks_dev, neigh)
    large[0].wait()
    wait_all(k_waits)
    span = neigh * BLK
    units = [(b, h) for b in range(blocks_dev) for h in range(heads_dev)]
    for b, h in units:
        cols = slice(h * HDIM, (h + 1) * HDIM)
        s = tdot(q_ref[b * BLK:(b + 1) * BLK, cols], kcat[b * span:(b + 1) * span, cols])
        score[b * heads_dev + h] = s * SCALE + shift_rows(keys, hosts, bias, b, h, blocks_dev, neigh)
    wait_all(v_waits)
    lane = lax.broadcasted_iota(jnp.int32, (BLK, BLK), 1)
    lse_all = jnp.zeros((BLK, BLK), jnp.float32)
    for b, h in units:
        cols = slice(h * HDIM, (h + 1) * HDIM)
        s = score[b * heads_dev + h]
        top = jnp.max(s, axis=1, keepdims=True)
        weights = jnp.exp(s - top)
        total = jnp.sum(weights, axis=1, keepdims=True)
        probs = (weights * (1.0 / total)).astype(jnp.bfloat16)
        out = ndot(probs, vcat[b * span:(b + 1) * span, cols])
        o32_ref[b * BLK:(b + 1) * BLK, cols] = out
        att[b * BLK:(b + 1) * BLK, cols] = out.astype(jnp.bfloat16)
        lse_all = jnp.where(lane == b * heads_dev + h, top + jnp.log(total), lse_all)
    lse_ref[...] = lse_all
    large[1].wait()
    me = lax.axis_index("head")
    part = rows // groups
    for step in range(groups):
        owner = piece_owner(me, step, groups, 1)
        turned[step * part:(step + 1) * part, :] = att[pl.ds(pl.multiple_of(owner * part, part), part), :]
    mixed = ndot(turned[...], w_ref[...]).astype(jnp.bfloat16)
    for step in range(groups):
        part_refs[step][...] = mixed[step * part:(step + 1) * part, :]


def upstream_kernel(groups, *refs):
    keys_hbm, w_hbm, own_hbm, o32_any, lse_any = refs[:5]
    piece_refs = refs[5:4 + groups]
    rest = refs[4 + groups + 1:]
    up_ref, stats_ref, keys, w_ref, grads, o32_ref, lse_ref, sem = rest
    rows, columns = o32_ref.shape
    blocks_dev, neigh = keys.shape
    heads_dev = columns // HDIM
    part = rows // groups
    cut = columns // 2
    waits = [
        start_all([(w_hbm.at[c * cut:(c + 1) * cut], w_ref.at[c * cut:(c + 1) * cut])], sem, c)[0]
        for c in range(2)
    ]
    pieces = (own_hbm,) + tuple(piece_refs)
    early = start_all(
        [(ref, grads.at[pl.ds(step * part, part)]) for step, ref in enumerate(pieces)]
        + [(keys_hbm, keys)],
        sem,
        2,
    )
    late = start_all([(o32_any, o32_ref), (lse_any, lse_ref)], sem, 3 + groups)
    wait_all(early)
    me = lax.axis_index("head")
    for c in range(2):
        waits[c].wait()
        product = tdot(grads[...], w_ref[c * cut:(c + 1) * cut, :]).astype(jnp.bfloat16)
        for step in range(groups):
            owner = piece_owner(me, step, groups, -1)
            up_ref[pl.ds(pl.multiple_of(owner * part, part), part), c * cut:(c + 1) * cut] = product[
                step * part:(step + 1) * part, :
            ]
    wait_all(late)
    pairs = blocks_dev * heads_dev
    lane = lax.broadcasted_iota(jnp.int32, (BLK, BLK), 1)
    stats = lse_ref[...]
    for b in range(blocks_dev):
        for h in range(heads_dev):
            cols = slice(h * HDIM, (h + 1) * HDIM)
            up = up_ref[b * BLK:(b + 1) * BLK, cols].astype(jnp.float32)
            term = jnp.sum(up * o32_ref[b * BLK:(b + 1) * BLK, cols], axis=1, keepdims=True)
            stats = jnp.where(lane == pairs + b * heads_dev + h, term, stats)
    stats_ref[...] = stats
    high = stat_rows(pairs)
    turned = jnp.transpose(stats)[:high, :]
    up_ref[rows:, :] = jnp.zeros((up_ref.shape[0] - rows, columns), jnp.bfloat16)
    pieces = []
    for index in range(3):
        piece = turned.astype(jnp.bfloat16)
        turned = turned - piece.astype(jnp.float32)
        pieces.append(piece)
    spot = lax.broadcasted_iota(jnp.int32, (high, BLK), 1)
    line = lax.broadcasted_iota(jnp.int32, (high, BLK), 0)
    listed = jnp.zeros((high, BLK), jnp.int32)
    for b in range(blocks_dev):
        for n in range(neigh):
            listed = jnp.where(spot == b * neigh + n, keys[b, n], listed)
    listed = jnp.where(line == 0, listed >> 7, listed & 127)
    pieces.append(listed.astype(jnp.float32).astype(jnp.bfloat16))
    for index, piece in enumerate(pieces):
        row = rows + high * (index * BLK // columns)
        col = index * BLK % columns
        up_ref[row:row + high, col:col + BLK] = piece


def query_kernel(size, v_tags, *refs):
    keys_hbm, hosts_hbm, bias_hbm, q_hbm, up_ref, stats_ref = refs[:6]
    k_refs = refs[6:6 + len(PAIR)]
    v_refs = refs[6 + len(PAIR):6 + len(PAIR) + len(v_tags)]
    dq_ref, keys, hosts, bias, q_ref, kcat, vcat, sem = refs[6 + len(PAIR) + len(v_tags):]
    rows, columns = q_ref.shape
    blocks_dev, neigh = keys.shape
    heads_dev = columns // HDIM
    pairs = blocks_dev * heads_dev
    small = start_all([(keys_hbm, keys), (hosts_hbm, hosts), (bias_hbm, bias)], sem)
    large = start_all([(q_hbm, q_ref)], sem, 3)
    wait_all(small)
    places = blocks_dev * neigh
    waits = gather_blocks(size, PAIR, keys, k_refs, kcat, sem, 4, blocks_dev, neigh)
    waits += gather_blocks(size, v_tags, keys, v_refs, vcat, sem, 4 + places, blocks_dev, neigh)
    wait_all(large)
    wait_all(waits)
    span = neigh * BLK
    for b in range(blocks_dev):
        for h in range(heads_dev):
            cols = slice(h * HDIM, (h + 1) * HDIM)
            pair = b * heads_dev + h
            q = q_ref[b * BLK:(b + 1) * BLK, cols]
            up = up_ref[b * BLK:(b + 1) * BLK, cols]
            k = kcat[b * span:(b + 1) * span, cols]
            lse = stats_ref[:, pair:pair + 1]
            term = stats_ref[:, pairs + pair:pairs + pair + 1]
            shift = shift_rows(keys, hosts, bias, b, h, blocks_dev, neigh)
            p = jnp.exp(tdot(q, k) * SCALE + shift - lse)
            dp = tdot(up, vcat[b * span:(b + 1) * span, cols])
            ds = (p * (dp - term) * SCALE).astype(jnp.bfloat16)
            dq_ref[b * BLK:(b + 1) * BLK, cols] = ndot(ds, k).astype(jnp.bfloat16)


def key_kernel(size, neigh, *refs):
    nsh = len(PAIR)
    hosts_hbm, bias_hbm, k_hbm, v_hbm = refs[:4]
    q_refs = refs[4:4 + nsh]
    up_refs = refs[4 + nsh:4 + 2 * nsh]
    dk_ref, dv_ref, mark_ref = refs[4 + 2 * nsh:7 + 2 * nsh]
    (hosts, bias, k_ref, v_ref, qwin, upwin, stats, lists, keys, hits, dk_acc, dv_acc, sem) = refs[
        7 + 2 * nsh:
    ]
    rows, columns = k_ref.shape
    long_rows = up_refs[0].shape[0]
    blocks_dev = rows // BLK
    heads_dev = columns // HDIM
    pairs = blocks_dev * heads_dev
    high = stat_rows(pairs)
    position = lax.axis_index("ctx")
    tail = [
        (ref.at[pl.ds(rows, long_rows - rows)], upwin.at[pl.ds(i * long_rows + rows, long_rows - rows)])
        for i, ref in enumerate(up_refs)
    ]
    first = start_all(tail, sem)
    body = [(ref.at[pl.ds(0, rows)], upwin.at[pl.ds(i * long_rows, rows)]) for i, ref in enumerate(up_refs)]
    body += [(ref, qwin.at[pl.ds(i * rows, rows)]) for i, ref in enumerate(q_refs)]
    body += [(hosts_hbm, hosts), (bias_hbm, bias), (k_hbm, k_ref), (v_hbm, v_ref)]
    later = start_all(body, sem, nsh)
    dk_acc[...] = jnp.zeros_like(dk_acc)
    dv_acc[...] = jnp.zeros_like(dv_acc)
    wait_all(first)

    def part_of(index, piece):
        row = index * long_rows + rows + high * (piece * BLK // columns)
        col = piece * BLK % columns
        return upwin[row:row + high, col:col + BLK].astype(jnp.float32)

    for index in range(nsh):
        stats[index] = (part_of(index, 2) + part_of(index, 1)) + part_of(index, 0)
        listed = part_of(index, 3).astype(jnp.int32)
        lists[index:index + 1, :] = listed[0:1, :] * 128 + listed[1:2, :]
    stats[nsh] = jnp.full((high, BLK), NEVER, jnp.float32)
    copy = pltpu.make_async_copy(lists, keys, sem.at[3 * nsh + 4])
    copy.start()
    copy.wait()

    counts = []
    for own in range(blocks_dev):
        mine = position * blocks_dev + own
        count = 0
        for index in range(nsh):
            for inner in range(blocks_dev):
                hit = keys[index, inner * neigh] == mine
                for n in range(1, neigh):
                    hit = hit | (keys[index, inner * neigh + n] == mine)
                hits[own, count] = index * blocks_dev + inner
                count = count + jnp.where(hit, 1, 0)
        hits[own, count] = -1
        counts.append(count)
    wait_all(later)

    for own in range(blocks_dev):
        mine = position * blocks_dev + own
        krow = slice(own * BLK, (own + 1) * BLK)

        def visit(step, carry, own=own, mine=mine, krow=krow):
            qs, ups, sames, lses, terms = [], [], [], [], []
            for turn in range(2):
                entry = hits[own, 2 * step + turn]
                spare = entry < 0
                entry = jnp.where(spare, 0, entry)
                shard = lax.div(entry, blocks_dev)
                inner = lax.rem(entry, blocks_dev)
                owner = 0
                for index, tag in enumerate(PAIR):
                    owner = owner + jnp.where(shard == index, tag_owner(position, tag, size, PAIR), 0)
                sames.append(hosts[owner * blocks_dev + inner] == hosts[mine])
                qs.append(pl.ds(pl.multiple_of(shard * rows + inner * BLK, BLK), BLK))
                ups.append(pl.ds(pl.multiple_of(shard * long_rows + inner * BLK, 16), BLK))
                lses.append((jnp.where(spare, nsh, shard), inner))
                terms.append((shard, inner))
            for h in range(heads_dev):
                cols = slice(h * HDIM, (h + 1) * HDIM)
                k = k_ref[krow, cols]
                v = v_ref[krow, cols]
                q = jnp.concatenate([qwin[r, cols] for r in qs], axis=0)
                up = jnp.concatenate([upwin[r, cols] for r in ups], axis=0)
                less = jnp.concatenate(
                    [
                        stats[shard, pl.ds(inner * heads_dev + h, 1), :] - jnp.where(same, bias[h], 0.0)
                        for (shard, inner), same in zip(lses, sames)
                    ],
                    axis=1,
                )
                term = jnp.concatenate(
                    [stats[shard, pl.ds(pairs + inner * heads_dev + h, 1), :] for shard, inner in terms],
                    axis=1,
                )
                p = jnp.exp(tdot(k, q) * SCALE - less)
                ds = (p * (tdot(v, up) - term) * SCALE).astype(jnp.bfloat16)
                dk_acc[krow, cols] += ndot(ds, q)
                dv_acc[krow, cols] += ndot(p.astype(jnp.bfloat16), up)
            return carry

        lax.fori_loop(0, lax.div(counts[own] + 1, 2), visit, 0)
    dk_ref[...] = dk_acc[...].astype(jnp.bfloat16)
    dv_ref[...] = dv_acc[...].astype(jnp.bfloat16)
    mark_ref[...] = jnp.zeros_like(mark_ref)


def sum_kernel(count, *refs):
    total = refs[0][...].astype(jnp.float32)
    for ref in refs[1:count]:
        total = total + ref[...].astype(jnp.float32)
    refs[-1][...] = total.astype(jnp.bfloat16)


def sum_after(arrays, before):
    return pl.pallas_call(
        functools.partial(sum_kernel, len(arrays)),
        out_shape=jax.ShapeDtypeStruct(arrays[0].shape, jnp.bfloat16),
        in_specs=[VMEM] * len(arrays) + [ANY],
        out_specs=VMEM,
        compiler_params=params(8),
        cost_estimate=cost(1000, 1000),
        name="sum_after",
    )(*arrays, before)


def copy_kernel(count, extra, *refs):
    sources, targets = refs[:count], refs[count + extra:2 * count + extra]
    between, sem = refs[2 * count + extra:-1], refs[-1]
    wait_all(start_all(list(zip(sources, between)), sem))
    wait_all(start_all(list(zip(between, targets)), sem))


def copies_after(arrays, before):
    return pl.pallas_call(
        functools.partial(copy_kernel, len(arrays), len(before)),
        out_shape=[jax.ShapeDtypeStruct(x.shape, x.dtype) for x in arrays],
        in_specs=[ANY] * (len(arrays) + len(before)),
        out_specs=[ANY] * len(arrays),
        scratch_shapes=[pltpu.VMEM(x.shape, x.dtype) for x in arrays]
        + [pltpu.SemaphoreType.DMA((len(arrays),))],
        compiler_params=params(60),
        cost_estimate=cost(1000, 1000),
        name="copies_after",
    )(*arrays, *before)


def cost(flops, nbytes):
    return pl.CostEstimate(flops=flops, bytes_accessed=nbytes, transcendentals=0)


def per_device(
    query_states, key_states, value_states, out_weight, grad_mixed, key_blocks, host_ids, host_bias
):
    size = lax.axis_size("ctx")
    rows, columns = query_states.shape
    width = out_weight.shape[1]
    blocks_dev, neigh = key_blocks.shape
    heads_dev = columns // HDIM
    pairs = blocks_dev * heads_dev
    places = blocks_dev * neigh
    groups = lax.axis_size("head")
    part = rows // groups
    v_tags = CUBE if size == 8 else PAIR
    nsh = len(PAIR)
    bf16, f32, i32 = jnp.bfloat16, jnp.float32, jnp.int32
    high = stat_rows(pairs)
    extra = high * (-(-4 * BLK // columns))
    long_rows = rows + extra

    def ring(x, step):
        return lax.ppermute(x, "head", [(i, (i + step) % groups) for i in range(groups)])

    def flip(x, mask):
        return lax.ppermute(x, "head", [(i, i ^ mask) for i in range(groups)])

    paired = groups == 4
    v_win = exchange_cube(value_states, size) if v_tags is CUBE else exchange_pair(value_states, size)
    k_win = exchange_pair(key_states, size)
    if paired:
        opposite = flip(grad_mixed, 2)
        beside = flip(grad_mixed, 1)
        pieces = [grad_mixed, beside, opposite, flip(opposite, 1)]
    else:
        pieces = [grad_mixed] + [ring(grad_mixed, step) for step in range(1, groups)]
    (late_query,) = copies_after((query_states,), (pieces[1], pieces[2]))
    q_win = exchange_pair(late_query, size)
    scalars = [
        pltpu.SMEM(key_blocks.shape, i32),
        pltpu.SMEM(host_ids.shape, i32),
        pltpu.SMEM(host_bias.shape, f32),
    ]

    parts_o32_lse = pl.pallas_call(
        functools.partial(attend_kernel, size, groups, v_tags),
        out_shape=[jax.ShapeDtypeStruct((part, width), bf16)] * groups
        + [jax.ShapeDtypeStruct((rows, columns), f32), jax.ShapeDtypeStruct((BLK, BLK), f32)],
        in_specs=[HBM] * 5 + [ANY] * (len(PAIR) + len(v_tags)),
        out_specs=[VMEM] * (groups + 2),
        scratch_shapes=scalars
        + [
            pltpu.VMEM((rows, columns), bf16),
            pltpu.VMEM((columns, width), bf16),
            pltpu.VMEM((places * BLK, columns), bf16),
            pltpu.VMEM((places * BLK, columns), bf16),
            pltpu.VMEM((pairs, BLK, neigh * BLK), f32),
            pltpu.VMEM((rows, columns), bf16),
            pltpu.VMEM((rows, columns), bf16),
            pltpu.SemaphoreType.DMA((5 + 2 * places,)),
        ],
        compiler_params=params(60),
        cost_estimate=cost(10**9, 10**6),
        name="attend",
    )(key_blocks, host_ids, host_bias, query_states, out_weight, *k_win, *v_win)
    parts = parts_o32_lse[:groups]
    o32, lse = parts_o32_lse[groups:]
    mixed = parts[0].astype(f32)
    if paired:
        relay = flip(parts[3], 1)
        beside_sum = flip(parts[1], 1)
        passed = (parts[2].astype(f32) + relay.astype(f32)).astype(bf16)
        arrived = [beside_sum, flip(passed, 2)]
    else:
        arrived = [ring(parts[step], step) for step in range(1, groups)]

    up, stats = pl.pallas_call(
        functools.partial(upstream_kernel, groups),
        out_shape=[
            jax.ShapeDtypeStruct((long_rows, columns), bf16),
            jax.ShapeDtypeStruct((BLK, BLK), f32),
        ],
        in_specs=[HBM] * 3 + [ANY] * (groups + 2),
        out_specs=[VMEM] * 2,
        scratch_shapes=[
            pltpu.SMEM(key_blocks.shape, i32),
            pltpu.VMEM((columns, width), bf16),
            pltpu.VMEM((rows, width), bf16),
            pltpu.VMEM((rows, columns), f32),
            pltpu.VMEM((BLK, BLK), f32),
            pltpu.SemaphoreType.DMA((5 + groups,)),
        ],
        compiler_params=params(60),
        cost_estimate=cost(1000, 1000),
        name="upstream",
    )(key_blocks, out_weight, grad_mixed, o32, lse, *pieces[1:], q_win[1])
    up_win = exchange_pair(up, size)

    grad_query = pl.pallas_call(
        functools.partial(query_kernel, size, v_tags),
        out_shape=jax.ShapeDtypeStruct((rows, columns), bf16),
        in_specs=[HBM] * 4 + [VMEM] * 2 + [ANY] * (len(PAIR) + len(v_tags)),
        out_specs=VMEM,
        scratch_shapes=scalars
        + [
            pltpu.VMEM((rows, columns), bf16),
            pltpu.VMEM((places * BLK, columns), bf16),
            pltpu.VMEM((places * BLK, columns), bf16),
            pltpu.SemaphoreType.DMA((4 + 2 * places,)),
        ],
        compiler_params=params(60),
        cost_estimate=cost(16 * 10**9, 32 * 10**6),
        name="query_grad",
    )(key_blocks, host_ids, host_bias, query_states, up, stats, *k_win, *v_win)

    grad_key, grad_value, mark = pl.pallas_call(
        functools.partial(key_kernel, size, neigh),
        out_shape=[jax.ShapeDtypeStruct((rows, columns), bf16)] * 2
        + [jax.ShapeDtypeStruct((8, BLK), f32)],
        in_specs=[HBM] * 5 + [ANY] * (2 * nsh - 1),
        out_specs=[VMEM] * 3,
        scratch_shapes=[
            pltpu.SMEM(host_ids.shape, i32),
            pltpu.SMEM(host_bias.shape, f32),
            pltpu.VMEM((rows, columns), bf16),
            pltpu.VMEM((rows, columns), bf16),
            pltpu.VMEM((nsh * rows, columns), bf16),
            pltpu.VMEM((nsh * long_rows, columns), bf16),
            pltpu.VMEM((nsh + 1, high, BLK), f32),
            pltpu.VMEM((8, BLK), i32),
            pltpu.SMEM((8, BLK), i32),
            pltpu.SMEM((blocks_dev, nsh * blocks_dev + 2), i32),
            pltpu.VMEM((rows, columns), f32),
            pltpu.VMEM((rows, columns), f32),
            pltpu.SemaphoreType.DMA((3 * nsh + 5,)),
        ],
        compiler_params=params(20),
        cost_estimate=cost(1000, 1000),
        name="key_grad",
    )(host_ids, host_bias, key_states, value_states, query_states, *q_win[1:], *up_win)

    mixed_out = sum_after((parts[0], *arrived), mark)
    return (mixed_out, grad_query, grad_key, grad_value)


def solution(mesh):
    in_specs = (
        P("ctx", "head"),
        P("ctx", "head"),
        P("ctx", "head"),
        P("head", None),
        P(("ctx", "head"), None),
        P("ctx", None),
        P(),
        P("head"),
    )
    out_specs = (P(("ctx", "head"), None), P("ctx", "head"), P("ctx", "head"), P("ctx", "head"))
    return jax.shard_map(
        per_device, mesh=mesh, in_specs=in_specs, out_specs=out_specs, check_vma=False
    )
```

```python
import functools

import jax
import jax.numpy as jnp
from jax import lax
from jax.experimental import pallas as pl
from jax.experimental.pallas import tpu as pltpu
from jax.sharding import PartitionSpec as P

HDIM = 128
BLK = 128
HOPS = 2
SCALE = HDIM ** (-0.5)
CUBE = (0, 1, 2, 3, 6, 7)
PAIR = (0, 1, 2, -2, -1)
NT = (((1,), (1,)), ((), ()))
VMEM = pl.BlockSpec(memory_space=pltpu.VMEM)
SMEM = pl.BlockSpec(memory_space=pltpu.SMEM)
ANY = pl.BlockSpec(memory_space=pl.ANY)
HBM = pl.BlockSpec(memory_space=pltpu.HBM)
NEVER = 1e30


def params(mebibytes):
    return pltpu.CompilerParams(vmem_limit_bytes=mebibytes * 1024 * 1024)


def ndot(a, b):
    return lax.dot_general(a, b, (((1,), (0,)), ((), ())), preferred_element_type=jnp.float32)


def tdot(a, b):
    return lax.dot_general(a, b, NT, preferred_element_type=jnp.float32)


def stat_rows(pairs):
    return -(-2 * pairs // 16) * 16


def tag_owner(position, tag, size, tags):
    if tags is CUBE:
        return position ^ tag
    return lax.rem(position + jnp.where(position % 2 == 0, tag, -tag) + size, size)


def find_shard(position, owner, size, tags):
    shard = 0
    for index, tag in enumerate(tags):
        shard = shard + jnp.where(tag_owner(position, tag, size, tags) == owner, index, 0)
    return shard


def permute_from(x, size, source):
    return lax.ppermute(x, "ctx", [(source(i) % size, i) for i in range(size)])


def exchange_pair(x, size):
    sign = lambda i: 1 if i % 2 == 0 else -1
    share = permute_from(x, size, lambda i: i + 2 * sign(i))
    solo = permute_from(x, size, lambda i: i - 2 * sign(i))
    mate = permute_from(x, size, lambda i: i ^ 1)
    return [x, mate, share, solo, permute_from(share, size, lambda i: i ^ 1)]


def exchange_cube(x, size):
    near = permute_from(x, size, lambda i: i ^ 2)
    far = permute_from(near, size, lambda i: i ^ 4)
    mate = permute_from(x, size, lambda i: i ^ 1)
    swap = lambda i: i ^ 1
    return [x, mate, near, permute_from(near, size, swap), far, permute_from(far, size, swap)]


def start_all(pairs, sem, first=0):
    copies = []
    for index, (source, target) in enumerate(pairs):
        copy = pltpu.make_async_copy(source, target, sem.at[first + index])
        copy.start()
        copies.append(copy)
    return copies


def wait_all(copies):
    for copy in copies:
        copy.wait()


def gather_blocks(size, tags, keys, refs, target, sem, first, blocks_dev, neigh):
    position = lax.axis_index("ctx")
    waits = []
    for b in range(blocks_dev):
        for n in range(neigh):
            j = keys[b, n]
            shard = find_shard(position, lax.div(j, blocks_dev), size, tags)
            row = pl.multiple_of(lax.rem(j, blocks_dev) * BLK, BLK)
            place = b * neigh + n
            for index, ref in enumerate(refs):

                @pl.when(shard == index)
                def _(ref=ref, place=place, row=row):
                    pltpu.make_async_copy(
                        ref.at[pl.ds(row, BLK)], target.at[pl.ds(place * BLK, BLK)], sem.at[first + place]
                    ).start()

            waits.append(
                pltpu.make_async_copy(
                    refs[0].at[pl.ds(0, BLK)], target.at[pl.ds(place * BLK, BLK)], sem.at[first + place]
                )
            )
    return waits


def shift_rows(keys, hosts, bias, b, h, blocks_dev, neigh):
    position = lax.axis_index("ctx")
    slot = lax.broadcasted_iota(jnp.int32, (1, neigh * BLK), 1) // BLK
    shift = jnp.zeros((1, neigh * BLK), jnp.float32)
    host = hosts[position * blocks_dev + b]
    for n in range(neigh):
        value = jnp.where(hosts[keys[b, n]] == host, bias[h], 0.0)
        shift = jnp.where(slot == n, value, shift)
    return shift


def piece_owner(me, step, groups, sign):
    return me ^ step if groups == 4 else lax.rem(me + sign * step + groups, groups)


def attend_kernel(size, groups, v_tags, *refs):
    keys_hbm, hosts_hbm, bias_hbm, q_hbm, w_hbm = refs[:5]
    k_refs = refs[5:5 + len(PAIR)]
    v_refs = refs[5 + len(PAIR):5 + len(PAIR) + len(v_tags)]
    rest = refs[5 + len(PAIR) + len(v_tags):]
    part_refs = rest[:groups]
    o32_ref, lse_ref = rest[groups:groups + 2]
    keys, hosts, bias, q_ref, w_ref, kcat, vcat, score, att, turned, sem = rest[groups + 2:]
    rows, columns = q_ref.shape
    blocks_dev, neigh = keys.shape
    heads_dev = columns // HDIM
    small = start_all([(keys_hbm, keys), (hosts_hbm, hosts), (bias_hbm, bias)], sem)
    large = start_all([(q_hbm, q_ref), (w_hbm, w_ref)], sem, 3)
    wait_all(small)
    places = blocks_dev * neigh
    k_waits = gather_blocks(size, PAIR, keys, k_refs, kcat, sem, 5, blocks_dev, neigh)
    v_waits = gather_blocks(size, v_tags, keys, v_refs, vcat, sem, 5 + places, blocks_dev, neigh)
    large[0].wait()
    wait_all(k_waits)
    span = neigh * BLK
    units = [(b, h) for b in range(blocks_dev) for h in range(heads_dev)]
    for b, h in units:
        cols = slice(h * HDIM, (h + 1) * HDIM)
        s = tdot(q_ref[b * BLK:(b + 1) * BLK, cols], kcat[b * span:(b + 1) * span, cols])
        score[b * heads_dev + h] = s * SCALE + shift_rows(keys, hosts, bias, b, h, blocks_dev, neigh)
    wait_all(v_waits)
    lane = lax.broadcasted_iota(jnp.int32, (BLK, BLK), 1)
    lse_all = jnp.zeros((BLK, BLK), jnp.float32)
    for b, h in units:
        cols = slice(h * HDIM, (h + 1) * HDIM)
        s = score[b * heads_dev + h]
        top = jnp.max(s, axis=1, keepdims=True)
        weights = jnp.exp(s - top)
        total = jnp.sum(weights, axis=1, keepdims=True)
        probs = (weights * (1.0 / total)).astype(jnp.bfloat16)
        out = ndot(probs, vcat[b * span:(b + 1) * span, cols])
        o32_ref[b * BLK:(b + 1) * BLK, cols] = out
        att[b * BLK:(b + 1) * BLK, cols] = out.astype(jnp.bfloat16)
        lse_all = jnp.where(lane == b * heads_dev + h, top + jnp.log(total), lse_all)
    lse_ref[...] = lse_all
    large[1].wait()
    me = lax.axis_index("head")
    part = rows // groups
    for step in range(groups):
        owner = piece_owner(me, step, groups, 1)
        turned[step * part:(step + 1) * part, :] = att[pl.ds(pl.multiple_of(owner * part, part), part), :]
    mixed = ndot(turned[...], w_ref[...]).astype(jnp.bfloat16)
    for step in range(groups):
        part_refs[step][...] = mixed[step * part:(step + 1) * part, :]


def upstream_kernel(groups, *refs):
    keys_hbm, w_hbm, own_hbm, o32_any, lse_any = refs[:5]
    piece_refs = refs[5:4 + groups]
    rest = refs[4 + groups + 1:]
    up_ref, stats_ref, keys, w_ref, grads, o32_ref, lse_ref, sem = rest
    rows, columns = o32_ref.shape
    blocks_dev, neigh = keys.shape
    heads_dev = columns // HDIM
    part = rows // groups
    cut = columns // 2
    waits = [
        start_all([(w_hbm.at[c * cut:(c + 1) * cut], w_ref.at[c * cut:(c + 1) * cut])], sem, c)[0]
        for c in range(2)
    ]
    pieces = (own_hbm,) + tuple(piece_refs)
    early = start_all(
        [(ref, grads.at[pl.ds(step * part, part)]) for step, ref in enumerate(pieces)]
        + [(keys_hbm, keys)],
        sem,
        2,
    )
    late = start_all([(o32_any, o32_ref), (lse_any, lse_ref)], sem, 3 + groups)
    wait_all(early)
    me = lax.axis_index("head")
    for c in range(2):
        waits[c].wait()
        product = tdot(grads[...], w_ref[c * cut:(c + 1) * cut, :]).astype(jnp.bfloat16)
        for step in range(groups):
            owner = piece_owner(me, step, groups, -1)
            up_ref[pl.ds(pl.multiple_of(owner * part, part), part), c * cut:(c + 1) * cut] = product[
                step * part:(step + 1) * part, :
            ]
    wait_all(late)
    pairs = blocks_dev * heads_dev
    lane = lax.broadcasted_iota(jnp.int32, (BLK, BLK), 1)
    stats = lse_ref[...]
    for b in range(blocks_dev):
        for h in range(heads_dev):
            cols = slice(h * HDIM, (h + 1) * HDIM)
            up = up_ref[b * BLK:(b + 1) * BLK, cols].astype(jnp.float32)
            term = jnp.sum(up * o32_ref[b * BLK:(b + 1) * BLK, cols], axis=1, keepdims=True)
            stats = jnp.where(lane == pairs + b * heads_dev + h, term, stats)
    stats_ref[...] = stats
    high = stat_rows(pairs)
    turned = jnp.transpose(stats)[:high, :]
    up_ref[rows:, :] = jnp.zeros((up_ref.shape[0] - rows, columns), jnp.bfloat16)
    pieces = []
    for index in range(3):
        piece = turned.astype(jnp.bfloat16)
        turned = turned - piece.astype(jnp.float32)
        pieces.append(piece)
    spot = lax.broadcasted_iota(jnp.int32, (high, BLK), 1)
    line = lax.broadcasted_iota(jnp.int32, (high, BLK), 0)
    listed = jnp.zeros((high, BLK), jnp.int32)
    for b in range(blocks_dev):
        for n in range(neigh):
            listed = jnp.where(spot == b * neigh + n, keys[b, n], listed)
    listed = jnp.where(line == 0, listed >> 7, listed & 127)
    pieces.append(listed.astype(jnp.float32).astype(jnp.bfloat16))
    for index, piece in enumerate(pieces):
        row = rows + high * (index * BLK // columns)
        col = index * BLK % columns
        up_ref[row:row + high, col:col + BLK] = piece


def query_kernel(size, v_tags, *refs):
    keys_hbm, hosts_hbm, bias_hbm, q_hbm, up_any, stats_any = refs[:6]
    k_refs = refs[6:6 + len(PAIR)]
    v_refs = refs[6 + len(PAIR):6 + len(PAIR) + len(v_tags)]
    (dq_ref, keys, hosts, bias, q_ref, up_ref, stats_ref, kcat, vcat, sem) = refs[
        6 + len(PAIR) + len(v_tags):
    ]
    rows, columns = q_ref.shape
    blocks_dev, neigh = keys.shape
    heads_dev = columns // HDIM
    pairs = blocks_dev * heads_dev
    small = start_all([(keys_hbm, keys), (hosts_hbm, hosts), (bias_hbm, bias)], sem)
    places = blocks_dev * neigh
    large = start_all([(q_hbm, q_ref)], sem, 3)
    large += start_all([(up_any.at[pl.ds(0, rows)], up_ref), (stats_any, stats_ref)], sem, 4 + 2 * places)
    wait_all(small)
    waits = gather_blocks(size, PAIR, keys, k_refs, kcat, sem, 4, blocks_dev, neigh)
    waits += gather_blocks(size, v_tags, keys, v_refs, vcat, sem, 4 + places, blocks_dev, neigh)
    wait_all(large)
    wait_all(waits)
    span = neigh * BLK
    for b in range(blocks_dev):
        for h in range(heads_dev):
            cols = slice(h * HDIM, (h + 1) * HDIM)
            pair = b * heads_dev + h
            q = q_ref[b * BLK:(b + 1) * BLK, cols]
            up = up_ref[b * BLK:(b + 1) * BLK, cols]
            k = kcat[b * span:(b + 1) * span, cols]
            lse = stats_ref[:, pair:pair + 1]
            term = stats_ref[:, pairs + pair:pairs + pair + 1]
            shift = shift_rows(keys, hosts, bias, b, h, blocks_dev, neigh)
            p = jnp.exp(tdot(q, k) * SCALE + shift - lse)
            dp = tdot(up, vcat[b * span:(b + 1) * span, cols])
            ds = (p * (dp - term) * SCALE).astype(jnp.bfloat16)
            dq_ref[b * BLK:(b + 1) * BLK, cols] = ndot(ds, k).astype(jnp.bfloat16)


def key_kernel(size, neigh, *refs):
    nsh = len(PAIR)
    hosts_hbm, bias_hbm, k_hbm, v_hbm = refs[:4]
    q_refs = refs[4:4 + nsh]
    up_refs = refs[4 + nsh:4 + 2 * nsh]
    dk_ref, dv_ref, mark_ref = refs[4 + 2 * nsh:7 + 2 * nsh]
    (hosts, bias, k_ref, v_ref, qwin, upwin, stats, lists, keys, hits, dk_acc, dv_acc, sem) = refs[
        7 + 2 * nsh:
    ]
    rows, columns = k_ref.shape
    long_rows = up_refs[0].shape[0]
    blocks_dev = rows // BLK
    heads_dev = columns // HDIM
    pairs = blocks_dev * heads_dev
    high = stat_rows(pairs)
    position = lax.axis_index("ctx")
    tail = [
        (ref.at[pl.ds(rows, long_rows - rows)], upwin.at[pl.ds(i * long_rows + rows, long_rows - rows)])
        for i, ref in enumerate(up_refs)
    ]
    first = start_all(tail, sem)
    body = [(ref.at[pl.ds(0, rows)], upwin.at[pl.ds(i * long_rows, rows)]) for i, ref in enumerate(up_refs)]
    body += [(ref, qwin.at[pl.ds(i * rows, rows)]) for i, ref in enumerate(q_refs)]
    body += [(hosts_hbm, hosts), (bias_hbm, bias), (k_hbm, k_ref), (v_hbm, v_ref)]
    later = start_all(body, sem, nsh)
    dk_acc[...] = jnp.zeros_like(dk_acc)
    dv_acc[...] = jnp.zeros_like(dv_acc)
    wait_all(first)

    def part_of(index, piece):
        row = index * long_rows + rows + high * (piece * BLK // columns)
        col = piece * BLK % columns
        return upwin[row:row + high, col:col + BLK].astype(jnp.float32)

    for index in range(nsh):
        stats[index] = (part_of(index, 2) + part_of(index, 1)) + part_of(index, 0)
        listed = part_of(index, 3).astype(jnp.int32)
        lists[index:index + 1, :] = listed[0:1, :] * 128 + listed[1:2, :]
    stats[nsh] = jnp.full((high, BLK), NEVER, jnp.float32)
    copy = pltpu.make_async_copy(lists, keys, sem.at[3 * nsh + 4])
    copy.start()
    copy.wait()

    counts = []
    for own in range(blocks_dev):
        mine = position * blocks_dev + own
        count = 0
        for index in range(nsh):
            for inner in range(blocks_dev):
                hit = keys[index, inner * neigh] == mine
                for n in range(1, neigh):
                    hit = hit | (keys[index, inner * neigh + n] == mine)
                hits[own, count] = index * blocks_dev + inner
                count = count + jnp.where(hit, 1, 0)
        hits[own, count] = -1
        counts.append(count)
    wait_all(later)

    for own in range(blocks_dev):
        mine = position * blocks_dev + own
        krow = slice(own * BLK, (own + 1) * BLK)

        def visit(step, carry, own=own, mine=mine, krow=krow):
            qs, ups, sames, lses, terms = [], [], [], [], []
            for turn in range(2):
                entry = hits[own, 2 * step + turn]
                spare = entry < 0
                entry = jnp.where(spare, 0, entry)
                shard = lax.div(entry, blocks_dev)
                inner = lax.rem(entry, blocks_dev)
                owner = 0
                for index, tag in enumerate(PAIR):
                    owner = owner + jnp.where(shard == index, tag_owner(position, tag, size, PAIR), 0)
                sames.append(hosts[owner * blocks_dev + inner] == hosts[mine])
                qs.append(pl.ds(pl.multiple_of(shard * rows + inner * BLK, BLK), BLK))
                ups.append(pl.ds(pl.multiple_of(shard * long_rows + inner * BLK, 16), BLK))
                lses.append((jnp.where(spare, nsh, shard), inner))
                terms.append((shard, inner))
            for h in range(heads_dev):
                cols = slice(h * HDIM, (h + 1) * HDIM)
                k = k_ref[krow, cols]
                v = v_ref[krow, cols]
                q = jnp.concatenate([qwin[r, cols] for r in qs], axis=0)
                up = jnp.concatenate([upwin[r, cols] for r in ups], axis=0)
                less = jnp.concatenate(
                    [
                        stats[shard, pl.ds(inner * heads_dev + h, 1), :] - jnp.where(same, bias[h], 0.0)
                        for (shard, inner), same in zip(lses, sames)
                    ],
                    axis=1,
                )
                term = jnp.concatenate(
                    [stats[shard, pl.ds(pairs + inner * heads_dev + h, 1), :] for shard, inner in terms],
                    axis=1,
                )
                p = jnp.exp(tdot(k, q) * SCALE - less)
                ds = (p * (tdot(v, up) - term) * SCALE).astype(jnp.bfloat16)
                dk_acc[krow, cols] += ndot(ds, q)
                dv_acc[krow, cols] += ndot(p.astype(jnp.bfloat16), up)
            return carry

        lax.fori_loop(0, lax.div(counts[own] + 1, 2), visit, 0)
    dk_ref[...] = dk_acc[...].astype(jnp.bfloat16)
    dv_ref[...] = dv_acc[...].astype(jnp.bfloat16)
    mark_ref[...] = jnp.zeros_like(mark_ref)


def sum_kernel(count, *refs):
    total = refs[0][...].astype(jnp.float32)
    for ref in refs[1:count]:
        total = total + ref[...].astype(jnp.float32)
    refs[-1][...] = total.astype(jnp.bfloat16)


def sum_after(arrays, before):
    return pl.pallas_call(
        functools.partial(sum_kernel, len(arrays)),
        out_shape=jax.ShapeDtypeStruct(arrays[0].shape, jnp.bfloat16),
        in_specs=[VMEM] * len(arrays) + [ANY],
        out_specs=VMEM,
        compiler_params=params(8),
        cost_estimate=cost(1000, 1000),
        name="sum_after",
    )(*arrays, before)


def copy_kernel(count, extra, *refs):
    sources, targets = refs[:count], refs[count + extra:2 * count + extra]
    between, sem = refs[2 * count + extra:-1], refs[-1]
    wait_all(start_all(list(zip(sources, between)), sem))
    wait_all(start_all(list(zip(between, targets)), sem))


def copies_after(arrays, before):
    return pl.pallas_call(
        functools.partial(copy_kernel, len(arrays), len(before)),
        out_shape=[jax.ShapeDtypeStruct(x.shape, x.dtype) for x in arrays],
        in_specs=[ANY] * (len(arrays) + len(before)),
        out_specs=[ANY] * len(arrays),
        scratch_shapes=[pltpu.VMEM(x.shape, x.dtype) for x in arrays]
        + [pltpu.SemaphoreType.DMA((len(arrays),))],
        compiler_params=params(60),
        cost_estimate=cost(1000, 1000),
        name="copies_after",
    )(*arrays, *before)


def cost(flops, nbytes):
    return pl.CostEstimate(flops=flops, bytes_accessed=nbytes, transcendentals=0)


def per_device(
    query_states, key_states, value_states, out_weight, grad_mixed, key_blocks, host_ids, host_bias
):
    size = lax.axis_size("ctx")
    rows, columns = query_states.shape
    width = out_weight.shape[1]
    blocks_dev, neigh = key_blocks.shape
    heads_dev = columns // HDIM
    pairs = blocks_dev * heads_dev
    places = blocks_dev * neigh
    groups = lax.axis_size("head")
    part = rows // groups
    v_tags = CUBE if size == 8 else PAIR
    nsh = len(PAIR)
    bf16, f32, i32 = jnp.bfloat16, jnp.float32, jnp.int32
    high = stat_rows(pairs)
    extra = high * (-(-4 * BLK // columns))
    long_rows = rows + extra

    def ring(x, step):
        return lax.ppermute(x, "head", [(i, (i + step) % groups) for i in range(groups)])

    def flip(x, mask):
        return lax.ppermute(x, "head", [(i, i ^ mask) for i in range(groups)])

    paired = groups == 4
    v_win = exchange_cube(value_states, size) if v_tags is CUBE else exchange_pair(value_states, size)
    k_win = exchange_pair(key_states, size)
    if paired:
        opposite = flip(grad_mixed, 2)
        beside = flip(grad_mixed, 1)
        pieces = [grad_mixed, beside, opposite, flip(opposite, 1)]
    else:
        pieces = [grad_mixed] + [ring(grad_mixed, step) for step in range(1, groups)]
    (late_query,) = copies_after((query_states,), (pieces[1], pieces[2]))
    q_win = exchange_pair(late_query, size)
    scalars = [
        pltpu.SMEM(key_blocks.shape, i32),
        pltpu.SMEM(host_ids.shape, i32),
        pltpu.SMEM(host_bias.shape, f32),
    ]

    parts_o32_lse = pl.pallas_call(
        functools.partial(attend_kernel, size, groups, v_tags),
        out_shape=[jax.ShapeDtypeStruct((part, width), bf16)] * groups
        + [jax.ShapeDtypeStruct((rows, columns), f32), jax.ShapeDtypeStruct((BLK, BLK), f32)],
        in_specs=[HBM] * 5 + [ANY] * (len(PAIR) + len(v_tags)),
        out_specs=[VMEM] * (groups + 2),
        scratch_shapes=scalars
        + [
            pltpu.VMEM((rows, columns), bf16),
            pltpu.VMEM((columns, width), bf16),
            pltpu.VMEM((places * BLK, columns), bf16),
            pltpu.VMEM((places * BLK, columns), bf16),
            pltpu.VMEM((pairs, BLK, neigh * BLK), f32),
            pltpu.VMEM((rows, columns), bf16),
            pltpu.VMEM((rows, columns), bf16),
            pltpu.SemaphoreType.DMA((5 + 2 * places,)),
        ],
        compiler_params=params(60),
        cost_estimate=cost(10**9, 10**6),
        name="attend",
    )(key_blocks, host_ids, host_bias, query_states, out_weight, *k_win, *v_win)
    parts = parts_o32_lse[:groups]
    o32, lse = parts_o32_lse[groups:]
    mixed = parts[0].astype(f32)
    if paired:
        relay = flip(parts[3], 1)
        beside_sum = flip(parts[1], 1)
        passed = (parts[2].astype(f32) + relay.astype(f32)).astype(bf16)
        arrived = [beside_sum, flip(passed, 2)]
    else:
        arrived = [ring(parts[step], step) for step in range(1, groups)]

    up, stats = pl.pallas_call(
        functools.partial(upstream_kernel, groups),
        out_shape=[
            jax.ShapeDtypeStruct((long_rows, columns), bf16),
            jax.ShapeDtypeStruct((BLK, BLK), f32),
        ],
        in_specs=[HBM] * 3 + [ANY] * (groups + 2),
        out_specs=[VMEM] * 2,
        scratch_shapes=[
            pltpu.SMEM(key_blocks.shape, i32),
            pltpu.VMEM((columns, width), bf16),
            pltpu.VMEM((rows, width), bf16),
            pltpu.VMEM((rows, columns), f32),
            pltpu.VMEM((BLK, BLK), f32),
            pltpu.SemaphoreType.DMA((5 + groups,)),
        ],
        compiler_params=params(60),
        cost_estimate=cost(1000, 1000),
        name="upstream",
    )(key_blocks, out_weight, grad_mixed, o32, lse, *pieces[1:], q_win[1])
    up_win = exchange_pair(up, size)

    grad_query = pl.pallas_call(
        functools.partial(query_kernel, size, v_tags),
        out_shape=jax.ShapeDtypeStruct((rows, columns), bf16),
        in_specs=[HBM] * 4 + [ANY] * (2 + len(PAIR) + len(v_tags)),
        out_specs=VMEM,
        scratch_shapes=scalars
        + [
            pltpu.VMEM((rows, columns), bf16),
            pltpu.VMEM((rows, columns), bf16),
            pltpu.VMEM((BLK, BLK), f32),
            pltpu.VMEM((places * BLK, columns), bf16),
            pltpu.VMEM((places * BLK, columns), bf16),
            pltpu.SemaphoreType.DMA((6 + 2 * places,)),
        ],
        compiler_params=params(60),
        cost_estimate=cost(16 * 10**9, 32 * 10**6),
        name="query_grad",
    )(key_blocks, host_ids, host_bias, query_states, up, stats, *k_win, *v_win)

    grad_key, grad_value, mark = pl.pallas_call(
        functools.partial(key_kernel, size, neigh),
        out_shape=[jax.ShapeDtypeStruct((rows, columns), bf16)] * 2
        + [jax.ShapeDtypeStruct((8, BLK), f32)],
        in_specs=[HBM] * 5 + [ANY] * (2 * nsh - 1),
        out_specs=[VMEM] * 3,
        scratch_shapes=[
            pltpu.SMEM(host_ids.shape, i32),
            pltpu.SMEM(host_bias.shape, f32),
            pltpu.VMEM((rows, columns), bf16),
            pltpu.VMEM((rows, columns), bf16),
            pltpu.VMEM((nsh * rows, columns), bf16),
            pltpu.VMEM((nsh * long_rows, columns), bf16),
            pltpu.VMEM((nsh + 1, high, BLK), f32),
            pltpu.VMEM((8, BLK), i32),
            pltpu.SMEM((8, BLK), i32),
            pltpu.SMEM((blocks_dev, nsh * blocks_dev + 2), i32),
            pltpu.VMEM((rows, columns), f32),
            pltpu.VMEM((rows, columns), f32),
            pltpu.SemaphoreType.DMA((3 * nsh + 5,)),
        ],
        compiler_params=params(20),
        cost_estimate=cost(1000, 1000),
        name="key_grad",
    )(host_ids, host_bias, key_states, value_states, query_states, *q_win[1:], *up_win)

    mixed_out = sum_after((parts[0], *arrived), mark)
    return (mixed_out, grad_query, grad_key, grad_value)


def solution(mesh):
    in_specs = (
        P("ctx", "head"),
        P("ctx", "head"),
        P("ctx", "head"),
        P("head", None),
        P(("ctx", "head"), None),
        P("ctx", None),
        P(),
        P("head"),
    )
    out_specs = (P(("ctx", "head"), None), P("ctx", "head"), P("ctx", "head"), P("ctx", "head"))
    return jax.shard_map(
        per_device, mesh=mesh, in_specs=in_specs, out_specs=out_specs, check_vma=False
    )
```

```python
import functools

import jax
import jax.numpy as jnp
from jax import lax
from jax.experimental import pallas as pl
from jax.experimental.pallas import tpu as pltpu
from jax.sharding import PartitionSpec as P

HDIM = 128
BLK = 128
HOPS = 2
SCALE = HDIM ** (-0.5)
CUBE = (0, 1, 2, 3, 6, 7)
PAIR = (0, 1, 2, -2, -1)
NT = (((1,), (1,)), ((), ()))
VMEM = pl.BlockSpec(memory_space=pltpu.VMEM)
SMEM = pl.BlockSpec(memory_space=pltpu.SMEM)
ANY = pl.BlockSpec(memory_space=pl.ANY)
HBM = pl.BlockSpec(memory_space=pltpu.HBM)
NEVER = 1e30


def params(mebibytes):
    return pltpu.CompilerParams(vmem_limit_bytes=mebibytes * 1024 * 1024)


def ndot(a, b):
    return lax.dot_general(a, b, (((1,), (0,)), ((), ())), preferred_element_type=jnp.float32)


def tdot(a, b):
    return lax.dot_general(a, b, NT, preferred_element_type=jnp.float32)


def stat_rows(pairs):
    return -(-2 * pairs // 16) * 16


def tag_owner(position, tag, size, tags):
    if tags is CUBE:
        return position ^ tag
    return lax.rem(position + jnp.where(position % 2 == 0, tag, -tag) + size, size)


def find_shard(position, owner, size, tags):
    shard = 0
    for index, tag in enumerate(tags):
        shard = shard + jnp.where(tag_owner(position, tag, size, tags) == owner, index, 0)
    return shard


def permute_from(x, size, source):
    return lax.ppermute(x, "ctx", [(source(i) % size, i) for i in range(size)])


def exchange_pair(x, size):
    sign = lambda i: 1 if i % 2 == 0 else -1
    share = permute_from(x, size, lambda i: i + 2 * sign(i))
    solo = permute_from(x, size, lambda i: i - 2 * sign(i))
    mate = permute_from(x, size, lambda i: i ^ 1)
    return [x, mate, share, solo, permute_from(share, size, lambda i: i ^ 1)]


def exchange_cube(x, size):
    near = permute_from(x, size, lambda i: i ^ 2)
    far = permute_from(near, size, lambda i: i ^ 4)
    mate = permute_from(x, size, lambda i: i ^ 1)
    swap = lambda i: i ^ 1
    return [x, mate, near, permute_from(near, size, swap), far, permute_from(far, size, swap)]


def start_all(pairs, sem, first=0):
    copies = []
    for index, (source, target) in enumerate(pairs):
        copy = pltpu.make_async_copy(source, target, sem.at[first + index])
        copy.start()
        copies.append(copy)
    return copies


def wait_all(copies):
    for copy in copies:
        copy.wait()


def gather_blocks(size, tags, keys, refs, target, sem, first, blocks_dev, neigh):
    position = lax.axis_index("ctx")
    waits = []
    for b in range(blocks_dev):
        for n in range(neigh):
            j = keys[b, n]
            shard = find_shard(position, lax.div(j, blocks_dev), size, tags)
            row = pl.multiple_of(lax.rem(j, blocks_dev) * BLK, BLK)
            place = b * neigh + n
            for index, ref in enumerate(refs):

                @pl.when(shard == index)
                def _(ref=ref, place=place, row=row):
                    pltpu.make_async_copy(
                        ref.at[pl.ds(row, BLK)], target.at[pl.ds(place * BLK, BLK)], sem.at[first + place]
                    ).start()

            waits.append(
                pltpu.make_async_copy(
                    refs[0].at[pl.ds(0, BLK)], target.at[pl.ds(place * BLK, BLK)], sem.at[first + place]
                )
            )
    return waits


def shift_rows(keys, hosts, bias, b, h, blocks_dev, neigh):
    position = lax.axis_index("ctx")
    slot = lax.broadcasted_iota(jnp.int32, (1, neigh * BLK), 1) // BLK
    shift = jnp.zeros((1, neigh * BLK), jnp.float32)
    host = hosts[position * blocks_dev + b]
    for n in range(neigh):
        value = jnp.where(hosts[keys[b, n]] == host, bias[h], 0.0)
        shift = jnp.where(slot == n, value, shift)
    return shift


def piece_owner(me, step, groups, sign):
    return me ^ step if groups == 4 else lax.rem(me + sign * step + groups, groups)


def attend_kernel(size, groups, v_tags, *refs):
    keys_hbm, hosts_hbm, bias_hbm, q_hbm, w_hbm = refs[:5]
    k_refs = refs[5:5 + len(PAIR)]
    v_refs = refs[5 + len(PAIR):5 + len(PAIR) + len(v_tags)]
    rest = refs[5 + len(PAIR) + len(v_tags):]
    part_refs = rest[:groups]
    o32_ref, lse_ref = rest[groups:groups + 2]
    keys, hosts, bias, q_ref, w_ref, kcat, vcat, score, att, turned, sem = rest[groups + 2:]
    rows, columns = q_ref.shape
    blocks_dev, neigh = keys.shape
    heads_dev = columns // HDIM
    small = start_all([(keys_hbm, keys), (hosts_hbm, hosts), (bias_hbm, bias)], sem)
    large = start_all([(q_hbm, q_ref)], sem, 3)
    wait_all(small)
    places = blocks_dev * neigh
    k_waits = gather_blocks(size, PAIR, keys, k_refs, kcat, sem, 5, blocks_dev, neigh)
    v_waits = gather_blocks(size, v_tags, keys, v_refs, vcat, sem, 5 + places, blocks_dev, neigh)
    large += start_all([(w_hbm, w_ref)], sem, 4)
    large[0].wait()
    wait_all(k_waits)
    span = neigh * BLK
    units = [(b, h) for b in range(blocks_dev) for h in range(heads_dev)]
    for b, h in units:
        cols = slice(h * HDIM, (h + 1) * HDIM)
        s = tdot(q_ref[b * BLK:(b + 1) * BLK, cols], kcat[b * span:(b + 1) * span, cols])
        score[b * heads_dev + h] = s * SCALE + shift_rows(keys, hosts, bias, b, h, blocks_dev, neigh)
    wait_all(v_waits)
    lane = lax.broadcasted_iota(jnp.int32, (BLK, BLK), 1)
    lse_all = jnp.zeros((BLK, BLK), jnp.float32)
    for b, h in units:
        cols = slice(h * HDIM, (h + 1) * HDIM)
        s = score[b * heads_dev + h]
        top = jnp.max(s, axis=1, keepdims=True)
        weights = jnp.exp(s - top)
        total = jnp.sum(weights, axis=1, keepdims=True)
        probs = (weights * (1.0 / total)).astype(jnp.bfloat16)
        out = ndot(probs, vcat[b * span:(b + 1) * span, cols])
        o32_ref[b * BLK:(b + 1) * BLK, cols] = out
        att[b * BLK:(b + 1) * BLK, cols] = out.astype(jnp.bfloat16)
        lse_all = jnp.where(lane == b * heads_dev + h, top + jnp.log(total), lse_all)
    lse_ref[...] = lse_all
    large[1].wait()
    me = lax.axis_index("head")
    part = rows // groups
    for step in range(groups):
        owner = piece_owner(me, step, groups, 1)
        turned[step * part:(step + 1) * part, :] = att[pl.ds(pl.multiple_of(owner * part, part), part), :]
    mixed = ndot(turned[...], w_ref[...]).astype(jnp.bfloat16)
    for step in range(groups):
        part_refs[step][...] = mixed[step * part:(step + 1) * part, :]


def upstream_kernel(groups, *refs):
    keys_hbm, w_hbm, own_hbm, o32_any, lse_any = refs[:5]
    piece_refs = refs[5:4 + groups]
    rest = refs[4 + groups + 1:]
    up_ref, stats_ref, keys, w_ref, grads, o32_ref, lse_ref, sem = rest
    rows, columns = o32_ref.shape
    blocks_dev, neigh = keys.shape
    heads_dev = columns // HDIM
    part = rows // groups
    cut = columns // 2
    pieces = (own_hbm,) + tuple(piece_refs)
    early = start_all(
        [(ref, grads.at[pl.ds(step * part, part)]) for step, ref in enumerate(pieces)]
        + [(keys_hbm, keys)],
        sem,
        2,
    )
    waits = [
        start_all([(w_hbm.at[c * cut:(c + 1) * cut], w_ref.at[c * cut:(c + 1) * cut])], sem, c)[0]
        for c in range(2)
    ]
    late = start_all([(o32_any, o32_ref), (lse_any, lse_ref)], sem, 3 + groups)
    wait_all(early)
    me = lax.axis_index("head")
    for c in range(2):
        waits[c].wait()
        product = tdot(grads[...], w_ref[c * cut:(c + 1) * cut, :]).astype(jnp.bfloat16)
        for step in range(groups):
            owner = piece_owner(me, step, groups, -1)
            up_ref[pl.ds(pl.multiple_of(owner * part, part), part), c * cut:(c + 1) * cut] = product[
                step * part:(step + 1) * part, :
            ]
    wait_all(late)
    pairs = blocks_dev * heads_dev
    lane = lax.broadcasted_iota(jnp.int32, (BLK, BLK), 1)
    stats = lse_ref[...]
    for b in range(blocks_dev):
        for h in range(heads_dev):
            cols = slice(h * HDIM, (h + 1) * HDIM)
            up = up_ref[b * BLK:(b + 1) * BLK, cols].astype(jnp.float32)
            term = jnp.sum(up * o32_ref[b * BLK:(b + 1) * BLK, cols], axis=1, keepdims=True)
            stats = jnp.where(lane == pairs + b * heads_dev + h, term, stats)
    stats_ref[...] = stats
    high = stat_rows(pairs)
    turned = jnp.transpose(stats)[:high, :]
    up_ref[rows:, :] = jnp.zeros((up_ref.shape[0] - rows, columns), jnp.bfloat16)
    pieces = []
    for index in range(3):
        piece = turned.astype(jnp.bfloat16)
        turned = turned - piece.astype(jnp.float32)
        pieces.append(piece)
    spot = lax.broadcasted_iota(jnp.int32, (high, BLK), 1)
    line = lax.broadcasted_iota(jnp.int32, (high, BLK), 0)
    listed = jnp.zeros((high, BLK), jnp.int32)
    for b in range(blocks_dev):
        for n in range(neigh):
            listed = jnp.where(spot == b * neigh + n, keys[b, n], listed)
    listed = jnp.where(line == 0, listed >> 7, listed & 127)
    pieces.append(listed.astype(jnp.float32).astype(jnp.bfloat16))
    for index, piece in enumerate(pieces):
        row = rows + high * (index * BLK // columns)
        col = index * BLK % columns
        up_ref[row:row + high, col:col + BLK] = piece


def query_kernel(size, v_tags, *refs):
    keys_hbm, hosts_hbm, bias_hbm, q_hbm, up_any, stats_any = refs[:6]
    k_refs = refs[6:6 + len(PAIR)]
    v_refs = refs[6 + len(PAIR):6 + len(PAIR) + len(v_tags)]
    (dq_ref, keys, hosts, bias, q_ref, up_ref, stats_ref, kcat, vcat, sem) = refs[
        6 + len(PAIR) + len(v_tags):
    ]
    rows, columns = q_ref.shape
    blocks_dev, neigh = keys.shape
    heads_dev = columns // HDIM
    pairs = blocks_dev * heads_dev
    small = start_all([(keys_hbm, keys), (hosts_hbm, hosts), (bias_hbm, bias)], sem)
    places = blocks_dev * neigh
    large = start_all([(q_hbm, q_ref)], sem, 3)
    large += start_all([(up_any.at[pl.ds(0, rows)], up_ref), (stats_any, stats_ref)], sem, 4 + 2 * places)
    wait_all(small)
    waits = gather_blocks(size, PAIR, keys, k_refs, kcat, sem, 4, blocks_dev, neigh)
    waits += gather_blocks(size, v_tags, keys, v_refs, vcat, sem, 4 + places, blocks_dev, neigh)
    wait_all(large)
    wait_all(waits)
    span = neigh * BLK
    for b in range(blocks_dev):
        for h in range(heads_dev):
            cols = slice(h * HDIM, (h + 1) * HDIM)
            pair = b * heads_dev + h
            q = q_ref[b * BLK:(b + 1) * BLK, cols]
            up = up_ref[b * BLK:(b + 1) * BLK, cols]
            k = kcat[b * span:(b + 1) * span, cols]
            lse = stats_ref[:, pair:pair + 1]
            term = stats_ref[:, pairs + pair:pairs + pair + 1]
            shift = shift_rows(keys, hosts, bias, b, h, blocks_dev, neigh)
            p = jnp.exp(tdot(q, k) * SCALE + shift - lse)
            dp = tdot(up, vcat[b * span:(b + 1) * span, cols])
            ds = (p * (dp - term) * SCALE).astype(jnp.bfloat16)
            dq_ref[b * BLK:(b + 1) * BLK, cols] = ndot(ds, k).astype(jnp.bfloat16)


def key_kernel(size, neigh, *refs):
    nsh = len(PAIR)
    hosts_hbm, bias_hbm, k_hbm, v_hbm = refs[:4]
    q_refs = refs[4:4 + nsh]
    up_refs = refs[4 + nsh:4 + 2 * nsh]
    dk_ref, dv_ref, mark_ref = refs[4 + 2 * nsh:7 + 2 * nsh]
    (hosts, bias, k_ref, v_ref, qwin, upwin, stats, lists, keys, hits, dk_acc, dv_acc, sem) = refs[
        7 + 2 * nsh:
    ]
    rows, columns = k_ref.shape
    long_rows = up_refs[0].shape[0]
    blocks_dev = rows // BLK
    heads_dev = columns // HDIM
    pairs = blocks_dev * heads_dev
    high = stat_rows(pairs)
    position = lax.axis_index("ctx")
    tail = [
        (ref.at[pl.ds(rows, long_rows - rows)], upwin.at[pl.ds(i * long_rows + rows, long_rows - rows)])
        for i, ref in enumerate(up_refs)
    ]
    first = start_all(tail, sem)
    body = [(ref.at[pl.ds(0, rows)], upwin.at[pl.ds(i * long_rows, rows)]) for i, ref in enumerate(up_refs)]
    body += [(ref, qwin.at[pl.ds(i * rows, rows)]) for i, ref in enumerate(q_refs)]
    body += [(hosts_hbm, hosts), (bias_hbm, bias), (k_hbm, k_ref), (v_hbm, v_ref)]
    later = start_all(body, sem, nsh)
    dk_acc[...] = jnp.zeros_like(dk_acc)
    dv_acc[...] = jnp.zeros_like(dv_acc)
    wait_all(first)

    def part_of(index, piece):
        row = index * long_rows + rows + high * (piece * BLK // columns)
        col = piece * BLK % columns
        return upwin[row:row + high, col:col + BLK].astype(jnp.float32)

    for index in range(nsh):
        stats[index] = (part_of(index, 2) + part_of(index, 1)) + part_of(index, 0)
        listed = part_of(index, 3).astype(jnp.int32)
        lists[index:index + 1, :] = listed[0:1, :] * 128 + listed[1:2, :]
    stats[nsh] = jnp.full((high, BLK), NEVER, jnp.float32)
    copy = pltpu.make_async_copy(lists, keys, sem.at[3 * nsh + 4])
    copy.start()
    copy.wait()

    counts = []
    for own in range(blocks_dev):
        mine = position * blocks_dev + own
        count = 0
        for index in range(nsh):
            for inner in range(blocks_dev):
                hit = keys[index, inner * neigh] == mine
                for n in range(1, neigh):
                    hit = hit | (keys[index, inner * neigh + n] == mine)
                hits[own, count] = index * blocks_dev + inner
                count = count + jnp.where(hit, 1, 0)
        hits[own, count] = -1
        counts.append(count)
    wait_all(later)

    for own in range(blocks_dev):
        mine = position * blocks_dev + own
        krow = slice(own * BLK, (own + 1) * BLK)

        def visit(step, carry, own=own, mine=mine, krow=krow):
            qs, ups, sames, lses, terms = [], [], [], [], []
            for turn in range(2):
                entry = hits[own, 2 * step + turn]
                spare = entry < 0
                entry = jnp.where(spare, 0, entry)
                shard = lax.div(entry, blocks_dev)
                inner = lax.rem(entry, blocks_dev)
                owner = 0
                for index, tag in enumerate(PAIR):
                    owner = owner + jnp.where(shard == index, tag_owner(position, tag, size, PAIR), 0)
                sames.append(hosts[owner * blocks_dev + inner] == hosts[mine])
                qs.append(pl.ds(pl.multiple_of(shard * rows + inner * BLK, BLK), BLK))
                ups.append(pl.ds(pl.multiple_of(shard * long_rows + inner * BLK, 16), BLK))
                lses.append((jnp.where(spare, nsh, shard), inner))
                terms.append((shard, inner))
            for h in range(heads_dev):
                cols = slice(h * HDIM, (h + 1) * HDIM)
                k = k_ref[krow, cols]
                v = v_ref[krow, cols]
                q = jnp.concatenate([qwin[r, cols] for r in qs], axis=0)
                up = jnp.concatenate([upwin[r, cols] for r in ups], axis=0)
                less = jnp.concatenate(
                    [
                        stats[shard, pl.ds(inner * heads_dev + h, 1), :] - jnp.where(same, bias[h], 0.0)
                        for (shard, inner), same in zip(lses, sames)
                    ],
                    axis=1,
                )
                term = jnp.concatenate(
                    [stats[shard, pl.ds(pairs + inner * heads_dev + h, 1), :] for shard, inner in terms],
                    axis=1,
                )
                p = jnp.exp(tdot(k, q) * SCALE - less)
                ds = (p * (tdot(v, up) - term) * SCALE).astype(jnp.bfloat16)
                dk_acc[krow, cols] += ndot(ds, q)
                dv_acc[krow, cols] += ndot(p.astype(jnp.bfloat16), up)
            return carry

        lax.fori_loop(0, lax.div(counts[own] + 1, 2), visit, 0)
    dk_ref[...] = dk_acc[...].astype(jnp.bfloat16)
    dv_ref[...] = dv_acc[...].astype(jnp.bfloat16)
    mark_ref[...] = jnp.zeros_like(mark_ref)


def sum_kernel(count, *refs):
    total = refs[0][...].astype(jnp.float32)
    for ref in refs[1:count]:
        total = total + ref[...].astype(jnp.float32)
    refs[-1][...] = total.astype(jnp.bfloat16)


def sum_after(arrays, before):
    return pl.pallas_call(
        functools.partial(sum_kernel, len(arrays)),
        out_shape=jax.ShapeDtypeStruct(arrays[0].shape, jnp.bfloat16),
        in_specs=[VMEM] * len(arrays) + [ANY],
        out_specs=VMEM,
        compiler_params=params(8),
        cost_estimate=cost(1000, 1000),
        name="sum_after",
    )(*arrays, before)


def copy_kernel(count, extra, *refs):
    sources, targets = refs[:count], refs[count + extra:2 * count + extra]
    between, sem = refs[2 * count + extra:-1], refs[-1]
    wait_all(start_all(list(zip(sources, between)), sem))
    wait_all(start_all(list(zip(between, targets)), sem))


def copies_after(arrays, before):
    return pl.pallas_call(
        functools.partial(copy_kernel, len(arrays), len(before)),
        out_shape=[jax.ShapeDtypeStruct(x.shape, x.dtype) for x in arrays],
        in_specs=[ANY] * (len(arrays) + len(before)),
        out_specs=[ANY] * len(arrays),
        scratch_shapes=[pltpu.VMEM(x.shape, x.dtype) for x in arrays]
        + [pltpu.SemaphoreType.DMA((len(arrays),))],
        compiler_params=params(60),
        cost_estimate=cost(1000, 1000),
        name="copies_after",
    )(*arrays, *before)


def cost(flops, nbytes):
    return pl.CostEstimate(flops=flops, bytes_accessed=nbytes, transcendentals=0)


def per_device(
    query_states, key_states, value_states, out_weight, grad_mixed, key_blocks, host_ids, host_bias
):
    size = lax.axis_size("ctx")
    rows, columns = query_states.shape
    width = out_weight.shape[1]
    blocks_dev, neigh = key_blocks.shape
    heads_dev = columns // HDIM
    pairs = blocks_dev * heads_dev
    places = blocks_dev * neigh
    groups = lax.axis_size("head")
    part = rows // groups
    v_tags = CUBE if size == 8 else PAIR
    nsh = len(PAIR)
    bf16, f32, i32 = jnp.bfloat16, jnp.float32, jnp.int32
    high = stat_rows(pairs)
    extra = high * (-(-4 * BLK // columns))
    long_rows = rows + extra

    def ring(x, step):
        return lax.ppermute(x, "head", [(i, (i + step) % groups) for i in range(groups)])

    def flip(x, mask):
        return lax.ppermute(x, "head", [(i, i ^ mask) for i in range(groups)])

    paired = groups == 4
    v_win = exchange_cube(value_states, size) if v_tags is CUBE else exchange_pair(value_states, size)
    k_win = exchange_pair(key_states, size)
    if paired:
        opposite = flip(grad_mixed, 2)
        beside = flip(grad_mixed, 1)
        pieces = [grad_mixed, beside, opposite, flip(opposite, 1)]
    else:
        pieces = [grad_mixed] + [ring(grad_mixed, step) for step in range(1, groups)]
    (late_query,) = copies_after((query_states,), (pieces[1], pieces[2]))
    q_win = exchange_pair(late_query, size)
    scalars = [
        pltpu.SMEM(key_blocks.shape, i32),
        pltpu.SMEM(host_ids.shape, i32),
        pltpu.SMEM(host_bias.shape, f32),
    ]

    parts_o32_lse = pl.pallas_call(
        functools.partial(attend_kernel, size, groups, v_tags),
        out_shape=[jax.ShapeDtypeStruct((part, width), bf16)] * groups
        + [jax.ShapeDtypeStruct((rows, columns), f32), jax.ShapeDtypeStruct((BLK, BLK), f32)],
        in_specs=[HBM] * 5 + [ANY] * (len(PAIR) + len(v_tags)),
        out_specs=[VMEM] * (groups + 2),
        scratch_shapes=scalars
        + [
            pltpu.VMEM((rows, columns), bf16),
            pltpu.VMEM((columns, width), bf16),
            pltpu.VMEM((places * BLK, columns), bf16),
            pltpu.VMEM((places * BLK, columns), bf16),
            pltpu.VMEM((pairs, BLK, neigh * BLK), f32),
            pltpu.VMEM((rows, columns), bf16),
            pltpu.VMEM((rows, columns), bf16),
            pltpu.SemaphoreType.DMA((5 + 2 * places,)),
        ],
        compiler_params=params(60),
        cost_estimate=cost(10**9, 10**6),
        name="attend",
    )(key_blocks, host_ids, host_bias, query_states, out_weight, *k_win, *v_win)
    parts = parts_o32_lse[:groups]
    o32, lse = parts_o32_lse[groups:]
    mixed = parts[0].astype(f32)
    if paired:
        relay = flip(parts[3], 1)
        beside_sum = flip(parts[1], 1)
        passed = (parts[2].astype(f32) + relay.astype(f32)).astype(bf16)
        arrived = [beside_sum, flip(passed, 2)]
    else:
        arrived = [ring(parts[step], step) for step in range(1, groups)]

    up, stats = pl.pallas_call(
        functools.partial(upstream_kernel, groups),
        out_shape=[
            jax.ShapeDtypeStruct((long_rows, columns), bf16),
            jax.ShapeDtypeStruct((BLK, BLK), f32),
        ],
        in_specs=[HBM] * 3 + [ANY] * (groups + 2),
        out_specs=[VMEM] * 2,
        scratch_shapes=[
            pltpu.SMEM(key_blocks.shape, i32),
            pltpu.VMEM((columns, width), bf16),
            pltpu.VMEM((rows, width), bf16),
            pltpu.VMEM((rows, columns), f32),
            pltpu.VMEM((BLK, BLK), f32),
            pltpu.SemaphoreType.DMA((5 + groups,)),
        ],
        compiler_params=params(60),
        cost_estimate=cost(1000, 1000),
        name="upstream",
    )(key_blocks, out_weight, grad_mixed, o32, lse, *pieces[1:], q_win[1])
    up_win = exchange_pair(up, size)

    grad_query = pl.pallas_call(
        functools.partial(query_kernel, size, v_tags),
        out_shape=jax.ShapeDtypeStruct((rows, columns), bf16),
        in_specs=[HBM] * 4 + [ANY] * (2 + len(PAIR) + len(v_tags)),
        out_specs=VMEM,
        scratch_shapes=scalars
        + [
            pltpu.VMEM((rows, columns), bf16),
            pltpu.VMEM((rows, columns), bf16),
            pltpu.VMEM((BLK, BLK), f32),
            pltpu.VMEM((places * BLK, columns), bf16),
            pltpu.VMEM((places * BLK, columns), bf16),
            pltpu.SemaphoreType.DMA((6 + 2 * places,)),
        ],
        compiler_params=params(60),
        cost_estimate=cost(16 * 10**9, 32 * 10**6),
        name="query_grad",
    )(key_blocks, host_ids, host_bias, query_states, up, stats, *k_win, *v_win)

    grad_key, grad_value, mark = pl.pallas_call(
        functools.partial(key_kernel, size, neigh),
        out_shape=[jax.ShapeDtypeStruct((rows, columns), bf16)] * 2
        + [jax.ShapeDtypeStruct((8, BLK), f32)],
        in_specs=[HBM] * 5 + [ANY] * (2 * nsh - 1),
        out_specs=[VMEM] * 3,
        scratch_shapes=[
            pltpu.SMEM(host_ids.shape, i32),
            pltpu.SMEM(host_bias.shape, f32),
            pltpu.VMEM((rows, columns), bf16),
            pltpu.VMEM((rows, columns), bf16),
            pltpu.VMEM((nsh * rows, columns), bf16),
            pltpu.VMEM((nsh * long_rows, columns), bf16),
            pltpu.VMEM((nsh + 1, high, BLK), f32),
            pltpu.VMEM((8, BLK), i32),
            pltpu.SMEM((8, BLK), i32),
            pltpu.SMEM((blocks_dev, nsh * blocks_dev + 2), i32),
            pltpu.VMEM((rows, columns), f32),
            pltpu.VMEM((rows, columns), f32),
            pltpu.SemaphoreType.DMA((3 * nsh + 5,)),
        ],
        compiler_params=params(20),
        cost_estimate=cost(1000, 1000),
        name="key_grad",
    )(host_ids, host_bias, key_states, value_states, query_states, *q_win[1:], *up_win)

    mixed_out = sum_after((parts[0], *arrived), mark)
    return (mixed_out, grad_query, grad_key, grad_value)


def solution(mesh):
    in_specs = (
        P("ctx", "head"),
        P("ctx", "head"),
        P("ctx", "head"),
        P("head", None),
        P(("ctx", "head"), None),
        P("ctx", None),
        P(),
        P("head"),
    )
    out_specs = (P(("ctx", "head"), None), P("ctx", "head"), P("ctx", "head"), P("ctx", "head"))
    return jax.shard_map(
        per_device, mesh=mesh, in_specs=in_specs, out_specs=out_specs, check_vma=False
    )
```
